128 devices in a mesh: prow: 64 (over z, y, x), pcol: 2 (over core).
Axes of the slice: x: 4, y: 4, z: 4, core: 2. Of those that a mesh axis runs over, the one named last changes fastest.
Arguments:
- hist_factor: bfloat16 [3, 4096, 65536], P(None, 'pcol', 'prow'), may hold values from -0.013671875 to 0.013671875
- hist_solution: bfloat16 [3, 1024, 65536], P(None, None, 'prow'), may hold values from -16 to 16
- diag_factor: bfloat16 [4096, 4096], P('pcol', 'prow'), may hold values from -2 to 2, as said below
- samples: bfloat16 [1024, 4096], P('prow', 'pcol'), may hold values from -6 to 6
Outputs:
- solution: float32 [1024, 4096], P('prow', 'pcol')
The draws below stay inside these ranges and needn't reach their ends.
Inputs may be any that keep to these rules, and one draw needn't show every extreme that they name: `diag_factor`: only the lower triangle with the diagonal is read; the diagonal entries are positive.
All inputs are finite; a program needn't handle non-finite values.
Results may differ from the reference program's by a relative error of at most 0.0003.
Values may be sent and summed in bfloat16 or wider, within the bound.
No kernel may reach another device: no remote copies, remote signals or barrier semaphores. Data moves between devices by JAX's collectives and lax.ppermute only.
A program may use at most 192 MiB of HBM per device.

```python
import jax
import jax.numpy as jnp
from jax import lax

NB = 1024
K = 4
R = 1024
HB = 3
N_PROW = 64


def draw_diag_factor(key, part):
    first, second = jax.random.split(key)
    width = K * NB
    spread = jax.random.normal(first, (width, width), jnp.float32)
    diagonal = jax.random.uniform(second, (width, width), jnp.float32, 0.8, 1.6)
    offdiag = jnp.clip(spread * (1.8 / width ** 0.5), -2.0, 2.0)
    rows = jnp.arange(width)[:, None]
    cols = jnp.arange(width)[None, :]
    return jnp.where(rows == cols, diagonal, offdiag).astype(jnp.bfloat16)


def strengthened(result, key, source, target, shards_of, factor):
    owner, partner = [(jnp.arange(result.shape[position]) // (result.shape[position] // shards_of)).reshape([-1 if axis == position else 1 for axis in range(result.ndim)]) for position in (source, target)]
    chosen = jax.random.permutation(key, shards_of)[partner]
    strong = (owner == chosen) | (owner == (partner + shards_of // 2) % shards_of)
    return jnp.where(strong, factor * result, result)


def level_of(key, dims, cuts, least, top_value):
    gain, own = 1.0, jax.random.fold_in(key, 6)
    for dim, blocks in cuts:
        draws = jnp.exp(jax.random.uniform(jax.random.fold_in(own, dim), (blocks,), jnp.float32, least / len(cuts), top_value / len(cuts)))
        gain = gain * jnp.repeat(draws, dims[dim] // blocks).reshape([-1 if axis == dim else 1 for axis in range(len(dims))])
    return gain


def centred(stream_key, dims, scale, limit, cuts=(), kind=jnp.bfloat16):
    entries = jax.random.normal(stream_key, dims, jnp.float32) * scale
    if len(cuts) > 0:
        entries = level_of(stream_key, dims, cuts, -0.22, 0.18) * entries
    return jnp.clip(entries, min=-limit, max=limit).astype(kind)


def heavy_noise(rng, shape, scale, most, shards, heavy, dtype=jnp.bfloat16):
    drawn = scale * jax.random.normal(rng, shape, jnp.float32)
    if shards:
        drawn = drawn * level_of(rng, shape, shards, -0.22, 0.18)
    return jnp.clip(strengthened(drawn, jax.random.fold_in(rng, 3), *heavy), -most, most).astype(dtype)


def setup_inputs(seed: int = 0) -> dict:
    splits = jax.random.split(jax.random.key(seed), 5)
    hist_factor = centred(splits[0], (HB, K * NB, N_PROW * NB), (HB * N_PROW * NB) ** -0.5, 0.013671875, ((1, 2), (2, 64)))
    hist_solution = heavy_noise(splits[1], (HB, R, N_PROW * NB), 1.0, 16.0, ((2, 64),), (2, 1, 64, 4.0))
    diag_factor = draw_diag_factor(jax.random.fold_in(splits[4], 71), 0)
    samples = centred(splits[3], (R, K * NB), 1.0, 6.0, ((0, 64), (1, 2)))
    return {"hist_factor": hist_factor, "hist_solution": hist_solution, "diag_factor": diag_factor, "samples": samples}


def reference(hist_factor, hist_solution, diag_factor, samples):
    history = jnp.zeros((R, K * NB), jnp.float32)
    for group in range(HB):
        history = history + lax.dot_general(hist_solution[group].astype(jnp.float32), hist_factor[group].astype(jnp.float32), (((1,), (1,)), ((), ())), preferred_element_type=jnp.float32)
    rhs = samples.astype(jnp.float32) - history
    lower = jnp.tril(diag_factor.astype(jnp.float32))
    return lax.linalg.triangular_solve(lower, rhs, left_side=False, lower=True, transpose_a=True)
```

```python
import functools

import jax
import jax.numpy as jnp
import numpy as np
from jax import lax
from jax.experimental import pallas as pl
from jax.experimental.pallas import tpu as pltpu
from jax.sharding import Mesh
from jax.sharding import PartitionSpec as P

F32 = jnp.float32
BF16 = jnp.bfloat16
SIDE = 4
ROWS = 16
STRIP = 64
BLOCK = 512
AXES = ("z", "y", "x")
EVERY = ("z", "y", "x", "pcol")
PARTS = ((0, 768, "xyz"), (768, 768, "yzx"), (1536, 512, "zxy"))
MB = 1 << 20


def split2(value):
    high = value.astype(BF16)
    return high, (value - high.astype(F32)).astype(BF16)


def dot(a, b):
    return jnp.dot(a, b, preferred_element_type=F32)


def dot_exact(a, b):
    high, low = split2(a)
    rows = a.shape[0]
    both = dot(jnp.concatenate([high, low], axis=0), b)
    return both[:rows] + both[rows:]


def dot_pair(a, b_high, b_low):
    high, low = split2(a)
    rows = a.shape[0]
    both = dot(jnp.concatenate([high, low], axis=0), b_high)
    return both[:rows] + both[rows:] + dot(high, b_low)


def pack_kernel(info, strip, out):
    out[:, : strip.shape[1]] = strip[...]
    block = strip[:, pl.ds(pl.multiple_of(info[0] * 128, 128), 128)].astype(F32)
    odd = info[1] > 0
    block = jnp.where(odd, pltpu.roll(block, 64, 1), block)
    rows = lax.broadcasted_iota(jnp.int32, block.shape, 0)
    lanes = lax.broadcasted_iota(jnp.int32, block.shape, 1)
    upper = jnp.where((lanes > rows) & (lanes < STRIP), block, 0.0)
    diagonal = jnp.sum(jnp.where(lanes == rows, block, 0.0), axis=1, keepdims=True)
    scale = jnp.broadcast_to(1.0 / diagonal, block.shape)
    todo = jnp.where(lanes == rows, 1.0, 0.0)
    for k in range(STRIP - 1, 0, -1):
        row = todo[k : k + 1, :] * scale[k : k + 1, :]
        todo = todo - upper[:, k : k + 1] * row
    inverse = todo * scale
    inverse = jnp.where(odd, pltpu.roll(inverse, 64, 1), inverse)
    high, low = split2(inverse)
    width = strip.shape[1]
    out[:, width : width + 128] = high
    out[:, width + 128 : width + 256] = low


def pack(info, strip):
    rows, width = strip.shape
    return pl.pallas_call(
        pack_kernel,
        out_shape=jax.ShapeDtypeStruct((rows, width + 256), BF16),
        in_specs=[
            pl.BlockSpec(memory_space=pltpu.SMEM),
            pl.BlockSpec(memory_space=pltpu.VMEM),
        ],
        out_specs=pl.BlockSpec(memory_space=pltpu.VMEM),
        compiler_params=pltpu.CompilerParams(vmem_limit_bytes=16 * MB),
        name="pack_inverse",
    )(info, strip)


def grow_kernel(core, window, out_high, out_low):
    width = window.shape[0]
    rows = lax.broadcasted_iota(jnp.int32, (128, 128), 0)
    lanes = lax.broadcasted_iota(jnp.int32, (128, 128), 1)
    corner = (rows < STRIP) & (lanes >= STRIP)
    level = []
    for start in range(0, width, 128):
        rng = slice(start, start + 128)
        high = window[rng, width : width + 128]
        low = window[rng, width + 128 : width + 256]
        both = high.astype(F32) + low.astype(F32)
        off = jnp.where(corner, window[rng, rng].astype(F32), 0.0).astype(BF16)
        level.append(both - dot_pair(dot_exact(both, off), high, low))
    size = 128
    while size < BLOCK:
        grown = []
        for n in range(0, len(level), 2):
            start = n * size
            off = window[start : start + size, start + size : start + 2 * size]
            high, low = split2(level[n + 1])
            corner_block = -dot_pair(dot_exact(level[n], off), high, low)
            if 2 * size < BLOCK:
                top = jnp.concatenate([level[n], corner_block], axis=1)
                bottom = jnp.concatenate([jnp.zeros_like(corner_block), level[n + 1]], axis=1)
                grown.append(jnp.concatenate([top, bottom], axis=0))
            else:
                b = n // 2
                corner_high, corner_low = split2(corner_block)
                first_high, first_low = split2(level[n])
                zero = jnp.zeros((size, size), BF16)
                for ref, first, mixed, second in (
                    (out_high, first_high, corner_high, high),
                    (out_low, first_low, corner_low, low),
                ):
                    ref[b, :size, :size] = first
                    ref[b, :size, size:] = mixed
                    ref[b, size:, :size] = zero
                    ref[b, size:, size:] = second
        level = grown
        size *= 2


def grow(core, window, slab):
    shape = jax.ShapeDtypeStruct((slab // BLOCK, BLOCK, BLOCK), BF16)
    return pl.pallas_call(
        grow_kernel,
        out_shape=(shape, shape),
        grid_spec=pltpu.PrefetchScalarGridSpec(
            num_scalar_prefetch=1,
            grid=(1,),
            in_specs=[pl.BlockSpec((slab, window.shape[1]), lambda i, core: (core[0], 0))],
            out_specs=[pl.BlockSpec(shape.shape, lambda i, core: (0, 0, 0))] * 2,
        ),
        compiler_params=pltpu.CompilerParams(vmem_limit_bytes=48 * MB),
        name="grow_inverse",
    )(core, window)


def solve_block(blocks, pending, factor, high, low, out, wait):
    for b in range(blocks):
        cols = slice(b * BLOCK, (b + 1) * BLOCK)
        wait(b)
        y = dot_pair(pending[:, cols], high[b], low[b])
        out[:, cols] = y
        if b + 1 < blocks:
            rest = slice((b + 1) * BLOCK, blocks * BLOCK)
            pending[:, rest] = pending[:, rest] - dot_exact(y, factor[cols, rest])


def solve_copies(base, slab, window, inv_high, inv_low, factor, high, low, sems):
    copies = []
    for b in range(slab // BLOCK):
        rows = pl.ds(pl.multiple_of(base + b * BLOCK, BLOCK), BLOCK)
        group = [
            pltpu.make_async_copy(inv_high.at[b], high.at[b], sems.at[0, b]),
            pltpu.make_async_copy(inv_low.at[b], low.at[b], sems.at[1, b]),
        ]
        if (b + 1) * BLOCK < slab:
            rest = pl.ds((b + 1) * BLOCK, slab - (b + 1) * BLOCK)
            group.append(
                pltpu.make_async_copy(
                    window.at[rows, rest],
                    factor.at[pl.ds(b * BLOCK, BLOCK), rest],
                    sems.at[2, b],
                )
            )
        copies.append(group)
    return copies


def first_kernel(core, right, window, inv_high, inv_low, out, factor, high, low, pending, sems):
    slab = right.shape[1]

    @pl.when(core[0] == 0)
    def _():
        copies = solve_copies(0, slab, window, inv_high, inv_low, factor, high, low, sems)
        for group in copies:
            for copy in group:
                copy.start()
        pending[...] = right[...]

        def wait(b):
            for copy in copies[b]:
                copy.wait()

        solve_block(slab // BLOCK, pending, factor, high, low, out, wait)

    @pl.when(core[0] != 0)
    def _():
        out[...] = jnp.zeros_like(out)


def second_kernel(
    core, right, own, other, window, inv_high, inv_low, out, factor, high, low, pending, below, sems, below_sems
):
    slab = right.shape[1]

    @pl.when(core[0] != 0)
    def _():
        belows = []
        for b in range(slab // BLOCK):
            rows = pl.ds(b * BLOCK, BLOCK)
            belows.append(
                pltpu.make_async_copy(window.at[rows, pl.ds(0, slab)], below.at[rows], below_sems.at[b])
            )
        copies = solve_copies(slab, slab, window, inv_high, inv_low, factor, high, low, sems)
        for copy in belows:
            copy.start()
        for group in copies:
            for copy in group:
                copy.start()
        pending[...] = right[...]
        for b in range(slab // BLOCK):
            cols = slice(b * BLOCK, (b + 1) * BLOCK)
            belows[b].wait()
            pending[...] = pending[...] - dot_exact(other[:, cols], below[cols, :])

        def wait(b):
            for copy in copies[b]:
                copy.wait()

        solve_block(slab // BLOCK, pending, factor, high, low, out, wait)

    @pl.when(core[0] == 0)
    def _():
        out[...] = own[...]


def solve_call(kernel, core, dense, window, inv_high, inv_low, extra, name):
    rows, slab = dense[0].shape
    blocks = slab // BLOCK
    vmem = pl.BlockSpec(memory_space=pltpu.VMEM)
    hbm = pl.BlockSpec(memory_space=pl.ANY)
    return pl.pallas_call(
        kernel,
        out_shape=jax.ShapeDtypeStruct((rows, slab), F32),
        in_specs=[pl.BlockSpec(memory_space=pltpu.SMEM)] + [vmem] * len(dense) + [hbm] * 3,
        out_specs=vmem,
        scratch_shapes=[
            pltpu.VMEM((slab, slab), BF16),
            pltpu.VMEM((blocks, BLOCK, BLOCK), BF16),
            pltpu.VMEM((blocks, BLOCK, BLOCK), BF16),
            pltpu.VMEM((rows, slab), F32),
        ]
        + ([pltpu.VMEM((slab, slab), BF16)] if extra else [])
        + [pltpu.SemaphoreType.DMA((3, blocks))]
        + ([pltpu.SemaphoreType.DMA((blocks,))] if extra else []),
        compiler_params=pltpu.CompilerParams(vmem_limit_bytes=40 * MB),
        name=name,
    )(core, *dense, window, inv_high, inv_low)


def product_kernel(first, start, order, left, right, out, a, b, a_sems, b_sems):
    groups, rows, _ = a.shape
    width = b.shape[1]
    for g in range(groups):
        pltpu.make_async_copy(right.at[g, pl.ds(start, width)], b.at[g], b_sems.at[g]).start()
        for n in range(rows // ROWS):
            source = pl.ds(pl.multiple_of(order[first + n] * ROWS, ROWS), ROWS)
            pltpu.make_async_copy(
                left.at[g, source], a.at[g, pl.ds(n * ROWS, ROWS)], a_sems.at[g]
            ).start()
    for g in range(groups):
        pltpu.make_async_copy(a.at[g], a.at[g], a_sems.at[g]).wait()
        pltpu.make_async_copy(b.at[g], b.at[g], b_sems.at[g]).wait()
        for col in range(0, width, 256):
            cols = slice(col, col + 256)
            term = lax.dot_general(
                a[g], b[g, cols, :], (((1,), (1,)), ((), ())), preferred_element_type=F32
            )
            if g == 0:
                out[:, cols] = term
            else:
                out[:, cols] = out[:, cols] + term


def product(order, left, right, first, rows, start, width, name):
    groups, _, depth = left.shape
    return pl.pallas_call(
        functools.partial(product_kernel, first, start),
        out_shape=jax.ShapeDtypeStruct((rows, width), F32),
        in_specs=[
            pl.BlockSpec(memory_space=pltpu.SMEM),
            pl.BlockSpec(memory_space=pl.ANY),
            pl.BlockSpec(memory_space=pl.ANY),
        ],
        out_specs=pl.BlockSpec(memory_space=pltpu.VMEM),
        scratch_shapes=[
            pltpu.VMEM((groups, rows, depth), BF16),
            pltpu.VMEM((groups, width, depth), BF16),
            pltpu.SemaphoreType.DMA((groups,)),
            pltpu.SemaphoreType.DMA((groups,)),
        ],
        compiler_params=pltpu.CompilerParams(vmem_limit_bytes=24 * MB),
        cost_estimate=pl.CostEstimate(
            flops=2 * groups * rows * width * depth,
            bytes_accessed=2 * groups * (rows + width) * depth + 4 * rows * width,
            transcendentals=0,
        ),
        name=name,
    )(order, left, right)


def partner_pairs(axis, second):
    pairs = []
    for z, y, x, c in np.ndindex(SIDE, SIDE, SIDE, 2):
        place = {"z": z, "y": y, "x": x}
        flip = (3 if c else 1) ^ (2 if second else 0)
        other = dict(place)
        other[axis] ^= flip
        index = lambda at: ((at["z"] * SIDE + at["y"]) * SIDE + at["x"]) * 2 + c
        pairs.append((index(place), index(other)))
    return pairs


def block_order(axes, place, core):
    flip = jnp.where(core == 0, 1, 3)
    masks = jnp.stack([jnp.full_like(flip, 2), flip, flip ^ 2, jnp.zeros_like(flip)])
    lists = {name: place[name] ^ masks for name in AXES}
    shape = {name: [1, 1, 1] for name in AXES}
    for position, name in enumerate(axes):
        shape[name][position] = SIDE
    at = {name: lists[name].reshape(shape[name]) for name in AXES}
    return (((at["z"] * SIDE + at["y"]) * SIDE + at["x"]).reshape(-1)).astype(jnp.int32)


def per_device(hist_factor, hist_solution, diag_factor, samples):
    slab = hist_factor.shape[1]
    samples_all = hist_solution.shape[1]
    core = lax.axis_index("pcol")
    place = {name: lax.axis_index(name) for name in AXES}
    chip = (place["z"] * SIDE + place["y"]) * SIDE + place["x"]
    core_arg = core.astype(jnp.int32).reshape(1)

    per_core = slab // STRIP
    local = chip % per_core
    info = jnp.stack([local // 2, local % 2]).astype(jnp.int32)
    packed = pack(info, diag_factor.T)
    window = lax.all_gather(packed, AXES, axis=0, tiled=True)

    half = samples_all // 2
    sends, keeps = [], []
    for number, (start, width, axes) in enumerate(PARTS):
        order = block_order(axes, place, core)
        sends.append(product(order, hist_solution, hist_factor, 0, half, start, width, f"send{number}"))
        keeps.append(
            product(order, hist_solution, hist_factor, half // ROWS, half, start, width, f"keep{number}")
        )
    for stage in range(3):
        for second in (False, True):
            got = [
                lax.ppermute(sends[n], EVERY, partner_pairs(PARTS[n][2][stage], second))
                for n in range(len(PARTS))
            ]
            if stage == 2 and second:
                keeps = [keeps[n] + got[n] for n in range(len(PARTS))]
                break
            middle = keeps[0].shape[0] // 2
            sends = [keeps[n][:middle] + got[n][:middle] for n in range(len(PARTS))]
            keeps = [keeps[n][middle:] + got[n][middle:] for n in range(len(PARTS))]
    pending = samples.astype(F32) - jnp.concatenate(keeps, axis=1)

    inv_high, inv_low = grow(core_arg, window, slab)
    first = solve_call(first_kernel, core_arg, (pending,), window, inv_high, inv_low, False, "solve0")
    other = lax.ppermute(first, "pcol", [(0, 1), (1, 0)])
    return solve_call(
        second_kernel, core_arg, (pending, first, other), window, inv_high, inv_low, True, "solve1"
    )


def solution(mesh):
    cube = Mesh(mesh.devices.reshape(SIDE, SIDE, SIDE, 2), EVERY)
    return jax.shard_map(
        per_device,
        mesh=cube,
        in_specs=(
            P(None, "pcol", AXES),
            P(None, None, AXES),
            P("pcol", AXES),
            P(AXES, "pcol"),
        ),
        out_specs=P(AXES, "pcol"),
        check_vma=False,
    )
```

```python
import functools

import jax
import jax.numpy as jnp
import numpy as np
from jax import lax
from jax.experimental import pallas as pl
from jax.experimental.pallas import tpu as pltpu
from jax.sharding import Mesh
from jax.sharding import PartitionSpec as P

F32 = jnp.float32
BF16 = jnp.bfloat16
SIDE = 4
ROWS = 16
STRIP = 64
BLOCK = 512
AXES = ("z", "y", "x")
EVERY = ("z", "y", "x", "pcol")
PARTS = ((0, 768, "xyz"), (768, 768, "yzx"), (1536, 512, "zxy"))
MB = 1 << 20


def split2(value):
    high = value.astype(BF16)
    return high, (value - high.astype(F32)).astype(BF16)


def dot(a, b):
    return jnp.dot(a, b, preferred_element_type=F32)


def dot_exact(a, b):
    high, low = split2(a)
    rows = a.shape[0]
    both = dot(jnp.concatenate([high, low], axis=0), b)
    return both[:rows] + both[rows:]


def dot_pair(a, b_high, b_low):
    high, low = split2(a)
    rows = a.shape[0]
    both = dot(jnp.concatenate([high, low], axis=0), b_high)
    return both[:rows] + both[rows:] + dot(high, b_low)


def pack_kernel(info, strip, out):
    out[:, : strip.shape[1]] = strip[...]
    block = strip[:, pl.ds(pl.multiple_of(info[0] * 128, 128), 128)].astype(F32)
    odd = info[1] > 0
    block = jnp.where(odd, pltpu.roll(block, 64, 1), block)
    rows = lax.broadcasted_iota(jnp.int32, block.shape, 0)
    lanes = lax.broadcasted_iota(jnp.int32, block.shape, 1)
    upper = jnp.where((lanes > rows) & (lanes < STRIP), block, 0.0)
    diagonal = jnp.sum(jnp.where(lanes == rows, block, 0.0), axis=1, keepdims=True)
    scale = jnp.broadcast_to(1.0 / diagonal, block.shape)
    todo = jnp.where(lanes == rows, 1.0, 0.0)
    for k in range(STRIP - 1, 0, -1):
        row = todo[k : k + 1, :] * scale[k : k + 1, :]
        todo = todo - upper[:, k : k + 1] * row
    inverse = todo * scale
    inverse = jnp.where(odd, pltpu.roll(inverse, 64, 1), inverse)
    high, low = split2(inverse)
    width = strip.shape[1]
    out[:, width : width + 128] = high
    out[:, width + 128 : width + 256] = low


def pack(info, strip):
    rows, width = strip.shape
    return pl.pallas_call(
        pack_kernel,
        out_shape=jax.ShapeDtypeStruct((rows, width + 256), BF16),
        in_specs=[
            pl.BlockSpec(memory_space=pltpu.SMEM),
            pl.BlockSpec(memory_space=pltpu.VMEM),
        ],
        out_specs=pl.BlockSpec(memory_space=pltpu.VMEM),
        compiler_params=pltpu.CompilerParams(vmem_limit_bytes=16 * MB),
        name="pack_inverse",
    )(info, strip)


def grow_kernel(core, window, out_high, out_low):
    width = window.shape[0]
    rows = lax.broadcasted_iota(jnp.int32, (128, 128), 0)
    lanes = lax.broadcasted_iota(jnp.int32, (128, 128), 1)
    corner = (rows < STRIP) & (lanes >= STRIP)
    level = []
    for start in range(0, width, 128):
        rng = slice(start, start + 128)
        high = window[rng, width : width + 128]
        low = window[rng, width + 128 : width + 256]
        both = high.astype(F32) + low.astype(F32)
        off = jnp.where(corner, window[rng, rng].astype(F32), 0.0).astype(BF16)
        level.append(both - dot_pair(dot_exact(both, off), high, low))
    size = 128
    while size < BLOCK:
        grown = []
        for n in range(0, len(level), 2):
            start = n * size
            off = window[start : start + size, start + size : start + 2 * size]
            high, low = split2(level[n + 1])
            corner_block = -dot_pair(dot_exact(level[n], off), high, low)
            if 2 * size < BLOCK:
                top = jnp.concatenate([level[n], corner_block], axis=1)
                bottom = jnp.concatenate([jnp.zeros_like(corner_block), level[n + 1]], axis=1)
                grown.append(jnp.concatenate([top, bottom], axis=0))
            else:
                b = n // 2
                corner_high, corner_low = split2(corner_block)
                first_high, first_low = split2(level[n])
                zero = jnp.zeros((size, size), BF16)
                for ref, first, mixed, second in (
                    (out_high, first_high, corner_high, high),
                    (out_low, first_low, corner_low, low),
                ):
                    ref[b, :size, :size] = first
                    ref[b, :size, size:] = mixed
                    ref[b, size:, :size] = zero
                    ref[b, size:, size:] = second
        level = grown
        size *= 2


def grow(core, window, slab):
    shape = jax.ShapeDtypeStruct((slab // BLOCK, BLOCK, BLOCK), BF16)
    return pl.pallas_call(
        grow_kernel,
        out_shape=(shape, shape),
        grid_spec=pltpu.PrefetchScalarGridSpec(
            num_scalar_prefetch=1,
            grid=(1,),
            in_specs=[pl.BlockSpec((slab, window.shape[1]), lambda i, core: (core[0], 0))],
            out_specs=[pl.BlockSpec(shape.shape, lambda i, core: (0, 0, 0))] * 2,
        ),
        compiler_params=pltpu.CompilerParams(vmem_limit_bytes=48 * MB),
        name="grow_inverse",
    )(core, window)


def solve_block(blocks, pending, factor, high, low, out, wait):
    for b in range(blocks):
        cols = slice(b * BLOCK, (b + 1) * BLOCK)
        wait(b)
        y = dot_pair(pending[:, cols], high[b], low[b])
        out[:, cols] = y
        if b + 1 < blocks:
            rest = slice((b + 1) * BLOCK, blocks * BLOCK)
            pending[:, rest] = pending[:, rest] - dot_exact(y, factor[cols, rest])


def solve_copies(base, slab, window, inv_high, inv_low, factor, high, low, sems):
    copies = []
    for b in range(slab // BLOCK):
        rows = pl.ds(pl.multiple_of(base + b * BLOCK, BLOCK), BLOCK)
        group = [
            pltpu.make_async_copy(inv_high.at[b], high.at[b], sems.at[0, b]),
            pltpu.make_async_copy(inv_low.at[b], low.at[b], sems.at[1, b]),
        ]
        if (b + 1) * BLOCK < slab:
            rest = pl.ds((b + 1) * BLOCK, slab - (b + 1) * BLOCK)
            group.append(
                pltpu.make_async_copy(
                    window.at[rows, rest],
                    factor.at[pl.ds(b * BLOCK, BLOCK), rest],
                    sems.at[2, b],
                )
            )
        copies.append(group)
    return copies


def first_kernel(core, right, window, inv_high, inv_low, out, factor, high, low, pending, sems):
    slab = right.shape[1]

    @pl.when(core[0] == 0)
    def _():
        copies = solve_copies(0, slab, window, inv_high, inv_low, factor, high, low, sems)
        for group in copies:
            for copy in group:
                copy.start()
        pending[...] = right[...]

        def wait(b):
            for copy in copies[b]:
                copy.wait()

        solve_block(slab // BLOCK, pending, factor, high, low, out, wait)

    @pl.when(core[0] != 0)
    def _():
        out[...] = jnp.zeros_like(out)


def second_kernel(
    core, right, own, other, window, inv_high, inv_low, out, factor, high, low, pending, below, sems, below_sems
):
    slab = right.shape[1]

    @pl.when(core[0] != 0)
    def _():
        belows = []
        for b in range(slab // BLOCK):
            rows = pl.ds(b * BLOCK, BLOCK)
            belows.append(
                pltpu.make_async_copy(window.at[rows, pl.ds(0, slab)], below.at[rows], below_sems.at[b])
            )
        copies = solve_copies(slab, slab, window, inv_high, inv_low, factor, high, low, sems)
        for copy in belows:
            copy.start()
        for group in copies:
            for copy in group:
                copy.start()
        pending[...] = right[...]
        for b in range(slab // BLOCK):
            cols = slice(b * BLOCK, (b + 1) * BLOCK)
            belows[b].wait()
            pending[...] = pending[...] - dot_exact(other[:, cols], below[cols, :])

        def wait(b):
            for copy in copies[b]:
                copy.wait()

        solve_block(slab // BLOCK, pending, factor, high, low, out, wait)

    @pl.when(core[0] == 0)
    def _():
        out[...] = own[...]


def solve_call(kernel, core, dense, window, inv_high, inv_low, extra, name):
    rows, slab = dense[0].shape
    blocks = slab // BLOCK
    vmem = pl.BlockSpec(memory_space=pltpu.VMEM)
    hbm = pl.BlockSpec(memory_space=pltpu.HBM)
    return pl.pallas_call(
        kernel,
        out_shape=jax.ShapeDtypeStruct((rows, slab), F32),
        in_specs=[pl.BlockSpec(memory_space=pltpu.SMEM)] + [vmem] * len(dense) + [hbm] * 3,
        out_specs=vmem,
        scratch_shapes=[
            pltpu.VMEM((slab, slab), BF16),
            pltpu.VMEM((blocks, BLOCK, BLOCK), BF16),
            pltpu.VMEM((blocks, BLOCK, BLOCK), BF16),
            pltpu.VMEM((rows, slab), F32),
        ]
        + ([pltpu.VMEM((slab, slab), BF16)] if extra else [])
        + [pltpu.SemaphoreType.DMA((3, blocks))]
        + ([pltpu.SemaphoreType.DMA((blocks,))] if extra else []),
        compiler_params=pltpu.CompilerParams(vmem_limit_bytes=40 * MB),
        name=name,
    )(core, *dense, window, inv_high, inv_low)


def product_kernel(parts, half, order, left, right, *refs):
    outs, (a, b, picked, a_sems, b_sems) = refs[: len(parts)], refs[len(parts) :]
    groups, _, depth = left.shape
    rows = picked.shape[0]
    spans = [(n, col) for n in range(len(parts)) for col in range(0, parts[n][2], 256)]
    loads = []
    for g in range(groups):
        lanes = pl.ds(g * depth, depth)
        copy = pltpu.make_async_copy(left.at[g], a.at[:, lanes], a_sems.at[g])
        copy.start()
        loads.append(copy)
    tiles = []
    for t, (n, col) in enumerate(spans):
        tile = []
        for g in range(groups):
            lanes = pl.ds(g * depth, depth)
            copy = pltpu.make_async_copy(
                right.at[g, pl.ds(parts[n][1] + col, 256)], b.at[t, :, lanes], b_sems.at[t, g]
            )
            copy.start()
            tile.append(copy)
        tiles.append(tile)
    for t, (n, col) in enumerate(spans):
        if col == 0:
            if t == 0:
                for copy in loads:
                    copy.wait()
            base = parts[n][0] * 2 * (rows // ROWS) + half * (rows // ROWS)
            for r in range(rows // ROWS):
                source = pl.ds(pl.multiple_of(order[base + r] * ROWS, ROWS), ROWS)
                picked[r * ROWS : (r + 1) * ROWS, :] = a[source, :]
        for copy in tiles[t]:
            copy.wait()
        outs[n][:, col : col + 256] = lax.dot_general(
            picked[...], b[t], (((1,), (1,)), ((), ())), preferred_element_type=F32
        )


def product(order, left, right, parts, half, name):
    groups, rows, depth = left.shape
    width = sum(part[2] for part in parts)
    return pl.pallas_call(
        functools.partial(product_kernel, parts, half),
        out_shape=[jax.ShapeDtypeStruct((rows // 2, part[2]), F32) for part in parts],
        in_specs=[
            pl.BlockSpec(memory_space=pltpu.SMEM),
            pl.BlockSpec(memory_space=pltpu.HBM),
            pl.BlockSpec(memory_space=pltpu.HBM),
        ],
        out_specs=[pl.BlockSpec(memory_space=pltpu.VMEM)] * len(parts),
        scratch_shapes=[
            pltpu.VMEM((rows, groups * depth), BF16),
            pltpu.VMEM((width // 256, 256, groups * depth), BF16),
            pltpu.VMEM((rows // 2, groups * depth), BF16),
            pltpu.SemaphoreType.DMA((groups,)),
            pltpu.SemaphoreType.DMA((width // 256, groups)),
        ],
        compiler_params=pltpu.CompilerParams(vmem_limit_bytes=40 * MB),
        cost_estimate=pl.CostEstimate(
            flops=groups * rows * width * depth,
            bytes_accessed=2 * groups * (rows + width) * depth + 2 * rows * width,
            transcendentals=0,
        ),
        name=name,
    )(order, left, right)


def partner_pairs(axis, second):
    pairs = []
    for z, y, x, c in np.ndindex(SIDE, SIDE, SIDE, 2):
        place = {"z": z, "y": y, "x": x}
        flip = (3 if c else 1) ^ (2 if second else 0)
        other = dict(place)
        other[axis] ^= flip
        index = lambda at: ((at["z"] * SIDE + at["y"]) * SIDE + at["x"]) * 2 + c
        pairs.append((index(place), index(other)))
    return pairs


def block_order(axes, place, core):
    flip = jnp.where(core == 0, 1, 3)
    masks = jnp.stack([jnp.full_like(flip, 2), flip, flip ^ 2, jnp.zeros_like(flip)])
    lists = {name: place[name] ^ masks for name in AXES}
    shape = {name: [1, 1, 1] for name in AXES}
    for position, name in enumerate(axes):
        shape[name][position] = SIDE
    at = {name: lists[name].reshape(shape[name]) for name in AXES}
    return (((at["z"] * SIDE + at["y"]) * SIDE + at["x"]).reshape(-1)).astype(jnp.int32)


def per_device(hist_factor, hist_solution, diag_factor, samples):
    slab = hist_factor.shape[1]
    core = lax.axis_index("pcol")
    place = {name: lax.axis_index(name) for name in AXES}
    chip = (place["z"] * SIDE + place["y"]) * SIDE + place["x"]
    core_arg = core.astype(jnp.int32).reshape(1)

    per_core = slab // STRIP
    local = chip % per_core
    info = jnp.stack([local // 2, local % 2]).astype(jnp.int32)
    packed = pack(info, diag_factor.T)
    window = lax.all_gather(packed, AXES, axis=0, tiled=True)

    order = jnp.concatenate([block_order(axes, place, core) for _, _, axes in PARTS])
    parts = [(n, start, width) for n, (start, width, _) in enumerate(PARTS)]
    sends = [
        *product(order, hist_solution, hist_factor, parts[:1], 0, "send_first"),
        *product(order, hist_solution, hist_factor, parts[1:], 0, "send_rest"),
    ]
    keeps = list(product(order, hist_solution, hist_factor, parts, 1, "keep_all"))
    for stage in range(3):
        for second in (False, True):
            got = [
                lax.ppermute(sends[n], EVERY, partner_pairs(PARTS[n][2][stage], second))
                for n in range(len(PARTS))
            ]
            if stage == 2 and second:
                keeps = [keeps[n] + got[n] for n in range(len(PARTS))]
                break
            middle = keeps[0].shape[0] // 2
            sends = [keeps[n][:middle] + got[n][:middle] for n in range(len(PARTS))]
            keeps = [keeps[n][middle:] + got[n][middle:] for n in range(len(PARTS))]
    pending = samples.astype(F32) - jnp.concatenate(keeps, axis=1)

    inv_high, inv_low = grow(core_arg, window, slab)
    first = solve_call(first_kernel, core_arg, (pending,), window, inv_high, inv_low, False, "solve0")
    other = lax.ppermute(first, "pcol", [(0, 1), (1, 0)])
    return solve_call(
        second_kernel, core_arg, (pending, first, other), window, inv_high, inv_low, True, "solve1"
    )


def solution(mesh):
    cube = Mesh(mesh.devices.reshape(SIDE, SIDE, SIDE, 2), EVERY)
    return jax.shard_map(
        per_device,
        mesh=cube,
        in_specs=(
            P(None, "pcol", AXES),
            P(None, None, AXES),
            P("pcol", AXES),
            P(AXES, "pcol"),
        ),
        out_specs=P(AXES, "pcol"),
        check_vma=False,
    )
```

```python
import functools

import jax
import jax.numpy as jnp
import numpy as np
from jax import lax
from jax.experimental import pallas as pl
from jax.experimental.pallas import tpu as pltpu
from jax.sharding import Mesh
from jax.sharding import PartitionSpec as P

F32 = jnp.float32
BF16 = jnp.bfloat16
SIDE = 4
ROWS = 16
STRIP = 64
BLOCK = 512
AXES = ("z", "y", "x")
EVERY = ("z", "y", "x", "pcol")
PARTS = ((0, 1024, "zyx"), (1024, 1024, "zxy"))
GATHER = ("yx", "xy")
MB = 1 << 20


def split2(value):
    high = value.astype(BF16)
    return high, (value - high.astype(F32)).astype(BF16)


def dot(a, b):
    return jnp.dot(a, b, preferred_element_type=F32)


def dot_exact(a, b):
    high, low = split2(a)
    rows = a.shape[0]
    both = dot(jnp.concatenate([high, low], axis=0), b)
    return both[:rows] + both[rows:]


def dot_pair(a, b_high, b_low):
    high, low = split2(a)
    rows = a.shape[0]
    both = dot(jnp.concatenate([high, low], axis=0), b_high)
    return both[:rows] + both[rows:] + dot(high, b_low)


def grow_kernel(chips, own_a, got_a, own_b, got_b, lower, below, out_high, out_low, small, sems):
    slab = lower.shape[0]
    half = slab // 2
    for n, (own, got) in enumerate(((own_a, got_a), (own_b, got_b))):
        share = own.shape[0] // 8
        for position in range(16):
            source = own if position < 8 else got
            base = (position % 8) * share
            row = pl.multiple_of(chips[16 * n + position] * STRIP, STRIP)
            if n == 0:
                moves = (
                    (base, STRIP, lower, row, 0),
                    (base + STRIP, STRIP // 2, lower, half + row, 0),
                )
            else:
                moves = (
                    (base, STRIP // 2, lower, half + row + STRIP // 2, 0),
                    (base + STRIP // 2, STRIP, below, row, 1),
                )
            for start, count, target, to, sem in moves:
                pltpu.make_async_copy(
                    source.at[pl.ds(start, count)],
                    target.at[pl.ds(pl.multiple_of(to, STRIP // 2), count)],
                    sems.at[sem],
                ).start()
    pltpu.make_async_copy(lower, lower, sems.at[0]).wait()

    rows = lax.broadcasted_iota(jnp.int32, (STRIP, 128), 0)
    lanes = lax.broadcasted_iota(jnp.int32, (STRIP, 128), 1)
    left = lanes < STRIP
    inner = jnp.where(left, lanes, lanes - STRIP)
    together = 4

    def invert(group, carry):
        todo, upper, scale = [], [], []
        for n in range(together):
            start = pl.multiple_of((group * together + n) * 128, 128)
            cols = pl.ds(start, 128)
            first = lower[pl.ds(start, STRIP), cols].astype(F32)
            second = lower[pl.ds(start + STRIP, STRIP), cols].astype(F32)
            block = jnp.where(left, first, second)
            diagonal = jnp.where(inner == rows, block, 0.0)
            one = jnp.sum(jnp.where(left, diagonal, 0.0), axis=1, keepdims=True)
            two = jnp.sum(jnp.where(left, 0.0, diagonal), axis=1, keepdims=True)
            upper.append(jnp.where(inner > rows, block, 0.0))
            scale.append(jnp.where(left, 1.0 / one, 1.0 / two))
            todo.append(jnp.where(inner == rows, 1.0, 0.0))
        for k in range(STRIP - 1, 0, -1):
            top = min(STRIP, (k + 7) // 8 * 8)
            for n in range(together):
                row = todo[n][k : k + 1, :] * scale[n][k : k + 1, :]
                col = jnp.where(
                    left[:top], upper[n][:top, k : k + 1], upper[n][:top, STRIP + k : STRIP + k + 1]
                )
                changed = todo[n][:top] - col * row
                todo[n] = (
                    changed if top == STRIP else jnp.concatenate([changed, todo[n][top:]], axis=0)
                )
        for n in range(together):
            small[group * together + n] = todo[n] * scale[n]
        return carry

    lax.fori_loop(0, slab // 128 // together, invert, 0)

    rows = lax.broadcasted_iota(jnp.int32, (128, 128), 0)
    lanes = lax.broadcasted_iota(jnp.int32, (128, 128), 1)
    corner = (rows < STRIP) & (lanes >= STRIP)
    same = (rows < STRIP) == (lanes < STRIP)
    level = []
    for k in range(slab // 128):
        rng = slice(k * 128, k * 128 + 128)
        both = jnp.where(same, jnp.concatenate([small[k], small[k]], axis=0), 0.0)
        off = jnp.where(corner, lower[rng, rng].astype(F32), 0.0).astype(BF16)
        level.append(both - dot_pair(dot_exact(both, off), *split2(both)))
    size = 128
    while size < BLOCK:
        grown = []
        for n in range(0, len(level), 2):
            start = n * size
            off = lower[start : start + size, start + size : start + 2 * size]
            high, low = split2(level[n + 1])
            corner_block = -dot_pair(dot_exact(level[n], off), high, low)
            if 2 * size < BLOCK:
                top = jnp.concatenate([level[n], corner_block], axis=1)
                bottom = jnp.concatenate([jnp.zeros_like(corner_block), level[n + 1]], axis=1)
                grown.append(jnp.concatenate([top, bottom], axis=0))
            else:
                b = n // 2
                corner_high, corner_low = split2(corner_block)
                first_high, first_low = split2(level[n])
                zero = jnp.zeros((size, size), BF16)
                for ref, first, mixed, second in (
                    (out_high, first_high, corner_high, high),
                    (out_low, first_low, corner_low, low),
                ):
                    ref[b, :size, :size] = first
                    ref[b, :size, size:] = mixed
                    ref[b, size:, :size] = zero
                    ref[b, size:, size:] = second
        level = grown
        size *= 2
    pltpu.make_async_copy(below, below, sems.at[1]).wait()


def grow(chips, pieces, slab):
    inverse = jax.ShapeDtypeStruct((slab // BLOCK, BLOCK, BLOCK), BF16)
    vmem = pl.BlockSpec(memory_space=pltpu.VMEM)
    return pl.pallas_call(
        grow_kernel,
        out_shape=(
            jax.ShapeDtypeStruct((slab, slab), BF16),
            jax.ShapeDtypeStruct((slab // 2, slab), BF16),
            inverse,
            inverse,
        ),
        in_specs=[pl.BlockSpec(memory_space=pltpu.SMEM)] + [pl.BlockSpec(memory_space=pltpu.HBM)] * 4,
        out_specs=[vmem] * 4,
        scratch_shapes=[
            pltpu.VMEM((slab // 128, STRIP, 128), F32),
            pltpu.SemaphoreType.DMA((2,)),
        ],
        compiler_params=pltpu.CompilerParams(vmem_limit_bytes=36 * MB),
        cost_estimate=pl.CostEstimate(
            flops=4 * 10**9, bytes_accessed=4 * slab * slab, transcendentals=0
        ),
        name="grow_inverse",
    )(chips, *pieces)


def solve_block(blocks, pending, factor, high, low, out, wait, after):
    for b in range(blocks):
        cols = slice(b * BLOCK, (b + 1) * BLOCK)
        wait(b)
        y = dot_pair(pending[:, cols], high[b], low[b])
        out[: pending.shape[0], cols] = y
        if b + 1 < blocks:
            rest = slice((b + 1) * BLOCK, blocks * BLOCK)
            pending[:, rest] = pending[:, rest] - dot_exact(y, factor[cols, rest])
        after(b, y)


def solve_copies(lower, inv_high, inv_low, factor, high, low, sems):
    copies = []
    slab = lower.shape[1]
    for b in range(slab // BLOCK):
        group = [
            pltpu.make_async_copy(inv_high.at[b], high.at[b], sems.at[0, b]),
            pltpu.make_async_copy(inv_low.at[b], low.at[b], sems.at[1, b]),
        ]
        if (b + 1) * BLOCK < slab:
            rest = pl.ds((b + 1) * BLOCK, slab - (b + 1) * BLOCK)
            rows = pl.ds(b * BLOCK, BLOCK)
            group.append(
                pltpu.make_async_copy(
                    lower.at[rows, rest], factor.at[rows, rest], sems.at[2, b]
                )
            )
        copies.append(group)
    return copies


def below_copies(below, under, sems):
    copies = []
    for b in range(below.shape[0] // BLOCK):
        rows = pl.ds(b * BLOCK, BLOCK)
        copies.append(pltpu.make_async_copy(below.at[rows], under.at[rows], sems.at[3, b]))
    return copies


def first_kernel(
    core, right, lower, below, inv_high, inv_low, out, factor, under, high, low, pending, sems
):
    rows, slab = right.shape

    @pl.when(core[0] == 0)
    def _():
        copies = solve_copies(lower, inv_high, inv_low, factor, high, low, sems)
        belows = below_copies(below, under, sems)
        for b, group in enumerate(copies):
            for copy in group:
                copy.start()
            if b < len(belows):
                belows[b].start()
        pending[...] = right[...]

        def wait(b):
            for copy in copies[b]:
                copy.wait()

        def after(b, y):
            if b < len(belows):
                belows[b].wait()
                term = dot_exact(y, under[b * BLOCK : (b + 1) * BLOCK, :])
                out[rows:, :] = term if b == 0 else out[rows:, :] + term

        solve_block(slab // BLOCK, pending, factor, high, low, out, wait, after)

    @pl.when(core[0] != 0)
    def _():
        out[...] = jnp.zeros_like(out)


def second_kernel(
    core, right, own, other, lower, below, inv_high, inv_low, out, factor, under, high, low, pending, sems
):
    rows, slab = right.shape
    half = slab // 2

    @pl.when(core[0] != 0)
    def _():
        copies = solve_copies(lower, inv_high, inv_low, factor, high, low, sems)
        belows = below_copies(below, under, sems)
        for copy in belows:
            copy.start()
        for group in copies:
            for copy in group:
                copy.start()
        pending[...] = right[...] - other[rows:, :]
        for b, copy in enumerate(belows):
            copy.wait()
            cols = slice(half + b * BLOCK, half + (b + 1) * BLOCK)
            term = dot_exact(other[:rows, cols], under[b * BLOCK : (b + 1) * BLOCK, :])
            pending[...] = pending[...] - term

        def wait(b):
            for copy in copies[b]:
                copy.wait()

        solve_block(slab // BLOCK, pending, factor, high, low, out, wait, lambda b, y: None)

    @pl.when(core[0] == 0)
    def _():
        out[...] = own[:rows, :]


def solve_call(kernel, core, dense, factor, out_rows, name):
    rows, slab = dense[0].shape
    blocks = slab // BLOCK
    vmem = pl.BlockSpec(memory_space=pltpu.VMEM)
    return pl.pallas_call(
        kernel,
        out_shape=jax.ShapeDtypeStruct((out_rows, slab), F32),
        in_specs=[pl.BlockSpec(memory_space=pltpu.SMEM)]
        + [vmem] * len(dense)
        + [pl.BlockSpec(memory_space=pl.ANY)] * 4,
        out_specs=vmem,
        scratch_shapes=[
            pltpu.VMEM((slab, slab), BF16),
            pltpu.VMEM((slab // 2, slab), BF16),
            pltpu.VMEM((blocks, BLOCK, BLOCK), BF16),
            pltpu.VMEM((blocks, BLOCK, BLOCK), BF16),
            pltpu.VMEM((rows, slab), F32),
            pltpu.SemaphoreType.DMA((4, blocks)),
        ],
        compiler_params=pltpu.CompilerParams(vmem_limit_bytes=28 * MB),
        name=name,
    )(core, *dense, *factor)


def product_kernel(parts, half, order, left, right, *refs):
    outs, (a, b, picked, a_sems, b_sems) = refs[: len(parts)], refs[len(parts) :]
    groups, _, depth = left.shape
    rows = picked.shape[0]
    loads = []
    for g in range(groups):
        lanes = pl.ds(g * depth, depth)
        copy = pltpu.make_async_copy(left.at[g], a.at[:, lanes], a_sems.at[g])
        copy.start()
        loads.append(copy)
    tiles = []
    for n, (_, start, width) in enumerate(parts):
        tile = []
        for g in range(groups):
            lanes = pl.ds(g * depth, depth)
            copy = pltpu.make_async_copy(
                right.at[g, pl.ds(start, width)], b.at[n, :, lanes], b_sems.at[n, g]
            )
            copy.start()
            tile.append(copy)
        tiles.append(tile)
    for copy in loads:
        copy.wait()
    for n, (number, _, _) in enumerate(parts):
        base = (2 * number + half) * (rows // ROWS)
        for r in range(rows // ROWS):
            source = pl.ds(pl.multiple_of(order[base + r] * ROWS, ROWS), ROWS)
            picked[r * ROWS : (r + 1) * ROWS, :] = a[source, :]
        for copy in tiles[n]:
            copy.wait()
        outs[n][...] = lax.dot_general(
            picked[...], b[n], (((1,), (1,)), ((), ())), preferred_element_type=F32
        )


def product(order, left, right, parts, half, name):
    groups, rows, depth = left.shape
    width = sum(part[2] for part in parts)
    return pl.pallas_call(
        functools.partial(product_kernel, parts, half),
        out_shape=[jax.ShapeDtypeStruct((rows // 2, part[2]), F32) for part in parts],
        in_specs=[
            pl.BlockSpec(memory_space=pltpu.SMEM),
            pl.BlockSpec(memory_space=pltpu.HBM),
            pl.BlockSpec(memory_space=pltpu.HBM),
        ],
        out_specs=[pl.BlockSpec(memory_space=pltpu.VMEM)] * len(parts),
        scratch_shapes=[
            pltpu.VMEM((rows, groups * depth), BF16),
            pltpu.VMEM((len(parts), parts[0][2], groups * depth), BF16),
            pltpu.VMEM((rows // 2, groups * depth), BF16),
            pltpu.SemaphoreType.DMA((groups,)),
            pltpu.SemaphoreType.DMA((len(parts), groups)),
        ],
        compiler_params=pltpu.CompilerParams(vmem_limit_bytes=40 * MB),
        cost_estimate=pl.CostEstimate(
            flops=groups * rows * width * depth,
            bytes_accessed=2 * groups * (rows + width) * depth + 2 * rows * width,
            transcendentals=0,
        ),
        name=name,
    )(order, left, right)


def chip_index(z, y, x, c):
    return ((z * SIDE + y) * SIDE + x) * 2 + c


def flip_pairs(axis, masks):
    pairs = []
    for z, y, x, c in np.ndindex(SIDE, SIDE, SIDE, 2):
        place = {"z": z, "y": y, "x": x}
        place[axis] ^= masks[c]
        pairs.append((chip_index(z, y, x, c), chip_index(place["z"], place["y"], place["x"], c)))
    return pairs


def partner_pairs(axis, second):
    return flip_pairs(axis, (3, 1) if second else (1, 3))


def block_order(axes, place, core):
    flip = jnp.where(core == 0, 1, 3)
    masks = jnp.stack([jnp.full_like(flip, 2), flip, flip ^ 2, jnp.zeros_like(flip)])
    lists = {name: place[name] ^ masks for name in AXES}
    shape = {name: [1, 1, 1] for name in AXES}
    for position, name in enumerate(axes):
        shape[name][position] = SIDE
    at = {name: lists[name].reshape(shape[name]) for name in AXES}
    return (((at["z"] * SIDE + at["y"]) * SIDE + at["x"]).reshape(-1)).astype(jnp.int32)


def gather_factor(strip, place, core):
    z = place["z"]
    pairs = [
        (chip_index(0, y, x, 1), chip_index(0, y, x, 0)) for y in range(SIDE) for x in range(SIDE)
    ]
    got = lax.ppermute(strip, EVERY, pairs)
    under = jnp.where(core == 0, got, strip)
    got = lax.ppermute(jnp.concatenate([strip, under]), EVERY, flip_pairs("z", (2, 2)))
    home = (z < 2) == (core == 0)
    mine = jnp.where(home, strip, got[:STRIP])
    under = jnp.where(z < 2, under, got[STRIP:])
    got = lax.ppermute(jnp.concatenate([mine, under]), EVERY, flip_pairs("z", (1, 1)))
    even = z % 2 == 0
    first = jnp.where(even, mine, got[:STRIP])
    second = jnp.where(even, got[:STRIP], mine)
    under = jnp.where(z % 2 == core, under, got[STRIP:])
    cut = STRIP // 2
    held = [
        jnp.concatenate([first, second[:cut]]),
        jnp.concatenate([second[cut:], under]),
    ]
    pieces = [None, None]
    for step in range(4):
        got = [
            lax.ppermute(held[n], EVERY, partner_pairs(GATHER[n][step // 2], step % 2 == 1))
            for n in range(2)
        ]
        if step == 3:
            pieces = [held[0], got[0], held[1], got[1]]
        else:
            held = [jnp.concatenate([held[n], got[n]]) for n in range(2)]
    flip = jnp.where(core == 0, 1, 3)
    masks = jnp.stack([jnp.zeros_like(flip), flip, flip ^ 2, jnp.full_like(flip, 2)])
    ys, xs = place["y"] ^ masks, place["x"] ^ masks
    chips = [
        ys[None, :] * SIDE + xs[:, None],
        ys[:, None] * SIDE + xs[None, :],
    ]
    return pieces, jnp.concatenate([c.reshape(-1) for c in chips]).astype(jnp.int32)


def per_device(hist_factor, hist_solution, diag_factor, samples):
    slab = hist_factor.shape[1]
    core = lax.axis_index("pcol")
    place = {name: lax.axis_index(name) for name in AXES}
    core_arg = core.astype(jnp.int32).reshape(1)

    order = jnp.concatenate([block_order(axes, place, core) for _, _, axes in PARTS])
    parts = [(n, start, width) for n, (start, width, _) in enumerate(PARTS)]
    sends = [
        *product(order, hist_solution, hist_factor, parts[:1], 0, "send_first"),
        *product(order, hist_solution, hist_factor, parts[1:], 0, "send_rest"),
    ]
    keeps = list(product(order, hist_solution, hist_factor, parts, 1, "keep_all"))

    pieces, chips = gather_factor(diag_factor.T, place, core)
    factor = grow(chips, pieces, slab)

    for step in range(6):
        got = [
            lax.ppermute(sends[n], EVERY, partner_pairs(PARTS[n][2][step // 2], step % 2 == 1))
            for n in range(len(PARTS))
        ]
        if step == 5:
            keeps = [keeps[n] + got[n] for n in range(len(PARTS))]
        else:
            middle = keeps[0].shape[0] // 2
            sends = [keeps[n][:middle] + got[n][:middle] for n in range(len(PARTS))]
            keeps = [keeps[n][middle:] + got[n][middle:] for n in range(len(PARTS))]
    pending = samples.astype(F32) - jnp.concatenate(keeps, axis=1)

    first = solve_call(first_kernel, core_arg, (pending,), factor, 2 * ROWS, "solve0")
    other = lax.ppermute(first, "pcol", [(0, 1)])
    return solve_call(second_kernel, core_arg, (pending, first, other), factor, ROWS, "solve1")


def solution(mesh):
    cube = Mesh(mesh.devices.reshape(SIDE, SIDE, SIDE, 2), EVERY)
    return jax.shard_map(
        per_device,
        mesh=cube,
        in_specs=(
            P(None, "pcol", AXES),
            P(None, None, AXES),
            P("pcol", AXES),
            P(AXES, "pcol"),
        ),
        out_specs=P(AXES, "pcol"),
        check_vma=False,
    )
```

```python
import functools

import jax
import jax.numpy as jnp
import numpy as np
from jax import lax
from jax.experimental import pallas as pl
from jax.experimental.pallas import tpu as pltpu
from jax.sharding import Mesh
from jax.sharding import PartitionSpec as P

F32 = jnp.float32
BF16 = jnp.bfloat16
SIDE = 4
ROWS = 16
STRIP = 64
BLOCK = 512
AXES = ("z", "y", "x")
EVERY = ("z", "y", "x", "pcol")
PARTS = ((0, 1024, "zyx"), (1024, 1024, "zxy"))
GATHER = ("yx", "xy")
MB = 1 << 20


def split2(value):
    high = value.astype(BF16)
    return high, (value - high.astype(F32)).astype(BF16)


def dot(a, b):
    return jnp.dot(a, b, preferred_element_type=F32)


def dot_exact(a, b):
    high, low = split2(a)
    rows = a.shape[0]
    both = dot(jnp.concatenate([high, low], axis=0), b)
    return both[:rows] + both[rows:]


def dot_pair(a, b_high, b_low):
    high, low = split2(a)
    rows = a.shape[0]
    both = dot(jnp.concatenate([high, low], axis=0), b_high)
    return both[:rows] + both[rows:] + dot(high, b_low)


def grow_kernel(chips, own_a, got_a, own_b, got_b, lower, below, out_high, out_low, sems):
    slab = lower.shape[0]
    half = slab // 2
    for n, (own, got) in enumerate(((own_a, got_a), (own_b, got_b))):
        share = own.shape[0] // 8
        for position in range(16):
            source = own if position < 8 else got
            base = (position % 8) * share
            row = pl.multiple_of(chips[16 * n + position] * STRIP, STRIP)
            if n == 0:
                moves = (
                    (base, STRIP, lower, row, 0),
                    (base + STRIP, STRIP // 2, lower, half + row, 0),
                )
            else:
                moves = (
                    (base, STRIP // 2, lower, half + row + STRIP // 2, 0),
                    (base + STRIP // 2, STRIP, below, row, 1),
                )
            for start, count, target, to, sem in moves:
                pltpu.make_async_copy(
                    source.at[pl.ds(start, count)],
                    target.at[pl.ds(pl.multiple_of(to, STRIP // 2), count)],
                    sems.at[sem],
                ).start()
    pltpu.make_async_copy(lower, lower, sems.at[0]).wait()

    rows = lax.broadcasted_iota(jnp.int32, (128, 128), 0)
    lanes = lax.broadcasted_iota(jnp.int32, (128, 128), 1)
    corner = (rows < STRIP) & (lanes >= STRIP)
    same = (rows < STRIP) == (lanes < STRIP)
    upright, turned = [], []
    for k in range(half // 128):
        rng = slice(half + k * 128, half + k * 128 + 128)
        pair = lower[rng, :128].astype(F32) + lower[rng, 128:256].astype(F32)
        swapped = pltpu.roll(pair, STRIP, 1)
        upright.append(jnp.where(same, jnp.where(rows < STRIP, pair, swapped), 0.0))
        turned.append(jnp.where(same, jnp.where(rows < STRIP, swapped, pair), 0.0))
    level = []
    for k, both in enumerate(upright + turned):
        rng = slice(k * 128, k * 128 + 128)
        off = jnp.where(corner, lower[rng, rng].astype(F32), 0.0).astype(BF16)
        level.append(both - dot_pair(dot_exact(both, off), *split2(both)))
    size = 128
    while size < BLOCK:
        grown = []
        for n in range(0, len(level), 2):
            start = n * size
            off = lower[start : start + size, start + size : start + 2 * size]
            high, low = split2(level[n + 1])
            corner_block = -dot_pair(dot_exact(level[n], off), high, low)
            if 2 * size < BLOCK:
                top = jnp.concatenate([level[n], corner_block], axis=1)
                bottom = jnp.concatenate([jnp.zeros_like(corner_block), level[n + 1]], axis=1)
                grown.append(jnp.concatenate([top, bottom], axis=0))
            else:
                b = n // 2
                corner_high, corner_low = split2(corner_block)
                first_high, first_low = split2(level[n])
                zero = jnp.zeros((size, size), BF16)
                for ref, first, mixed, second in (
                    (out_high, first_high, corner_high, high),
                    (out_low, first_low, corner_low, low),
                ):
                    ref[b, :size, :size] = first
                    ref[b, :size, size:] = mixed
                    ref[b, size:, :size] = zero
                    ref[b, size:, size:] = second
        level = grown
        size *= 2
    pltpu.make_async_copy(below, below, sems.at[1]).wait()


def grow(chips, pieces, slab):
    inverse = jax.ShapeDtypeStruct((slab // BLOCK, BLOCK, BLOCK), BF16)
    vmem = pl.BlockSpec(memory_space=pltpu.VMEM)
    return pl.pallas_call(
        grow_kernel,
        out_shape=(
            jax.ShapeDtypeStruct((slab, slab), BF16),
            jax.ShapeDtypeStruct((slab // 2, slab), BF16),
            inverse,
            inverse,
        ),
        in_specs=[pl.BlockSpec(memory_space=pltpu.SMEM)] + [pl.BlockSpec(memory_space=pltpu.HBM)] * 4,
        out_specs=[vmem] * 4,
        scratch_shapes=[pltpu.SemaphoreType.DMA((2,))],
        compiler_params=pltpu.CompilerParams(vmem_limit_bytes=36 * MB),
        cost_estimate=pl.CostEstimate(
            flops=4 * 10**9, bytes_accessed=4 * slab * slab, transcendentals=0
        ),
        name="grow_inverse",
    )(chips, *pieces)


def solve_block(blocks, pending, factor, high, low, out, wait, after):
    for b in range(blocks):
        cols = slice(b * BLOCK, (b + 1) * BLOCK)
        wait(b)
        y = dot_pair(pending[:, cols], high[b], low[b])
        out[: pending.shape[0], cols] = y
        if b + 1 < blocks:
            rest = slice((b + 1) * BLOCK, blocks * BLOCK)
            pending[:, rest] = pending[:, rest] - dot_exact(y, factor[cols, rest])
        after(b, y)


def solve_copies(lower, inv_high, inv_low, factor, high, low, sems):
    copies = []
    slab = lower.shape[1]
    for b in range(slab // BLOCK):
        group = [
            pltpu.make_async_copy(inv_high.at[b], high.at[b], sems.at[0, b]),
            pltpu.make_async_copy(inv_low.at[b], low.at[b], sems.at[1, b]),
        ]
        if (b + 1) * BLOCK < slab:
            rest = pl.ds((b + 1) * BLOCK, slab - (b + 1) * BLOCK)
            rows = pl.ds(b * BLOCK, BLOCK)
            group.append(
                pltpu.make_async_copy(
                    lower.at[rows, rest], factor.at[rows, rest], sems.at[2, b]
                )
            )
        copies.append(group)
    return copies


def below_copies(below, under, sems):
    copies = []
    for b in range(below.shape[0] // BLOCK):
        rows = pl.ds(b * BLOCK, BLOCK)
        copies.append(pltpu.make_async_copy(below.at[rows], under.at[rows], sems.at[3, b]))
    return copies


def first_kernel(
    core, right, lower, below, inv_high, inv_low, out, factor, under, high, low, pending, sems
):
    rows, slab = right.shape

    @pl.when(core[0] == 0)
    def _():
        copies = solve_copies(lower, inv_high, inv_low, factor, high, low, sems)
        belows = below_copies(below, under, sems)
        for b, group in enumerate(copies):
            for copy in group:
                copy.start()
            if b < len(belows):
                belows[b].start()
        pending[...] = right[...]

        def wait(b):
            for copy in copies[b]:
                copy.wait()

        def after(b, y):
            if b < len(belows):
                belows[b].wait()
                term = dot_exact(y, under[b * BLOCK : (b + 1) * BLOCK, :])
                out[rows:, :] = term if b == 0 else out[rows:, :] + term

        solve_block(slab // BLOCK, pending, factor, high, low, out, wait, after)

    @pl.when(core[0] != 0)
    def _():
        out[...] = jnp.zeros_like(out)


def second_kernel(
    core, right, own, other, lower, below, inv_high, inv_low, out, factor, under, high, low, pending, sems
):
    rows, slab = right.shape
    half = slab // 2

    @pl.when(core[0] != 0)
    def _():
        copies = solve_copies(lower, inv_high, inv_low, factor, high, low, sems)
        belows = below_copies(below, under, sems)
        for copy in belows:
            copy.start()
        for group in copies:
            for copy in group:
                copy.start()
        pending[...] = right[...] - other[rows:, :]
        for b, copy in enumerate(belows):
            copy.wait()
            cols = slice(half + b * BLOCK, half + (b + 1) * BLOCK)
            term = dot_exact(other[:rows, cols], under[b * BLOCK : (b + 1) * BLOCK, :])
            pending[...] = pending[...] - term

        def wait(b):
            for copy in copies[b]:
                copy.wait()

        solve_block(slab // BLOCK, pending, factor, high, low, out, wait, lambda b, y: None)

    @pl.when(core[0] == 0)
    def _():
        out[...] = own[:rows, :]


def solve_call(kernel, core, dense, factor, out_rows, name):
    rows, slab = dense[0].shape
    blocks = slab // BLOCK
    vmem = pl.BlockSpec(memory_space=pltpu.VMEM)
    return pl.pallas_call(
        kernel,
        out_shape=jax.ShapeDtypeStruct((out_rows, slab), F32),
        in_specs=[pl.BlockSpec(memory_space=pltpu.SMEM)]
        + [vmem] * len(dense)
        + [pl.BlockSpec(memory_space=pl.ANY)] * 4,
        out_specs=vmem,
        scratch_shapes=[
            pltpu.VMEM((slab, slab), BF16),
            pltpu.VMEM((slab // 2, slab), BF16),
            pltpu.VMEM((blocks, BLOCK, BLOCK), BF16),
            pltpu.VMEM((blocks, BLOCK, BLOCK), BF16),
            pltpu.VMEM((rows, slab), F32),
            pltpu.SemaphoreType.DMA((4, blocks)),
        ],
        compiler_params=pltpu.CompilerParams(vmem_limit_bytes=56 * MB),
        name=name,
    )(core, *dense, *factor)


def product_kernel(parts, half, order, left, right, _, *refs):
    outs, (a, b, picked, a_sems, b_sems) = refs[: len(parts)], refs[len(parts) :]
    groups, _, depth = left.shape
    rows = picked.shape[0]
    slab = rows // 2
    step = b.shape[1]
    spans = [(n, col) for n in range(len(parts)) for col in range(0, parts[n][2], step)]
    lanes = [pl.ds(g * depth, depth) for g in range(groups)]

    def slabs(n):
        copies = []
        for h in range(2):
            block = order[(2 * parts[n][0] + half) * (rows // ROWS) + h * (slab // ROWS)]
            source = pl.ds(pl.multiple_of(block // (slab // ROWS) * slab, slab), slab)
            for g in range(groups):
                copies.append(
                    pltpu.make_async_copy(
                        left.at[g, source], a.at[pl.ds(h * slab, slab), lanes[g]], a_sems.at[h, g]
                    )
                )
        return copies

    loads = slabs(0)
    for copy in loads:
        copy.start()
    tiles = []
    for t, (n, col) in enumerate(spans):
        tile = [
            pltpu.make_async_copy(
                right.at[g, pl.ds(parts[n][1] + col, step)], b.at[t, :, lanes[g]], b_sems.at[t, g]
            )
            for g in range(groups)
        ]
        for copy in tile:
            copy.start()
        tiles.append(tile)
    for copy in loads:
        copy.wait()
    for t, (n, col) in enumerate(spans):
        if col == 0:
            base = (2 * parts[n][0] + half) * (rows // ROWS)
            for r in range(rows // ROWS):
                inside = order[base + r] % (slab // ROWS) + r // (slab // ROWS) * (slab // ROWS)
                source = pl.ds(pl.multiple_of(inside * ROWS, ROWS), ROWS)
                picked[r * ROWS : (r + 1) * ROWS, :] = a[source, :]
        for copy in tiles[t]:
            copy.wait()
        outs[n][:, col : col + step] = lax.dot_general(
            picked[...], b[t], (((1,), (1,)), ((), ())), preferred_element_type=F32
        )


def product(order, left, right, token, parts, half, name):
    groups, rows, depth = left.shape
    width = sum(part[2] for part in parts)
    step = 512
    return pl.pallas_call(
        functools.partial(product_kernel, parts, half),
        out_shape=[jax.ShapeDtypeStruct((rows // 2, part[2]), F32) for part in parts],
        in_specs=[pl.BlockSpec(memory_space=pltpu.SMEM)] + [pl.BlockSpec(memory_space=pltpu.HBM)] * 3,
        out_specs=[pl.BlockSpec(memory_space=pltpu.VMEM)] * len(parts),
        scratch_shapes=[
            pltpu.VMEM((rows // 2, groups * depth), BF16),
            pltpu.VMEM((width // step, step, groups * depth), BF16),
            pltpu.VMEM((rows // 2, groups * depth), BF16),
            pltpu.SemaphoreType.DMA((2, groups)),
            pltpu.SemaphoreType.DMA((width // step, groups)),
        ],
        compiler_params=pltpu.CompilerParams(vmem_limit_bytes=56 * MB),
        cost_estimate=pl.CostEstimate(
            flops=groups * rows * width * depth,
            bytes_accessed=2 * groups * (rows // 2 + width) * depth + 2 * rows * width,
            transcendentals=0,
        ),
        name=name,
    )(order, left, right, token)


def chip_index(z, y, x, c):
    return ((z * SIDE + y) * SIDE + x) * 2 + c


def flip_pairs(axis, masks):
    pairs = []
    for z, y, x, c in np.ndindex(SIDE, SIDE, SIDE, 2):
        place = {"z": z, "y": y, "x": x}
        place[axis] ^= masks[c]
        pairs.append((chip_index(z, y, x, c), chip_index(place["z"], place["y"], place["x"], c)))
    return pairs


def partner_pairs(axis, second):
    return flip_pairs(axis, (3, 1) if second else (1, 3))


def block_order(axes, place, core):
    flip = jnp.where(core == 0, 1, 3)
    masks = jnp.stack([jnp.full_like(flip, 2), flip, flip ^ 2, jnp.zeros_like(flip)])
    lists = {name: place[name] ^ masks for name in AXES}
    shape = {name: [1, 1, 1] for name in AXES}
    for position, name in enumerate(axes):
        shape[name][position] = SIDE
    at = {name: lists[name].reshape(shape[name]) for name in AXES}
    return (((at["z"] * SIDE + at["y"]) * SIDE + at["x"]).reshape(-1)).astype(jnp.int32)


def pair_kernel(flags, strip, got, both):
    both[:STRIP] = strip[...]
    both[STRIP:] = jnp.where(flags[0] > 0, strip[...], got[...])


def choose_kernel(flags, held, got, _, both):
    both[:STRIP] = jnp.where(flags[1] > 0, held[:STRIP], got[:STRIP])
    both[STRIP:] = jnp.where(flags[2] > 0, held[STRIP:], got[STRIP:])


def pack_kernel(flags, held, got, _, out_a, out_b, odd):
    mine = flags[3] > 0
    width = held.shape[1]
    cut = STRIP // 2
    even = out_a.at[:STRIP]
    even[...] = jnp.where(mine, held[:STRIP], got[:STRIP])
    odd[...] = jnp.where(mine, got[:STRIP], held[:STRIP])
    out_b[cut:] = jnp.where(mine, held[STRIP:], got[STRIP:])

    at = pl.multiple_of(flags[4] * 128, 128)
    turn = flags[5] > 0
    one = even[:, pl.ds(at, 128)].astype(F32)
    two = odd[:, pl.ds(pl.multiple_of(at + width // 2, 128), 128)].astype(F32)
    one = jnp.where(turn, pltpu.roll(one, STRIP, 1), one)
    two = jnp.where(turn, two, pltpu.roll(two, STRIP, 1))
    rows = lax.broadcasted_iota(jnp.int32, (STRIP, 128), 0)
    lanes = lax.broadcasted_iota(jnp.int32, (STRIP, 128), 1)
    left = lanes < STRIP
    inner = jnp.where(left, lanes, lanes - STRIP)
    block = jnp.where(left, one, two)
    diagonal = jnp.where(inner == rows, block, 0.0)
    scale = jnp.where(
        left,
        1.0 / jnp.sum(jnp.where(left, diagonal, 0.0), axis=1, keepdims=True),
        1.0 / jnp.sum(jnp.where(left, 0.0, diagonal), axis=1, keepdims=True),
    )
    upper = jnp.where(inner > rows, block, 0.0)
    todo = jnp.where(inner == rows, 1.0, 0.0)
    for k in range(STRIP - 1, 0, -1):
        row = todo[k : k + 1, :] * scale[k : k + 1, :]
        col = jnp.where(left, upper[:, k : k + 1], upper[:, STRIP + k : STRIP + k + 1])
        todo = todo - col * row
    high, low = split2(todo * scale)
    odd[:, :128] = high
    odd[:, 128:256] = low
    out_a[STRIP:] = odd[:cut]
    out_b[:cut] = odd[cut:]


def small_call(kernel, name, shapes, scratch, flags, *operands, token=None):
    vmem = pl.BlockSpec(memory_space=pltpu.VMEM)
    tokens = () if token is None else (token,)
    return pl.pallas_call(
        kernel,
        out_shape=[jax.ShapeDtypeStruct(shape, BF16) for shape in shapes],
        in_specs=[pl.BlockSpec(memory_space=pltpu.SMEM)]
        + [vmem] * len(operands)
        + [pl.BlockSpec(memory_space=pl.ANY)] * len(tokens),
        out_specs=[vmem] * len(shapes),
        scratch_shapes=scratch,
        compiler_params=pltpu.CompilerParams(vmem_limit_bytes=16 * MB),
        name=name,
    )(flags, *operands, *tokens)


def gather_order(place, core):
    flip = jnp.where(core == 0, 1, 3)
    masks = jnp.stack([jnp.zeros_like(flip), flip, flip ^ 2, jnp.full_like(flip, 2)])
    ys, xs = place["y"] ^ masks, place["x"] ^ masks
    chips = [
        ys[None, :] * SIDE + xs[:, None],
        ys[:, None] * SIDE + xs[None, :],
    ]
    return jnp.concatenate([c.reshape(-1) for c in chips]).astype(jnp.int32)


def per_device(hist_factor, hist_solution, diag_factor, samples):
    slab = hist_factor.shape[1]
    core = lax.axis_index("pcol")
    place = {name: lax.axis_index(name) for name in AXES}
    core_arg = core.astype(jnp.int32).reshape(1)

    order = jnp.concatenate([block_order(axes, place, core) for _, _, axes in PARTS])
    parts = [(n, start, width) for n, (start, width, _) in enumerate(PARTS)]
    z = place["z"]
    at = place["y"] * SIDE + place["x"]
    outer = (z == 0) | (z == 3)
    flags = jnp.stack(
        [core > 0, (z < 2) == (core == 0), z < 2, outer == (core == 0), at // 2, at % 2]
    ).astype(jnp.int32)
    chips = gather_order(place, core)
    strip = diag_factor.T
    width = strip.shape[1]

    to_first = [
        (chip_index(0, y, x, 1), chip_index(0, y, x, 0)) for y in range(SIDE) for x in range(SIDE)
    ]
    got = lax.ppermute(strip, EVERY, to_first)
    (held,) = small_call(pair_kernel, "pair", [(2 * STRIP, width)], [], flags, strip, got)
    got = lax.ppermute(held, EVERY, flip_pairs("z", (3, 3)))
    (send0,) = product(order, hist_solution, hist_factor, held, parts[:1], 0, "send_first")
    (held,) = small_call(
        choose_kernel, "choose", [(2 * STRIP, width)], [], flags, held, got, token=send0
    )
    got = lax.ppermute(held, EVERY, flip_pairs("z", (1, 1)))
    (send1,) = product(order, hist_solution, hist_factor, held, parts[1:], 0, "send_rest")
    share = STRIP + STRIP // 2
    held = small_call(
        pack_kernel,
        "pack",
        [(share, width)] * 2,
        [pltpu.VMEM((STRIP, width), BF16)],
        flags,
        held,
        got,
        token=send1,
    )
    sends = [send0, send1]
    keeps = list(product(order, hist_solution, hist_factor, held[0], parts, 1, "keep_all"))

    for step in range(4):
        got = [
            lax.ppermute(held[n], EVERY, partner_pairs(GATHER[n][step // 2], step % 2 == 1))
            for n in range(2)
        ]
        if step < 3:
            held = [jnp.concatenate([held[n], got[n]]) for n in range(2)]
    factor = grow(chips, [held[0], got[0], held[1], got[1]], slab)

    for step in range(6):
        got = [
            lax.ppermute(sends[n], EVERY, partner_pairs(PARTS[n][2][step // 2], step % 2 == 1))
            for n in range(len(PARTS))
        ]
        if step == 5:
            keeps = [keeps[n] + got[n] for n in range(len(PARTS))]
        else:
            middle = keeps[0].shape[0] // 2
            sends = [keeps[n][:middle] + got[n][:middle] for n in range(len(PARTS))]
            keeps = [keeps[n][middle:] + got[n][middle:] for n in range(len(PARTS))]
    pending = samples.astype(F32) - jnp.concatenate(keeps, axis=1)

    first = solve_call(first_kernel, core_arg, (pending,), factor, 2 * ROWS, "solve0")
    other = lax.ppermute(first, "pcol", [(0, 1)])
    return solve_call(second_kernel, core_arg, (pending, first, other), factor, ROWS, "solve1")


def solution(mesh):
    cube = Mesh(mesh.devices.reshape(SIDE, SIDE, SIDE, 2), EVERY)
    return jax.shard_map(
        per_device,
        mesh=cube,
        in_specs=(
            P(None, "pcol", AXES),
            P(None, None, AXES),
            P("pcol", AXES),
            P(AXES, "pcol"),
        ),
        out_specs=P(AXES, "pcol"),
        check_vma=False,
    )
```

```python
import functools

import jax
import jax.numpy as jnp
import numpy as np
from jax import lax
from jax.experimental import pallas as pl
from jax.experimental.pallas import tpu as pltpu
from jax.sharding import Mesh
from jax.sharding import PartitionSpec as P

F32 = jnp.float32
BF16 = jnp.bfloat16
SIDE = 4
ROWS = 16
STRIP = 64
BLOCK = 512
AXES = ("z", "y", "x")
EVERY = ("z", "y", "x", "pcol")
PARTS = ((0, 1024, "zyx"), (1024, 1024, "zxy"))
GATHER = ("yx", "xy")
MB = 1 << 20
TOKEN = jax.ShapeDtypeStruct((8, 128), F32)


def split2(value):
    high = value.astype(BF16)
    return high, (value - high.astype(F32)).astype(BF16)


def dot(a, b):
    return jnp.dot(a, b, preferred_element_type=F32)


def dot_exact(a, b):
    high, low = split2(a)
    rows = a.shape[0]
    both = dot(jnp.concatenate([high, low], axis=0), b)
    return both[:rows] + both[rows:]


def dot_pair(a, b_high, b_low):
    high, low = split2(a)
    rows = a.shape[0]
    both = dot(jnp.concatenate([high, low], axis=0), b_high)
    return both[:rows] + both[rows:] + dot(high, b_low)


def strip_copies(chips, pieces, lower, below, sems):
    own_a, got_a, own_b, got_b = pieces
    half = lower.shape[0] // 2
    cut = STRIP // 2
    groups = ([], [], [])

    def add(group, source, start, count, target, to):
        groups[group].append(
            pltpu.make_async_copy(
                source.at[pl.ds(start, count)],
                target.at[pl.ds(pl.multiple_of(to, cut), count)],
                sems.at[group],
            )
        )

    for position in range(16):
        base = (position % 8) * (STRIP + cut)
        row = pl.multiple_of(chips[position] * STRIP, STRIP)
        source = own_a if position < 8 else got_a
        add(0, source, base, STRIP, lower, row)
        add(1, source, base + STRIP, cut, lower, half + row)
        row = pl.multiple_of(chips[16 + position] * STRIP, STRIP)
        source = own_b if position < 8 else got_b
        add(1, source, base, cut, lower, half + row + cut)
        if below is not None:
            add(2, source, base + cut, STRIP, below, row)
    return groups


def start_all(copies):
    for copy in copies:
        copy.start()


def wait_for(target, sem):
    pltpu.make_async_copy(target, target, sem).wait()


def grow_kernel(chips, own_a, got_a, own_b, got_b, out_high, out_low, token, lower, sems):
    slab = lower.shape[0]
    half = slab // 2
    even, odd, _ = strip_copies(chips, (own_a, got_a, own_b, got_b), lower, None, sems)
    start_all(even)
    start_all(odd)
    token[...] = jnp.zeros_like(token)
    wait_for(lower.at[:half], sems.at[0])
    wait_for(lower.at[half:], sems.at[1])

    rows = lax.broadcasted_iota(jnp.int32, (128, 128), 0)
    lanes = lax.broadcasted_iota(jnp.int32, (128, 128), 1)
    corner = (rows < STRIP) & (lanes >= STRIP)
    same = (rows < STRIP) == (lanes < STRIP)
    upright, turned = [], []
    for k in range(half // 128):
        rng = slice(half + k * 128, half + k * 128 + 128)
        pair = lower[rng, :128].astype(F32) + lower[rng, 128:256].astype(F32)
        swapped = pltpu.roll(pair, STRIP, 1)
        upright.append(jnp.where(same, jnp.where(rows < STRIP, pair, swapped), 0.0))
        turned.append(jnp.where(same, jnp.where(rows < STRIP, swapped, pair), 0.0))
    level = []
    for k, both in enumerate(upright + turned):
        rng = slice(k * 128, k * 128 + 128)
        off = jnp.where(corner, lower[rng, rng].astype(F32), 0.0).astype(BF16)
        level.append(both - dot_pair(dot_exact(both, off), *split2(both)))
    size = 128
    while size < BLOCK:
        grown = []
        for n in range(0, len(level), 2):
            start = n * size
            off = lower[start : start + size, start + size : start + 2 * size]
            high, low = split2(level[n + 1])
            corner_block = -dot_pair(dot_exact(level[n], off), high, low)
            if 2 * size < BLOCK:
                top = jnp.concatenate([level[n], corner_block], axis=1)
                bottom = jnp.concatenate([jnp.zeros_like(corner_block), level[n + 1]], axis=1)
                grown.append(jnp.concatenate([top, bottom], axis=0))
            else:
                b = n // 2
                corner_high, corner_low = split2(corner_block)
                first_high, first_low = split2(level[n])
                zero = jnp.zeros((size, size), BF16)
                for ref, first, mixed, second in (
                    (out_high, first_high, corner_high, high),
                    (out_low, first_low, corner_low, low),
                ):
                    ref[b, :size, :size] = first
                    ref[b, :size, size:] = mixed
                    ref[b, size:, :size] = zero
                    ref[b, size:, size:] = second
        level = grown
        size *= 2


def grow(chips, pieces, slab):
    inverse = jax.ShapeDtypeStruct((slab // BLOCK, BLOCK, BLOCK), BF16)
    vmem = pl.BlockSpec(memory_space=pltpu.VMEM)
    return pl.pallas_call(
        grow_kernel,
        out_shape=(inverse, inverse, TOKEN),
        in_specs=[pl.BlockSpec(memory_space=pltpu.SMEM)] + [pl.BlockSpec(memory_space=pl.ANY)] * 4,
        out_specs=[vmem] * 3,
        scratch_shapes=[pltpu.VMEM((slab, slab), BF16), pltpu.SemaphoreType.DMA((2,))],
        compiler_params=pltpu.CompilerParams(vmem_limit_bytes=28 * MB),
        cost_estimate=pl.CostEstimate(flops=4 * 10**9, bytes_accessed=2 * slab * slab, transcendentals=0),
        name="grow_inverse",
    )(chips, *pieces)


def solve_block(blocks, pending, factor, high, low, out, wait, before_update, after):
    for b in range(blocks):
        cols = slice(b * BLOCK, (b + 1) * BLOCK)
        wait(b)
        y = dot_pair(pending[:, cols], high[b], low[b])
        out[: pending.shape[0], cols] = y
        before_update(b)
        if b + 1 < blocks:
            rest = slice((b + 1) * BLOCK, blocks * BLOCK)
            pending[:, rest] = pending[:, rest] - dot_exact(y, factor[cols, rest])
        after(b, y)


def inverse_copies(inv_high, inv_low, high, low, sems):
    return [
        [
            pltpu.make_async_copy(inv_high.at[b], high.at[b], sems.at[0, b]),
            pltpu.make_async_copy(inv_low.at[b], low.at[b], sems.at[1, b]),
        ]
        for b in range(high.shape[0])
    ]


def solve_kernel(first, core, chips, right, *refs):
    dense = refs[: 0 if first else 2]
    pieces = refs[len(dense) : len(dense) + 4]
    inv_high, inv_low, out, factor, under, high, low, pending, sems, strip_sems = refs[len(dense) + 4 :]
    rows, slab = right.shape
    half = slab // 2
    inner = half // BLOCK
    active = (core[0] == 0) if first else (core[0] != 0)

    @pl.when(active)
    def _():
        even, odd, below = strip_copies(chips, pieces, factor, under, strip_sems)
        inverse = inverse_copies(inv_high, inv_low, high, low, sems)
        order = [inverse[0], even, *inverse[1:], odd, below] if first else [below, *inverse, even, odd]
        for copies in order:
            start_all(copies)
        if first:
            pending[...] = right[...]
        else:
            own, other = dense
            pending[...] = right[...] - other[rows:, :]
            wait_for(under, strip_sems.at[2])
            pending[...] = pending[...] - dot_exact(other[:rows, half:], under[...])

        def wait(b):
            for copy in inverse[b]:
                copy.wait()

        def after(b, y):
            if first and b + 1 == inner:
                wait_for(under, strip_sems.at[2])
                out[rows:, :] = dot_exact(out[:rows, :half], under[...])

        def before_update(b):
            if b == 0:
                wait_for(factor.at[:half], strip_sems.at[0])
            if b == inner:
                wait_for(factor.at[half:], strip_sems.at[1])

        solve_block(slab // BLOCK, pending, factor, high, low, out, wait, before_update, after)

    @pl.when(jnp.logical_not(active))
    def _():
        out[...] = jnp.zeros_like(out) if first else dense[0][:rows, :]


def solve_call(first, core, chips, dense, pieces, inverses, name):
    rows, slab = dense[0].shape
    blocks = slab // BLOCK
    vmem = pl.BlockSpec(memory_space=pltpu.VMEM)
    smem = pl.BlockSpec(memory_space=pltpu.SMEM)
    return pl.pallas_call(
        functools.partial(solve_kernel, first),
        out_shape=jax.ShapeDtypeStruct((2 * rows if first else rows, slab), F32),
        in_specs=[smem, smem] + [vmem] * len(dense) + [pl.BlockSpec(memory_space=pl.ANY)] * 6,
        out_specs=vmem,
        scratch_shapes=[
            pltpu.VMEM((slab, slab), BF16),
            pltpu.VMEM((slab // 2, slab), BF16),
            pltpu.VMEM((blocks, BLOCK, BLOCK), BF16),
            pltpu.VMEM((blocks, BLOCK, BLOCK), BF16),
            pltpu.VMEM((rows, slab), F32),
            pltpu.SemaphoreType.DMA((2, blocks)),
            pltpu.SemaphoreType.DMA((3,)),
        ],
        compiler_params=pltpu.CompilerParams(vmem_limit_bytes=36 * MB),
        name=name,
    )(core, chips, *dense, *pieces, *inverses)


def product_kernel(parts, half, order, left, right, _, *refs):
    outs, token, (a, b, picked, a_sems, b_sems) = refs[: len(parts)], refs[len(parts)], refs[len(parts) + 1 :]
    token[...] = jnp.zeros_like(token)
    groups, _, depth = left.shape
    rows = picked.shape[0]
    slab = rows // 2
    step = b.shape[1]
    spans = [(n, col) for n in range(len(parts)) for col in range(0, parts[n][2], step)]
    lanes = [pl.ds(g * depth, depth) for g in range(groups)]

    def slabs(n):
        copies = []
        for h in range(2):
            block = order[(2 * parts[n][0] + half) * (rows // ROWS) + h * (slab // ROWS)]
            source = pl.ds(pl.multiple_of(block // (slab // ROWS) * slab, slab), slab)
            for g in range(groups):
                copies.append(
                    pltpu.make_async_copy(
                        left.at[g, source], a.at[pl.ds(h * slab, slab), lanes[g]], a_sems.at[h, g]
                    )
                )
        return copies

    loads = slabs(0)
    for copy in loads:
        copy.start()
    tiles = []
    for t, (n, col) in enumerate(spans):
        tile = [
            pltpu.make_async_copy(
                right.at[g, pl.ds(parts[n][1] + col, step)], b.at[t, :, lanes[g]], b_sems.at[t, g]
            )
            for g in range(groups)
        ]
        for copy in tile:
            copy.start()
        tiles.append(tile)
    for copy in loads:
        copy.wait()
    for t, (n, col) in enumerate(spans):
        if col == 0:
            base = (2 * parts[n][0] + half) * (rows // ROWS)
            for r in range(rows // ROWS):
                inside = order[base + r] % (slab // ROWS) + r // (slab // ROWS) * (slab // ROWS)
                source = pl.ds(pl.multiple_of(inside * ROWS, ROWS), ROWS)
                picked[r * ROWS : (r + 1) * ROWS, :] = a[source, :]
        for copy in tiles[t]:
            copy.wait()
        outs[n][:, col : col + step] = lax.dot_general(
            picked[...], b[t], (((1,), (1,)), ((), ())), preferred_element_type=F32
        )


def product(order, left, right, token, parts, half, name):
    groups, rows, depth = left.shape
    width = sum(part[2] for part in parts)
    step = parts[0][2]
    return pl.pallas_call(
        functools.partial(product_kernel, parts, half),
        out_shape=[jax.ShapeDtypeStruct((rows // 2, part[2]), F32) for part in parts] + [TOKEN],
        in_specs=[pl.BlockSpec(memory_space=pltpu.SMEM)]
        + [pl.BlockSpec(memory_space=pltpu.HBM)] * 2
        + [pl.BlockSpec(memory_space=pltpu.VMEM)],
        out_specs=[pl.BlockSpec(memory_space=pltpu.VMEM)] * (len(parts) + 1),
        scratch_shapes=[
            pltpu.VMEM((rows // 2, groups * depth), BF16),
            pltpu.VMEM((width // step, step, groups * depth), BF16),
            pltpu.VMEM((rows // 2, groups * depth), BF16),
            pltpu.SemaphoreType.DMA((2, groups)),
            pltpu.SemaphoreType.DMA((width // step, groups)),
        ],
        compiler_params=pltpu.CompilerParams(vmem_limit_bytes=56 * MB),
        cost_estimate=pl.CostEstimate(
            flops=groups * rows * width * depth,
            bytes_accessed=2 * groups * (rows // 2 + width) * depth + 2 * rows * width,
            transcendentals=0,
        ),
        name=name,
    )(order, left, right, token)


def chip_index(z, y, x, c):
    return ((z * SIDE + y) * SIDE + x) * 2 + c


def flip_pairs(axis, masks):
    pairs = []
    for z, y, x, c in np.ndindex(SIDE, SIDE, SIDE, 2):
        place = {"z": z, "y": y, "x": x}
        place[axis] ^= masks[c]
        pairs.append((chip_index(z, y, x, c), chip_index(place["z"], place["y"], place["x"], c)))
    return pairs


def partner_pairs(axis, second):
    return flip_pairs(axis, (3, 1) if second else (1, 3))


def block_order(axes, place, core):
    flip = jnp.where(core == 0, 1, 3)
    masks = jnp.stack([jnp.full_like(flip, 2), flip, flip ^ 2, jnp.zeros_like(flip)])
    lists = {name: place[name] ^ masks for name in AXES}
    shape = {name: [1, 1, 1] for name in AXES}
    for position, name in enumerate(axes):
        shape[name][position] = SIDE
    at = {name: lists[name].reshape(shape[name]) for name in AXES}
    return (((at["z"] * SIDE + at["y"]) * SIDE + at["x"]).reshape(-1)).astype(jnp.int32)


def pair_kernel(flags, strip, got, both, token):
    token[...] = jnp.zeros_like(token)
    both[:STRIP] = strip[...]
    both[STRIP:] = jnp.where(flags[0] > 0, strip[...], got[...])


def choose_kernel(flags, held, got, _, both, token):
    token[...] = jnp.zeros_like(token)
    both[:STRIP] = jnp.where(flags[1] > 0, held[:STRIP], got[:STRIP])
    both[STRIP:] = jnp.where(flags[2] > 0, held[STRIP:], got[STRIP:])


def pack_kernel(flags, held, got, _, out_a, out_b, token, odd):
    token[...] = jnp.zeros_like(token)
    mine = flags[3] > 0
    width = held.shape[1]
    cut = STRIP // 2
    even = out_a.at[:STRIP]
    even[...] = jnp.where(mine, held[:STRIP], got[:STRIP])
    odd[...] = jnp.where(mine, got[:STRIP], held[:STRIP])
    out_b[cut:] = jnp.where(mine, held[STRIP:], got[STRIP:])

    at = pl.multiple_of(flags[4] * 128, 128)
    turn = flags[5] > 0
    one = even[:, pl.ds(at, 128)].astype(F32)
    two = odd[:, pl.ds(pl.multiple_of(at + width // 2, 128), 128)].astype(F32)
    one = jnp.where(turn, pltpu.roll(one, STRIP, 1), one)
    two = jnp.where(turn, two, pltpu.roll(two, STRIP, 1))
    rows = lax.broadcasted_iota(jnp.int32, (STRIP, 128), 0)
    lanes = lax.broadcasted_iota(jnp.int32, (STRIP, 128), 1)
    left = lanes < STRIP
    inner = jnp.where(left, lanes, lanes - STRIP)
    block = jnp.where(left, one, two)
    diagonal = jnp.where(inner == rows, block, 0.0)
    scale = jnp.where(
        left,
        1.0 / jnp.sum(jnp.where(left, diagonal, 0.0), axis=1, keepdims=True),
        1.0 / jnp.sum(jnp.where(left, 0.0, diagonal), axis=1, keepdims=True),
    )
    upper = jnp.where(inner > rows, block, 0.0)
    todo = jnp.where(inner == rows, 1.0, 0.0)
    for k in range(STRIP - 1, 0, -1):
        row = todo[k : k + 1, :] * scale[k : k + 1, :]
        col = jnp.where(left, upper[:, k : k + 1], upper[:, STRIP + k : STRIP + k + 1])
        todo = todo - col * row
    high, low = split2(todo * scale)
    odd[:, :128] = high
    odd[:, 128:256] = low
    out_a[STRIP:] = odd[:cut]
    out_b[:cut] = odd[cut:]


def small_call(kernel, name, shapes, scratch, flags, *operands, token=None):
    vmem = pl.BlockSpec(memory_space=pltpu.VMEM)
    tokens = () if token is None else (token,)
    return pl.pallas_call(
        kernel,
        out_shape=[jax.ShapeDtypeStruct(shape, BF16) for shape in shapes] + [TOKEN],
        in_specs=[pl.BlockSpec(memory_space=pltpu.SMEM)]
        + [vmem] * (len(operands) + len(tokens)),
        out_specs=[vmem] * (len(shapes) + 1),
        scratch_shapes=scratch,
        compiler_params=pltpu.CompilerParams(vmem_limit_bytes=16 * MB),
        name=name,
    )(flags, *operands, *tokens)


def join_kernel(held_a, got_a, held_b, got_b, _, out_a, out_b, token, sems):
    copies = []
    for n, (held, got, out) in enumerate(((held_a, got_a, out_a), (held_b, got_b, out_b))):
        rows = held.shape[0]
        copies.append(pltpu.make_async_copy(held, out.at[pl.ds(0, rows)], sems.at[n, 0]))
        copies.append(pltpu.make_async_copy(got, out.at[pl.ds(rows, rows)], sems.at[n, 1]))
    start_all(copies)
    token[...] = jnp.zeros_like(token)
    for copy in copies:
        copy.wait()


def join(held, got, token):
    rows, width = held[0].shape
    shape = jax.ShapeDtypeStruct((2 * rows, width), BF16)
    anywhere = pl.BlockSpec(memory_space=pl.ANY)
    *joined, token = pl.pallas_call(
        join_kernel,
        out_shape=[shape, shape, TOKEN],
        in_specs=[anywhere] * 4 + [pl.BlockSpec(memory_space=pltpu.VMEM)],
        out_specs=[anywhere] * 2 + [pl.BlockSpec(memory_space=pltpu.VMEM)],
        scratch_shapes=[pltpu.SemaphoreType.DMA((2, 2))],
        compiler_params=pltpu.CompilerParams(vmem_limit_bytes=4 * MB),
        name="join",
    )(held[0], got[0], held[1], got[1], token)
    return joined, token


def add_kernel(keep, got, _, send, kept, token):
    token[...] = jnp.zeros_like(token)
    middle = send.shape[0]
    send[...] = keep[:middle] + got[:middle]
    kept[...] = keep[middle:] + got[middle:]


def add(keep, got, token):
    vmem = pl.BlockSpec(memory_space=pltpu.VMEM)
    shape = jax.ShapeDtypeStruct((keep.shape[0] // 2, keep.shape[1]), F32)
    return pl.pallas_call(
        add_kernel,
        out_shape=[shape, shape, TOKEN],
        in_specs=[vmem] * 3,
        out_specs=[vmem] * 3,
        compiler_params=pltpu.CompilerParams(vmem_limit_bytes=16 * MB),
        name="add",
    )(keep, got, token)


def gather_order(place, core):
    flip = jnp.where(core == 0, 1, 3)
    masks = jnp.stack([jnp.zeros_like(flip), flip, flip ^ 2, jnp.full_like(flip, 2)])
    ys, xs = place["y"] ^ masks, place["x"] ^ masks
    chips = [
        ys[None, :] * SIDE + xs[:, None],
        ys[:, None] * SIDE + xs[None, :],
    ]
    return jnp.concatenate([c.reshape(-1) for c in chips]).astype(jnp.int32)


def per_device(hist_factor, hist_solution, diag_factor, samples):
    slab = hist_factor.shape[1]
    core = lax.axis_index("pcol")
    place = {name: lax.axis_index(name) for name in AXES}
    core_arg = core.astype(jnp.int32).reshape(1)

    order = jnp.concatenate([block_order(axes, place, core) for _, _, axes in PARTS])
    parts = [(n, start, width) for n, (start, width, _) in enumerate(PARTS)]
    z = place["z"]
    at = place["y"] * SIDE + place["x"]
    outer = (z == 0) | (z == 3)
    flags = jnp.stack(
        [core > 0, (z < 2) == (core == 0), z < 2, outer == (core == 0), at // 2, at % 2]
    ).astype(jnp.int32)
    chips = gather_order(place, core)
    strip = diag_factor.T
    width = strip.shape[1]

    to_first = [
        (chip_index(0, y, x, 1), chip_index(0, y, x, 0)) for y in range(SIDE) for x in range(SIDE)
    ]
    def half_product(n, half, token, name):
        return product(order, hist_solution, hist_factor, token, parts[n : n + 1], half, name)

    def gather_step(held, step):
        return [
            lax.ppermute(held[n], EVERY, partner_pairs(GATHER[n][step // 2], step % 2 == 1))
            for n in range(2)
        ]

    def sum_step(n, send, step):
        return lax.ppermute(send, EVERY, partner_pairs(PARTS[n][2][step // 2], step % 2 == 1))

    got = lax.ppermute(strip, EVERY, to_first)
    held, token = small_call(pair_kernel, "pair", [(2 * STRIP, width)], [], flags, strip, got)
    got = lax.ppermute(held, EVERY, flip_pairs("z", (3, 3)))
    send0, token = half_product(0, 0, token, "send0")
    held, token = small_call(
        choose_kernel, "choose", [(2 * STRIP, width)], [], flags, held, got, token=token
    )
    got = lax.ppermute(held, EVERY, flip_pairs("z", (1, 1)))
    come = [sum_step(0, send0, 0), None]
    send1, token = half_product(1, 0, token, "send1")
    share = STRIP + STRIP // 2
    *held, token = small_call(
        pack_kernel,
        "pack",
        [(share, width)] * 2,
        [pltpu.VMEM((STRIP, width), BF16)],
        flags,
        held,
        got,
        token=token,
    )
    come[1] = sum_step(1, send1, 0)
    got = gather_step(held, 0)
    held, token = join(held, got, token)
    got = gather_step(held, 1)
    keep0, token = half_product(0, 1, token, "keep0")
    held, token = join(held, got, token)
    got = gather_step(held, 2)
    keep1, token = half_product(1, 1, token, "keep1")
    send0, keep0, token = add(keep0, come[0], token)
    come[0] = sum_step(0, send0, 1)
    held, token = join(held, got, token)
    got = gather_step(held, 3)
    send1, keep1, token = add(keep1, come[1], token)
    come[1] = sum_step(1, send1, 1)
    pieces = [held[0], got[0], held[1], got[1]]
    *inverses, token = grow(chips, pieces, slab)
    keeps = [keep0, keep1]
    for step in range(1, 5):
        for n in range(2):
            if step == 4:
                send, keeps[n], _ = add(keeps[n], come[n], token)
            else:
                middle = keeps[n].shape[0] // 2
                send = keeps[n][:middle] + come[n][:middle]
                keeps[n] = keeps[n][middle:] + come[n][middle:]
            come[n] = sum_step(n, send, step + 1)
    history = jnp.concatenate([keeps[n] + come[n] for n in range(2)], axis=1)
    pending = samples.astype(F32) - history

    first = solve_call(True, core_arg, chips, (pending,), pieces, inverses, "solve0")
    other = lax.ppermute(first, "pcol", [(0, 1)])
    return solve_call(False, core_arg, chips, (pending, first, other), pieces, inverses, "solve1")


def solution(mesh):
    cube = Mesh(mesh.devices.reshape(SIDE, SIDE, SIDE, 2), EVERY)
    return jax.shard_map(
        per_device,
        mesh=cube,
        in_specs=(
            P(None, "pcol", AXES),
            P(None, None, AXES),
            P("pcol", AXES),
            P(AXES, "pcol"),
        ),
        out_specs=P(AXES, "pcol"),
        check_vma=False,
    )
```

```python
import functools

import jax
import jax.numpy as jnp
import numpy as np
from jax import lax
from jax.experimental import pallas as pl
from jax.experimental.pallas import tpu as pltpu
from jax.sharding import Mesh
from jax.sharding import PartitionSpec as P

F32 = jnp.float32
BF16 = jnp.bfloat16
SIDE = 4
ROWS = 16
STRIP = 64
BLOCK = 512
AXES = ("z", "y", "x")
EVERY = ("z", "y", "x", "pcol")
PARTS = ((0, 1024, "zyx"), (1024, 1024, "zxy"))
GATHER = ("yx", "xy")
MB = 1 << 20
TOKEN = jax.ShapeDtypeStruct((8, 128), F32)


def split2(value):
    high = value.astype(BF16)
    return high, (value - high.astype(F32)).astype(BF16)


def dot(a, b):
    return jnp.dot(a, b, preferred_element_type=F32)


def dot_exact(a, b):
    high, low = split2(a)
    rows = a.shape[0]
    both = dot(jnp.concatenate([high, low], axis=0), b)
    return both[:rows] + both[rows:]


def dot_pair(a, b_high, b_low):
    high, low = split2(a)
    rows = a.shape[0]
    both = dot(jnp.concatenate([high, low], axis=0), b_high)
    return both[:rows] + both[rows:] + dot(high, b_low)


def strip_copies(chips, pieces, lower, below, sems):
    own_a, got_a, own_b, got_b = pieces
    half = lower.shape[0] // 2
    cut = STRIP // 2
    groups = ([], [], [])

    def add(group, source, start, count, target, to):
        groups[group].append(
            pltpu.make_async_copy(
                source.at[pl.ds(start, count)],
                target.at[pl.ds(pl.multiple_of(to, cut), count)],
                sems.at[group],
            )
        )

    for position in range(16):
        base = (position % 8) * (STRIP + cut)
        row = pl.multiple_of(chips[position] * STRIP, STRIP)
        source = own_a if position < 8 else got_a
        add(0, source, base, STRIP, lower, row)
        add(1, source, base + STRIP, cut, lower, half + row)
        row = pl.multiple_of(chips[16 + position] * STRIP, STRIP)
        source = own_b if position < 8 else got_b
        add(1, source, base, cut, lower, half + row + cut)
        if below is not None:
            add(2, source, base + cut, STRIP, below, row)
    return groups


def start_all(copies):
    for copy in copies:
        copy.start()


def wait_for(target, sem):
    pltpu.make_async_copy(target, target, sem).wait()


def grow_kernel(chips, own_a, got_a, own_b, got_b, out_high, out_low, token, lower, sems):
    slab = lower.shape[0]
    half = slab // 2
    even, odd, _ = strip_copies(chips, (own_a, got_a, own_b, got_b), lower, None, sems)
    start_all(even)
    start_all(odd)
    del token
    wait_for(lower.at[:half], sems.at[0])
    wait_for(lower.at[half:], sems.at[1])

    rows = lax.broadcasted_iota(jnp.int32, (128, 128), 0)
    lanes = lax.broadcasted_iota(jnp.int32, (128, 128), 1)
    corner = (rows < STRIP) & (lanes >= STRIP)
    same = (rows < STRIP) == (lanes < STRIP)
    upright, turned = [], []
    for k in range(half // 128):
        rng = slice(half + k * 128, half + k * 128 + 128)
        pair = lower[rng, :128].astype(F32) + lower[rng, 128:256].astype(F32)
        swapped = pltpu.roll(pair, STRIP, 1)
        upright.append(jnp.where(same, jnp.where(rows < STRIP, pair, swapped), 0.0))
        turned.append(jnp.where(same, jnp.where(rows < STRIP, swapped, pair), 0.0))
    level = []
    for k, both in enumerate(upright + turned):
        rng = slice(k * 128, k * 128 + 128)
        off = jnp.where(corner, lower[rng, rng].astype(F32), 0.0).astype(BF16)
        level.append(both - dot_pair(dot_exact(both, off), *split2(both)))
    size = 128
    while size < BLOCK:
        grown = []
        for n in range(0, len(level), 2):
            start = n * size
            off = lower[start : start + size, start + size : start + 2 * size]
            high, low = split2(level[n + 1])
            corner_block = -dot_pair(dot_exact(level[n], off), high, low)
            if 2 * size < BLOCK:
                top = jnp.concatenate([level[n], corner_block], axis=1)
                bottom = jnp.concatenate([jnp.zeros_like(corner_block), level[n + 1]], axis=1)
                grown.append(jnp.concatenate([top, bottom], axis=0))
            else:
                b = n // 2
                corner_high, corner_low = split2(corner_block)
                first_high, first_low = split2(level[n])
                zero = jnp.zeros((size, size), BF16)
                for ref, first, mixed, second in (
                    (out_high, first_high, corner_high, high),
                    (out_low, first_low, corner_low, low),
                ):
                    ref[b, :size, :size] = first
                    ref[b, :size, size:] = mixed
                    ref[b, size:, :size] = zero
                    ref[b, size:, size:] = second
        level = grown
        size *= 2


def grow(chips, pieces, slab):
    inverse = jax.ShapeDtypeStruct((slab // BLOCK, BLOCK, BLOCK), BF16)
    vmem = pl.BlockSpec(memory_space=pltpu.VMEM)
    return pl.pallas_call(
        grow_kernel,
        out_shape=(inverse, inverse, TOKEN),
        in_specs=[pl.BlockSpec(memory_space=pltpu.SMEM)] + [pl.BlockSpec(memory_space=pl.ANY)] * 4,
        out_specs=[vmem] * 2 + [pl.BlockSpec(memory_space=pltpu.HBM)],
        scratch_shapes=[pltpu.VMEM((slab, slab), BF16), pltpu.SemaphoreType.DMA((2,))],
        compiler_params=pltpu.CompilerParams(vmem_limit_bytes=28 * MB),
        cost_estimate=pl.CostEstimate(flops=4 * 10**9, bytes_accessed=2 * slab * slab, transcendentals=0),
        name="grow_inverse",
    )(chips, *pieces)


def solve_block(blocks, pending, factor, high, low, out, wait, before_update, after):
    for b in range(blocks):
        cols = slice(b * BLOCK, (b + 1) * BLOCK)
        wait(b)
        y = dot_pair(pending[:, cols], high[b], low[b])
        out[: pending.shape[0], cols] = y
        before_update(b)
        if b + 1 < blocks:
            rest = slice((b + 1) * BLOCK, blocks * BLOCK)
            pending[:, rest] = pending[:, rest] - dot_exact(y, factor[cols, rest])
        after(b, y)


def inverse_copies(inv_high, inv_low, high, low, sems):
    return [
        [
            pltpu.make_async_copy(inv_high.at[b], high.at[b], sems.at[0, b]),
            pltpu.make_async_copy(inv_low.at[b], low.at[b], sems.at[1, b]),
        ]
        for b in range(high.shape[0])
    ]


def solve_kernel(first, core, chips, right, *refs):
    dense = refs[: 0 if first else 2]
    pieces = refs[len(dense) : len(dense) + 4]
    inv_high, inv_low, out, factor, under, high, low, pending, sems, strip_sems = refs[len(dense) + 4 :]
    rows, slab = right.shape
    half = slab // 2
    inner = half // BLOCK
    active = (core[0] == 0) if first else (core[0] != 0)

    @pl.when(active)
    def _():
        even, odd, below = strip_copies(chips, pieces, factor, under, strip_sems)
        inverse = inverse_copies(inv_high, inv_low, high, low, sems)
        order = [inverse[0], even, *inverse[1:], odd, below] if first else [below, *inverse, even, odd]
        for copies in order:
            start_all(copies)
        if first:
            pending[...] = right[...]
        else:
            own, other = dense
            pending[...] = right[...] - other[rows:, :]
            wait_for(under, strip_sems.at[2])
            pending[...] = pending[...] - dot_exact(other[:rows, half:], under[...])

        def wait(b):
            for copy in inverse[b]:
                copy.wait()

        def after(b, y):
            if first and b + 1 == inner:
                wait_for(under, strip_sems.at[2])
                out[rows:, :] = dot_exact(out[:rows, :half], under[...])

        def before_update(b):
            if b == 0:
                wait_for(factor.at[:half], strip_sems.at[0])
            if b == inner:
                wait_for(factor.at[half:], strip_sems.at[1])

        solve_block(slab // BLOCK, pending, factor, high, low, out, wait, before_update, after)

    @pl.when(jnp.logical_not(active))
    def _():
        out[...] = jnp.zeros_like(out) if first else dense[0][:rows, :]


def solve_call(first, core, chips, dense, pieces, inverses, name):
    rows, slab = dense[0].shape
    blocks = slab // BLOCK
    vmem = pl.BlockSpec(memory_space=pltpu.VMEM)
    smem = pl.BlockSpec(memory_space=pltpu.SMEM)
    return pl.pallas_call(
        functools.partial(solve_kernel, first),
        out_shape=jax.ShapeDtypeStruct((2 * rows if first else rows, slab), F32),
        in_specs=[smem, smem] + [vmem] * len(dense) + [pl.BlockSpec(memory_space=pl.ANY)] * 6,
        out_specs=vmem,
        scratch_shapes=[
            pltpu.VMEM((slab, slab), BF16),
            pltpu.VMEM((slab // 2, slab), BF16),
            pltpu.VMEM((blocks, BLOCK, BLOCK), BF16),
            pltpu.VMEM((blocks, BLOCK, BLOCK), BF16),
            pltpu.VMEM((rows, slab), F32),
            pltpu.SemaphoreType.DMA((2, blocks)),
            pltpu.SemaphoreType.DMA((3,)),
        ],
        compiler_params=pltpu.CompilerParams(vmem_limit_bytes=36 * MB),
        name=name,
    )(core, chips, *dense, *pieces, *inverses)


def product_kernel(parts, half, order, left, right, _, *refs):
    outs, token, (a, b, picked, a_sems, b_sems) = refs[: len(parts)], refs[len(parts)], refs[len(parts) + 1 :]
    del token
    groups, _, depth = left.shape
    rows = picked.shape[0]
    slab = rows // 2
    step = b.shape[1]
    spans = [(n, col) for n in range(len(parts)) for col in range(0, parts[n][2], step)]
    lanes = [pl.ds(g * depth, depth) for g in range(groups)]

    def slabs(n):
        copies = []
        for h in range(2):
            block = order[(2 * parts[n][0] + half) * (rows // ROWS) + h * (slab // ROWS)]
            source = pl.ds(pl.multiple_of(block // (slab // ROWS) * slab, slab), slab)
            for g in range(groups):
                copies.append(
                    pltpu.make_async_copy(
                        left.at[g, source], a.at[pl.ds(h * slab, slab), lanes[g]], a_sems.at[h, g]
                    )
                )
        return copies

    loads = slabs(0)
    for copy in loads:
        copy.start()
    tiles = []
    for t, (n, col) in enumerate(spans):
        tile = [
            pltpu.make_async_copy(
                right.at[g, pl.ds(parts[n][1] + col, step)], b.at[t, :, lanes[g]], b_sems.at[t, g]
            )
            for g in range(groups)
        ]
        for copy in tile:
            copy.start()
        tiles.append(tile)
    for copy in loads:
        copy.wait()
    for t, (n, col) in enumerate(spans):
        if col == 0:
            base = (2 * parts[n][0] + half) * (rows // ROWS)
            for r in range(rows // ROWS):
                inside = order[base + r] % (slab // ROWS) + r // (slab // ROWS) * (slab // ROWS)
                source = pl.ds(pl.multiple_of(inside * ROWS, ROWS), ROWS)
                picked[r * ROWS : (r + 1) * ROWS, :] = a[source, :]
        for copy in tiles[t]:
            copy.wait()
        outs[n][:, col : col + step] = lax.dot_general(
            picked[...], b[t], (((1,), (1,)), ((), ())), preferred_element_type=F32
        )


def product(order, left, right, token, parts, half, name):
    groups, rows, depth = left.shape
    width = sum(part[2] for part in parts)
    step = parts[0][2]
    return pl.pallas_call(
        functools.partial(product_kernel, parts, half),
        out_shape=[jax.ShapeDtypeStruct((rows // 2, part[2]), F32) for part in parts] + [TOKEN],
        in_specs=[pl.BlockSpec(memory_space=pltpu.SMEM)]
        + [pl.BlockSpec(memory_space=pltpu.HBM)] * 3,
        out_specs=[pl.BlockSpec(memory_space=pltpu.VMEM)] * len(parts)
        + [pl.BlockSpec(memory_space=pltpu.HBM)],
        scratch_shapes=[
            pltpu.VMEM((rows // 2, groups * depth), BF16),
            pltpu.VMEM((width // step, step, groups * depth), BF16),
            pltpu.VMEM((rows // 2, groups * depth), BF16),
            pltpu.SemaphoreType.DMA((2, groups)),
            pltpu.SemaphoreType.DMA((width // step, groups)),
        ],
        compiler_params=pltpu.CompilerParams(vmem_limit_bytes=48 * MB),
        cost_estimate=pl.CostEstimate(
            flops=groups * rows * width * depth,
            bytes_accessed=2 * groups * (rows // 2 + width) * depth + 2 * rows * width,
            transcendentals=0,
        ),
        name=name,
    )(order, left, right, token)


def chip_index(z, y, x, c):
    return ((z * SIDE + y) * SIDE + x) * 2 + c


def flip_pairs(axis, masks):
    pairs = []
    for z, y, x, c in np.ndindex(SIDE, SIDE, SIDE, 2):
        place = {"z": z, "y": y, "x": x}
        place[axis] ^= masks[c]
        pairs.append((chip_index(z, y, x, c), chip_index(place["z"], place["y"], place["x"], c)))
    return pairs


def partner_pairs(axis, second):
    return flip_pairs(axis, (3, 1) if second else (1, 3))


def block_order(axes, place, core):
    flip = jnp.where(core == 0, 1, 3)
    masks = jnp.stack([jnp.full_like(flip, 2), flip, flip ^ 2, jnp.zeros_like(flip)])
    lists = {name: place[name] ^ masks for name in AXES}
    shape = {name: [1, 1, 1] for name in AXES}
    for position, name in enumerate(axes):
        shape[name][position] = SIDE
    at = {name: lists[name].reshape(shape[name]) for name in AXES}
    return (((at["z"] * SIDE + at["y"]) * SIDE + at["x"]).reshape(-1)).astype(jnp.int32)


def pair_kernel(flags, strip, got, both, token):
    del token
    both[:STRIP] = strip[...]
    both[STRIP:] = jnp.where(flags[0] > 0, strip[...], got[...])


def choose_kernel(flags, held, got, _, both, token):
    del token
    both[:STRIP] = jnp.where(flags[1] > 0, held[:STRIP], got[:STRIP])
    both[STRIP:] = jnp.where(flags[2] > 0, held[STRIP:], got[STRIP:])


def pack_kernel(flags, held, got, _, out_a, out_b, token, odd):
    del token
    mine = flags[3] > 0
    width = held.shape[1]
    cut = STRIP // 2
    even = out_a.at[:STRIP]
    even[...] = jnp.where(mine, held[:STRIP], got[:STRIP])
    odd[...] = jnp.where(mine, got[:STRIP], held[:STRIP])
    out_b[cut:] = jnp.where(mine, held[STRIP:], got[STRIP:])

    at = pl.multiple_of(flags[4] * 128, 128)
    turn = flags[5] > 0
    one = even[:, pl.ds(at, 128)].astype(F32)
    two = odd[:, pl.ds(pl.multiple_of(at + width // 2, 128), 128)].astype(F32)
    one = jnp.where(turn, pltpu.roll(one, STRIP, 1), one)
    two = jnp.where(turn, two, pltpu.roll(two, STRIP, 1))
    rows = lax.broadcasted_iota(jnp.int32, (STRIP, 128), 0)
    lanes = lax.broadcasted_iota(jnp.int32, (STRIP, 128), 1)
    left = lanes < STRIP
    inner = jnp.where(left, lanes, lanes - STRIP)
    block = jnp.where(left, one, two)
    diagonal = jnp.where(inner == rows, block, 0.0)
    scale = jnp.where(
        left,
        1.0 / jnp.sum(jnp.where(left, diagonal, 0.0), axis=1, keepdims=True),
        1.0 / jnp.sum(jnp.where(left, 0.0, diagonal), axis=1, keepdims=True),
    )
    upper = jnp.where(inner > rows, block, 0.0)
    todo = jnp.where(inner == rows, 1.0, 0.0)
    for k in range(STRIP - 1, 0, -1):
        row = todo[k : k + 1, :] * scale[k : k + 1, :]
        col = jnp.where(left, upper[:, k : k + 1], upper[:, STRIP + k : STRIP + k + 1])
        todo = todo - col * row
    high, low = split2(todo * scale)
    odd[:, :128] = high
    odd[:, 128:256] = low
    out_a[STRIP:] = odd[:cut]
    out_b[:cut] = odd[cut:]


def small_call(kernel, name, shapes, scratch, flags, *operands, token=None):
    vmem = pl.BlockSpec(memory_space=pltpu.VMEM)
    hbm = pl.BlockSpec(memory_space=pltpu.HBM)
    tokens = () if token is None else (token,)
    return pl.pallas_call(
        kernel,
        out_shape=[jax.ShapeDtypeStruct(shape, BF16) for shape in shapes] + [TOKEN],
        in_specs=[pl.BlockSpec(memory_space=pltpu.SMEM)]
        + [vmem] * len(operands)
        + [hbm] * len(tokens),
        out_specs=[vmem] * len(shapes) + [hbm],
        scratch_shapes=scratch,
        compiler_params=pltpu.CompilerParams(vmem_limit_bytes=16 * MB),
        name=name,
    )(flags, *operands, *tokens)


def join_kernel(held_a, got_a, held_b, got_b, _, out_a, out_b, token, stage, in_sems, out_sems):
    del token
    loads, stores = [], []
    for n, (held, got, out) in enumerate(((held_a, got_a, out_a), (held_b, got_b, out_b))):
        rows = held.shape[0]
        for h, source in enumerate((held, got)):
            place = pl.ds(h * rows, rows)
            loads.append(pltpu.make_async_copy(source, stage.at[n, place], in_sems.at[n, h]))
            stores.append(pltpu.make_async_copy(stage.at[n, place], out.at[place], out_sems.at[n, h]))
    start_all(loads)
    for load, store in zip(loads, stores):
        load.wait()
        store.start()
    for store in stores:
        store.wait()


def join(held, got, token):
    rows, width = held[0].shape
    shape = jax.ShapeDtypeStruct((2 * rows, width), BF16)
    hbm = pl.BlockSpec(memory_space=pltpu.HBM)
    *joined, token = pl.pallas_call(
        join_kernel,
        out_shape=[shape, shape, TOKEN],
        in_specs=[pl.BlockSpec(memory_space=pl.ANY)] * 4 + [hbm],
        out_specs=[hbm] * 3,
        scratch_shapes=[
            pltpu.VMEM((2, 2 * rows, width), BF16),
            pltpu.SemaphoreType.DMA((2, 2)),
            pltpu.SemaphoreType.DMA((2, 2)),
        ],
        compiler_params=pltpu.CompilerParams(vmem_limit_bytes=12 * MB),
        name="join",
    )(held[0], got[0], held[1], got[1], token)
    return joined, token


def add_kernel(keep, got, _, send, kept, token):
    del token
    middle = send.shape[0]
    send[...] = keep[:middle] + got[:middle]
    kept[...] = keep[middle:] + got[middle:]


def add(keep, got, token):
    vmem = pl.BlockSpec(memory_space=pltpu.VMEM)
    hbm = pl.BlockSpec(memory_space=pltpu.HBM)
    shape = jax.ShapeDtypeStruct((keep.shape[0] // 2, keep.shape[1]), F32)
    return pl.pallas_call(
        add_kernel,
        out_shape=[shape, shape, TOKEN],
        in_specs=[vmem, vmem, hbm],
        out_specs=[vmem, vmem, hbm],
        compiler_params=pltpu.CompilerParams(vmem_limit_bytes=16 * MB),
        name="add",
    )(keep, got, token)


def gather_order(place, core):
    flip = jnp.where(core == 0, 1, 3)
    masks = jnp.stack([jnp.zeros_like(flip), flip, flip ^ 2, jnp.full_like(flip, 2)])
    ys, xs = place["y"] ^ masks, place["x"] ^ masks
    chips = [
        ys[None, :] * SIDE + xs[:, None],
        ys[:, None] * SIDE + xs[None, :],
    ]
    return jnp.concatenate([c.reshape(-1) for c in chips]).astype(jnp.int32)


def per_device(hist_factor, hist_solution, diag_factor, samples):
    slab = hist_factor.shape[1]
    core = lax.axis_index("pcol")
    place = {name: lax.axis_index(name) for name in AXES}
    core_arg = core.astype(jnp.int32).reshape(1)

    order = jnp.concatenate([block_order(axes, place, core) for _, _, axes in PARTS])
    parts = [(n, start, width) for n, (start, width, _) in enumerate(PARTS)]
    z = place["z"]
    at = place["y"] * SIDE + place["x"]
    outer = (z == 0) | (z == 3)
    flags = jnp.stack(
        [core > 0, (z < 2) == (core == 0), z < 2, outer == (core == 0), at // 2, at % 2]
    ).astype(jnp.int32)
    chips = gather_order(place, core)
    strip = diag_factor.T
    width = strip.shape[1]

    to_first = [
        (chip_index(0, y, x, 1), chip_index(0, y, x, 0)) for y in range(SIDE) for x in range(SIDE)
    ]
    def half_product(n, half, token, name):
        return product(order, hist_solution, hist_factor, token, parts[n : n + 1], half, name)

    def gather_step(held, step):
        return [
            lax.ppermute(held[n], EVERY, partner_pairs(GATHER[n][step // 2], step % 2 == 1))
            for n in range(2)
        ]

    def sum_step(n, send, step):
        return lax.ppermute(send, EVERY, partner_pairs(PARTS[n][2][step // 2], step % 2 == 1))

    got = lax.ppermute(strip, EVERY, to_first)
    held, token = small_call(pair_kernel, "pair", [(2 * STRIP, width)], [], flags, strip, got)
    got = lax.ppermute(held, EVERY, flip_pairs("z", (3, 3)))
    send0, token = half_product(0, 0, token, "send0")
    held, token = small_call(
        choose_kernel, "choose", [(2 * STRIP, width)], [], flags, held, got, token=token
    )
    got = lax.ppermute(held, EVERY, flip_pairs("z", (1, 1)))
    come = [sum_step(0, send0, 0), None]
    share = STRIP + STRIP // 2
    *held, token = small_call(
        pack_kernel,
        "pack",
        [(share, width)] * 2,
        [pltpu.VMEM((STRIP, width), BF16)],
        flags,
        held,
        got,
        token=token,
    )
    got = gather_step(held, 0)
    send1, token = half_product(1, 0, token, "send1")
    come[1] = sum_step(1, send1, 0)
    held, token = join(held, got, token)
    got = gather_step(held, 1)
    keep0, token = half_product(0, 1, token, "keep0")
    held, token = join(held, got, token)
    got = gather_step(held, 2)
    send0, keep0, token = add(keep0, come[0], token)
    come[0] = sum_step(0, send0, 1)
    keep1, token = half_product(1, 1, token, "keep1")
    send1, keep1, token = add(keep1, come[1], token)
    come[1] = sum_step(1, send1, 1)
    held, token = join(held, got, token)
    got = gather_step(held, 3)
    pieces = [held[0], got[0], held[1], got[1]]
    *inverses, token = grow(chips, pieces, slab)
    keeps = [keep0, keep1]
    for step in range(1, 5):
        for n in range(2):
            if step == 4:
                send, keeps[n], _ = add(keeps[n], come[n], token)
            else:
                middle = keeps[n].shape[0] // 2
                send = keeps[n][:middle] + come[n][:middle]
                keeps[n] = keeps[n][middle:] + come[n][middle:]
            come[n] = sum_step(n, send, step + 1)
    history = jnp.concatenate([keeps[n] + come[n] for n in range(2)], axis=1)
    pending = samples.astype(F32) - history

    first = solve_call(True, core_arg, chips, (pending,), pieces, inverses, "solve0")
    other = lax.ppermute(first, "pcol", [(0, 1)])
    return solve_call(False, core_arg, chips, (pending, first, other), pieces, inverses, "solve1")


def solution(mesh):
    cube = Mesh(mesh.devices.reshape(SIDE, SIDE, SIDE, 2), EVERY)
    return jax.shard_map(
        per_device,
        mesh=cube,
        in_specs=(
            P(None, "pcol", AXES),
            P(None, None, AXES),
            P("pcol", AXES),
            P(AXES, "pcol"),
        ),
        out_specs=P(AXES, "pcol"),
        check_vma=False,
    )
```

```python
import functools

import jax
import jax.numpy as jnp
import numpy as np
from jax import lax
from jax.experimental import pallas as pl
from jax.experimental.pallas import tpu as pltpu
from jax.sharding import Mesh
from jax.sharding import PartitionSpec as P

F32 = jnp.float32
BF16 = jnp.bfloat16
SIDE = 4
ROWS = 16
STRIP = 64
BLOCK = 512
AXES = ("z", "y", "x")
EVERY = ("z", "y", "x", "pcol")
PARTS = ((0, 1024, "zyx"), (1024, 1024, "zxy"))
GATHER = ("yx", "xy")
MB = 1 << 20
TOKEN = jax.ShapeDtypeStruct((8, 128), F32)


def split2(value):
    high = value.astype(BF16)
    return high, (value - high.astype(F32)).astype(BF16)


def dot(a, b):
    return jnp.dot(a, b, preferred_element_type=F32)


def dot_exact(a, b):
    high, low = split2(a)
    rows = a.shape[0]
    both = dot(jnp.concatenate([high, low], axis=0), b)
    return both[:rows] + both[rows:]


def dot_pair(a, b_high, b_low):
    high, low = split2(a)
    rows = a.shape[0]
    both = dot(jnp.concatenate([high, low], axis=0), b_high)
    return both[:rows] + both[rows:] + dot(high, b_low)


def strip_copies(chips, pieces, lower, below, sems, spans):
    own_a, got_a, own_b, got_b = pieces
    half = lower.shape[0] // 2
    cut = STRIP // 2
    groups = ([], [], [])

    def add(group, source, start, count, target, to):
        cols = pl.ds(*spans[group])
        groups[group].append(
            pltpu.make_async_copy(
                source.at[pl.ds(start, count), cols],
                target.at[pl.ds(pl.multiple_of(to, cut), count), cols],
                sems.at[group],
            )
        )

    for position in range(16):
        base = (position % 8) * (STRIP + cut)
        row = pl.multiple_of(chips[position] * STRIP, STRIP)
        source = own_a if position < 8 else got_a
        add(0, source, base, STRIP, lower, row)
        add(1, source, base + STRIP, cut, lower, half + row)
        row = pl.multiple_of(chips[16 + position] * STRIP, STRIP)
        source = own_b if position < 8 else got_b
        add(1, source, base, cut, lower, half + row + cut)
        if below is not None:
            add(2, source, base + cut, STRIP, below, row)
    return groups


def start_all(copies):
    for copy in copies:
        copy.start()


def wait_for(target, sem):
    pltpu.make_async_copy(target, target, sem).wait()


def grow_kernel(chips, own_a, got_a, own_b, got_b, out_high, out_low, token, lower, sems):
    slab = lower.shape[0]
    half = slab // 2
    spans = ((0, slab), (0, slab), (0, slab))
    even, odd, _ = strip_copies(chips, (own_a, got_a, own_b, got_b), lower, None, sems, spans)
    start_all(even)
    start_all(odd)
    del token
    wait_for(lower.at[:half], sems.at[0])
    wait_for(lower.at[half:], sems.at[1])

    rows = lax.broadcasted_iota(jnp.int32, (128, 128), 0)
    lanes = lax.broadcasted_iota(jnp.int32, (128, 128), 1)
    corner = (rows < STRIP) & (lanes >= STRIP)
    same = (rows < STRIP) == (lanes < STRIP)
    upright, turned = [], []
    for k in range(half // 128):
        rng = slice(half + k * 128, half + k * 128 + 128)
        pair = lower[rng, :128].astype(F32) + lower[rng, 128:256].astype(F32)
        swapped = pltpu.roll(pair, STRIP, 1)
        upright.append(jnp.where(same, jnp.where(rows < STRIP, pair, swapped), 0.0))
        turned.append(jnp.where(same, jnp.where(rows < STRIP, swapped, pair), 0.0))
    level = []
    for k, both in enumerate(upright + turned):
        rng = slice(k * 128, k * 128 + 128)
        off = jnp.where(corner, lower[rng, rng].astype(F32), 0.0).astype(BF16)
        level.append(both - dot_pair(dot_exact(both, off), *split2(both)))
    size = 128
    while size < BLOCK:
        grown = []
        for n in range(0, len(level), 2):
            start = n * size
            off = lower[start : start + size, start + size : start + 2 * size]
            high, low = split2(level[n + 1])
            corner_block = -dot_pair(dot_exact(level[n], off), high, low)
            if 2 * size < BLOCK:
                top = jnp.concatenate([level[n], corner_block], axis=1)
                bottom = jnp.concatenate([jnp.zeros_like(corner_block), level[n + 1]], axis=1)
                grown.append(jnp.concatenate([top, bottom], axis=0))
            else:
                b = n // 2
                corner_high, corner_low = split2(corner_block)
                first_high, first_low = split2(level[n])
                zero = jnp.zeros((size, size), BF16)
                for ref, first, mixed, second in (
                    (out_high, first_high, corner_high, high),
                    (out_low, first_low, corner_low, low),
                ):
                    ref[b, :size, :size] = first
                    ref[b, :size, size:] = mixed
                    ref[b, size:, :size] = zero
                    ref[b, size:, size:] = second
        level = grown
        size *= 2


def grow(chips, pieces, slab):
    inverse = jax.ShapeDtypeStruct((slab // BLOCK, BLOCK, BLOCK), BF16)
    vmem = pl.BlockSpec(memory_space=pltpu.VMEM)
    return pl.pallas_call(
        grow_kernel,
        out_shape=(inverse, inverse, TOKEN),
        in_specs=[pl.BlockSpec(memory_space=pltpu.SMEM)] + [pl.BlockSpec(memory_space=pl.ANY)] * 4,
        out_specs=[vmem] * 2 + [pl.BlockSpec(memory_space=pltpu.HBM)],
        scratch_shapes=[pltpu.VMEM((slab, slab), BF16), pltpu.SemaphoreType.DMA((2,))],
        compiler_params=pltpu.CompilerParams(vmem_limit_bytes=28 * MB),
        cost_estimate=pl.CostEstimate(flops=4 * 10**9, bytes_accessed=2 * slab * slab, transcendentals=0),
        name="grow_inverse",
    )(chips, *pieces)


def solve_block(blocks, pending, factor, high, low, out, wait, before_update, after):
    for b in range(blocks):
        cols = slice(b * BLOCK, (b + 1) * BLOCK)
        wait(b)
        y = dot_pair(pending[:, cols], high[b], low[b])
        out[: pending.shape[0], cols] = y
        before_update(b)
        if b + 1 < blocks:
            rest = slice((b + 1) * BLOCK, blocks * BLOCK)
            pending[:, rest] = pending[:, rest] - dot_exact(y, factor[cols, rest])
        after(b, y)


def inverse_copies(inv_high, inv_low, high, low, sems):
    return [
        [
            pltpu.make_async_copy(inv_high.at[b], high.at[b], sems.at[0, b]),
            pltpu.make_async_copy(inv_low.at[b], low.at[b], sems.at[1, b]),
        ]
        for b in range(high.shape[0])
    ]


def solve_kernel(first, core, chips, right, *refs):
    dense = refs[: 0 if first else 2]
    pieces = refs[len(dense) : len(dense) + 4]
    inv_high, inv_low, out, factor, under, high, low, pending, sems, strip_sems = refs[len(dense) + 4 :]
    rows, slab = right.shape
    half = slab // 2
    inner = half // BLOCK
    active = (core[0] == 0) if first else (core[0] != 0)

    @pl.when(active)
    def _():
        spans = ((BLOCK, slab - BLOCK), (half + BLOCK, half - BLOCK), (0, slab))
        even, odd, below = strip_copies(chips, pieces, factor, under, strip_sems, spans)
        inverse = inverse_copies(inv_high, inv_low, high, low, sems)
        order = [inverse[0], even, *inverse[1:], odd, below] if first else [below, *inverse, even, odd]
        for copies in order:
            start_all(copies)
        if first:
            pending[...] = right[...]
        else:
            own, other = dense
            pending[...] = right[...] - other[rows:, :]
            wait_for(under, strip_sems.at[2])
            pending[...] = pending[...] - dot_exact(other[:rows, half:], under[...])

        def wait(b):
            for copy in inverse[b]:
                copy.wait()

        def after(b, y):
            if first and b + 1 == inner:
                wait_for(under, strip_sems.at[2])
                out[rows:, :] = dot_exact(out[:rows, :half], under[...])

        def before_update(b):
            if b == 0:
                wait_for(factor.at[:half, BLOCK:], strip_sems.at[0])
            if b == inner:
                wait_for(factor.at[half:, half + BLOCK :], strip_sems.at[1])

        solve_block(slab // BLOCK, pending, factor, high, low, out, wait, before_update, after)

    @pl.when(jnp.logical_not(active))
    def _():
        out[...] = jnp.zeros_like(out) if first else dense[0][:rows, :]


def solve_call(first, core, chips, dense, pieces, inverses, name):
    rows, slab = dense[0].shape
    blocks = slab // BLOCK
    vmem = pl.BlockSpec(memory_space=pltpu.VMEM)
    smem = pl.BlockSpec(memory_space=pltpu.SMEM)
    return pl.pallas_call(
        functools.partial(solve_kernel, first),
        out_shape=jax.ShapeDtypeStruct((2 * rows if first else rows, slab), F32),
        in_specs=[smem, smem] + [vmem] * len(dense) + [pl.BlockSpec(memory_space=pl.ANY)] * 6,
        out_specs=vmem,
        scratch_shapes=[
            pltpu.VMEM((slab, slab), BF16),
            pltpu.VMEM((slab // 2, slab), BF16),
            pltpu.VMEM((blocks, BLOCK, BLOCK), BF16),
            pltpu.VMEM((blocks, BLOCK, BLOCK), BF16),
            pltpu.VMEM((rows, slab), F32),
            pltpu.SemaphoreType.DMA((2, blocks)),
            pltpu.SemaphoreType.DMA((3,)),
        ],
        compiler_params=pltpu.CompilerParams(vmem_limit_bytes=36 * MB),
        name=name,
    )(core, chips, *dense, *pieces, *inverses)


def product_kernel(parts, half, order, left, right, _, *refs):
    outs, token, (a, b, picked, a_sems, b_sems) = refs[: len(parts)], refs[len(parts)], refs[len(parts) + 1 :]
    del token
    groups, _, depth = left.shape
    rows = picked.shape[0]
    slab = rows // 2
    step = b.shape[1]
    spans = [(n, col) for n in range(len(parts)) for col in range(0, parts[n][2], step)]
    lanes = [pl.ds(g * depth, depth) for g in range(groups)]

    def slabs(n):
        copies = []
        for h in range(2):
            block = order[(2 * parts[n][0] + half) * (rows // ROWS) + h * (slab // ROWS)]
            source = pl.ds(pl.multiple_of(block // (slab // ROWS) * slab, slab), slab)
            for g in range(groups):
                copies.append(
                    pltpu.make_async_copy(
                        left.at[g, source], a.at[pl.ds(h * slab, slab), lanes[g]], a_sems.at[h, g]
                    )
                )
        return copies

    loads = slabs(0)
    for copy in loads:
        copy.start()
    tiles = []
    for t, (n, col) in enumerate(spans):
        tile = [
            pltpu.make_async_copy(
                right.at[g, pl.ds(parts[n][1] + col, step)], b.at[t, :, lanes[g]], b_sems.at[t, g]
            )
            for g in range(groups)
        ]
        for copy in tile:
            copy.start()
        tiles.append(tile)
    for copy in loads:
        copy.wait()
    for t, (n, col) in enumerate(spans):
        if col == 0:
            base = (2 * parts[n][0] + half) * (rows // ROWS)
            for r in range(rows // ROWS):
                inside = order[base + r] % (slab // ROWS) + r // (slab // ROWS) * (slab // ROWS)
                source = pl.ds(pl.multiple_of(inside * ROWS, ROWS), ROWS)
                picked[r * ROWS : (r + 1) * ROWS, :] = a[source, :]
        for copy in tiles[t]:
            copy.wait()
        outs[n][:, col : col + step] = lax.dot_general(
            picked[...], b[t], (((1,), (1,)), ((), ())), preferred_element_type=F32
        )


def product(order, left, right, token, parts, half, name):
    groups, rows, depth = left.shape
    width = sum(part[2] for part in parts)
    step = parts[0][2]
    return pl.pallas_call(
        functools.partial(product_kernel, parts, half),
        out_shape=[jax.ShapeDtypeStruct((rows // 2, part[2]), F32) for part in parts] + [TOKEN],
        in_specs=[pl.BlockSpec(memory_space=pltpu.SMEM)]
        + [pl.BlockSpec(memory_space=pltpu.HBM)] * 3,
        out_specs=[pl.BlockSpec(memory_space=pltpu.VMEM)] * len(parts)
        + [pl.BlockSpec(memory_space=pltpu.HBM)],
        scratch_shapes=[
            pltpu.VMEM((rows // 2, groups * depth), BF16),
            pltpu.VMEM((width // step, step, groups * depth), BF16),
            pltpu.VMEM((rows // 2, groups * depth), BF16),
            pltpu.SemaphoreType.DMA((2, groups)),
            pltpu.SemaphoreType.DMA((width // step, groups)),
        ],
        compiler_params=pltpu.CompilerParams(vmem_limit_bytes=48 * MB),
        cost_estimate=pl.CostEstimate(
            flops=groups * rows * width * depth,
            bytes_accessed=2 * groups * (rows // 2 + width) * depth + 2 * rows * width,
            transcendentals=0,
        ),
        name=name,
    )(order, left, right, token)


def chip_index(z, y, x, c):
    return ((z * SIDE + y) * SIDE + x) * 2 + c


def flip_pairs(axis, masks):
    pairs = []
    for z, y, x, c in np.ndindex(SIDE, SIDE, SIDE, 2):
        place = {"z": z, "y": y, "x": x}
        place[axis] ^= masks[c]
        pairs.append((chip_index(z, y, x, c), chip_index(place["z"], place["y"], place["x"], c)))
    return pairs


def partner_pairs(axis, second):
    return flip_pairs(axis, (3, 1) if second else (1, 3))


def block_order(axes, place, core):
    flip = jnp.where(core == 0, 1, 3)
    masks = jnp.stack([jnp.full_like(flip, 2), flip, flip ^ 2, jnp.zeros_like(flip)])
    lists = {name: place[name] ^ masks for name in AXES}
    shape = {name: [1, 1, 1] for name in AXES}
    for position, name in enumerate(axes):
        shape[name][position] = SIDE
    at = {name: lists[name].reshape(shape[name]) for name in AXES}
    return (((at["z"] * SIDE + at["y"]) * SIDE + at["x"]).reshape(-1)).astype(jnp.int32)


def choose_kernel(which, flags, held, got, *rest):
    out = rest[-2]
    out[...] = jnp.where(flags[which] > 0, held[...], got[...])


def pack_kernel(flags, held, got, under, got_under, out_a, out_b, token, odd):
    del token
    mine = flags[3] > 0
    width = held.shape[1]
    cut = STRIP // 2
    even = out_a.at[:STRIP]
    even[...] = jnp.where(mine, held[...], got[...])
    odd[...] = jnp.where(mine, got[...], held[...])
    out_b[cut:] = jnp.where(mine, under[...], got_under[...])

    at = pl.multiple_of(flags[4] * 128, 128)
    turn = flags[5] > 0
    one = even[:, pl.ds(at, 128)].astype(F32)
    two = odd[:, pl.ds(pl.multiple_of(at + width // 2, 128), 128)].astype(F32)
    one = jnp.where(turn, pltpu.roll(one, STRIP, 1), one)
    two = jnp.where(turn, two, pltpu.roll(two, STRIP, 1))
    rows = lax.broadcasted_iota(jnp.int32, (STRIP, 128), 0)
    lanes = lax.broadcasted_iota(jnp.int32, (STRIP, 128), 1)
    left = lanes < STRIP
    inner = jnp.where(left, lanes, lanes - STRIP)
    block = jnp.where(left, one, two)
    diagonal = jnp.where(inner == rows, block, 0.0)
    scale = jnp.where(
        left,
        1.0 / jnp.sum(jnp.where(left, diagonal, 0.0), axis=1, keepdims=True),
        1.0 / jnp.sum(jnp.where(left, 0.0, diagonal), axis=1, keepdims=True),
    )
    upper = jnp.where(inner > rows, block, 0.0)
    todo = jnp.where(inner == rows, 1.0, 0.0)
    for k in range(STRIP - 1, 0, -1):
        row = todo[k : k + 1, :] * scale[k : k + 1, :]
        col = jnp.where(left, upper[:, k : k + 1], upper[:, STRIP + k : STRIP + k + 1])
        todo = todo - col * row
    high, low = split2(todo * scale)
    odd[:, :128] = high
    odd[:, 128:256] = low
    out_a[STRIP:] = odd[:cut]
    out_b[:cut] = odd[cut:]


def small_call(kernel, name, shapes, scratch, flags, *operands, token=None):
    vmem = pl.BlockSpec(memory_space=pltpu.VMEM)
    hbm = pl.BlockSpec(memory_space=pltpu.HBM)
    tokens = () if token is None else (token,)
    return pl.pallas_call(
        kernel,
        out_shape=[jax.ShapeDtypeStruct(shape, BF16) for shape in shapes] + [TOKEN],
        in_specs=[pl.BlockSpec(memory_space=pltpu.SMEM)]
        + [vmem] * len(operands)
        + [hbm] * len(tokens),
        out_specs=[vmem] * len(shapes) + [hbm],
        scratch_shapes=scratch,
        compiler_params=pltpu.CompilerParams(vmem_limit_bytes=16 * MB),
        name=name,
    )(flags, *operands, *tokens)


def join_kernel(held_a, got_a, held_b, got_b, _, out_a, out_b, token, stage, in_sems, out_sems):
    del token
    loads, stores = [], []
    for n, (held, got, out) in enumerate(((held_a, got_a, out_a), (held_b, got_b, out_b))):
        rows = held.shape[0]
        for h, source in enumerate((held, got)):
            place = pl.ds(h * rows, rows)
            loads.append(pltpu.make_async_copy(source, stage.at[n, place], in_sems.at[n, h]))
            stores.append(pltpu.make_async_copy(stage.at[n, place], out.at[place], out_sems.at[n, h]))
    start_all(loads)
    for load, store in zip(loads, stores):
        load.wait()
        store.start()
    for store in stores:
        store.wait()


def join(held, got, token):
    rows, width = held[0].shape
    shape = jax.ShapeDtypeStruct((2 * rows, width), BF16)
    hbm = pl.BlockSpec(memory_space=pltpu.HBM)
    *joined, token = pl.pallas_call(
        join_kernel,
        out_shape=[shape, shape, TOKEN],
        in_specs=[pl.BlockSpec(memory_space=pl.ANY)] * 4 + [hbm],
        out_specs=[hbm] * 3,
        scratch_shapes=[
            pltpu.VMEM((2, 2 * rows, width), BF16),
            pltpu.SemaphoreType.DMA((2, 2)),
            pltpu.SemaphoreType.DMA((2, 2)),
        ],
        compiler_params=pltpu.CompilerParams(vmem_limit_bytes=12 * MB),
        name="join",
    )(held[0], got[0], held[1], got[1], token)
    return joined, token


def add_kernel(keep, got, _, send, kept, token):
    del token
    middle = send.shape[0]
    send[...] = keep[:middle] + got[:middle]
    kept[...] = keep[middle:] + got[middle:]


def add(keep, got, token):
    vmem = pl.BlockSpec(memory_space=pltpu.VMEM)
    hbm = pl.BlockSpec(memory_space=pltpu.HBM)
    shape = jax.ShapeDtypeStruct((keep.shape[0] // 2, keep.shape[1]), F32)
    return pl.pallas_call(
        add_kernel,
        out_shape=[shape, shape, TOKEN],
        in_specs=[vmem, vmem, hbm],
        out_specs=[vmem, vmem, hbm],
        compiler_params=pltpu.CompilerParams(vmem_limit_bytes=16 * MB),
        name="add",
    )(keep, got, token)


def gather_order(place, core):
    flip = jnp.where(core == 0, 1, 3)
    masks = jnp.stack([jnp.zeros_like(flip), flip, flip ^ 2, jnp.full_like(flip, 2)])
    ys, xs = place["y"] ^ masks, place["x"] ^ masks
    chips = [
        ys[None, :] * SIDE + xs[:, None],
        ys[:, None] * SIDE + xs[None, :],
    ]
    return jnp.concatenate([c.reshape(-1) for c in chips]).astype(jnp.int32)


def per_device(hist_factor, hist_solution, diag_factor, samples):
    slab = hist_factor.shape[1]
    core = lax.axis_index("pcol")
    place = {name: lax.axis_index(name) for name in AXES}
    core_arg = core.astype(jnp.int32).reshape(1)

    order = jnp.concatenate([block_order(axes, place, core) for _, _, axes in PARTS])
    parts = [(n, start, width) for n, (start, width, _) in enumerate(PARTS)]
    z = place["z"]
    at = place["y"] * SIDE + place["x"]
    outer = (z == 0) | (z == 3)
    flags = jnp.stack(
        [core > 0, (z < 2) == (core == 0), z < 2, outer == (core == 0), at // 2, at % 2]
    ).astype(jnp.int32)
    chips = gather_order(place, core)
    strip = diag_factor.T
    width = strip.shape[1]

    def along_z(*moves):
        return [
            (chip_index(start, y, x, c), chip_index(stop, y, x, d))
            for start, c, stop, d in moves
            for y in range(SIDE)
            for x in range(SIDE)
        ]

    def choose(which, own, got, name, token=None):
        kernel = functools.partial(choose_kernel, which)
        return small_call(kernel, name, [(STRIP, width)], [], flags, own, got, token=token)

    def half_product(n, half, token, name):
        return product(order, hist_solution, hist_factor, token, parts[n : n + 1], half, name)

    def gather_step(held, step):
        return [
            lax.ppermute(held[n], EVERY, partner_pairs(GATHER[n][step // 2], step % 2 == 1))
            for n in range(2)
        ]

    def sum_step(n, send, step):
        return lax.ppermute(send, EVERY, partner_pairs(PARTS[n][2][step // 2], step % 2 == 1))

    got = lax.ppermute(strip, EVERY, along_z((0, 0, 3, 0), (1, 0, 2, 0), (2, 1, 1, 1), (3, 1, 0, 1)))
    got_under = lax.ppermute(strip, EVERY, along_z((0, 1, 0, 0)))
    under, token = choose(0, strip, got_under, "below0")
    got_under = lax.ppermute(under, EVERY, along_z((0, 0, 3, 0), (1, 1, 2, 1)))
    mine, token = choose(1, strip, got, "strip1", token=token)
    got = lax.ppermute(mine, EVERY, flip_pairs("z", (1, 1)))
    send0, token = half_product(0, 0, token, "send0")
    under, token = choose(2, under, got_under, "below1", token=token)
    got_under = lax.ppermute(
        under, EVERY, along_z((0, 0, 1, 0), (3, 0, 2, 0), (1, 1, 0, 1), (2, 1, 3, 1))
    )
    come = [sum_step(0, send0, 0), None]
    share = STRIP + STRIP // 2
    *held, token = small_call(
        pack_kernel,
        "pack",
        [(share, width)] * 2,
        [pltpu.VMEM((STRIP, width), BF16)],
        flags,
        mine,
        got,
        under,
        got_under,
    )
    got = gather_step(held, 0)
    send1, token = half_product(1, 0, token, "send1")
    come[1] = sum_step(1, send1, 0)
    held, token = join(held, got, token)
    got = gather_step(held, 1)
    keep0, token = half_product(0, 1, token, "keep0")
    held, token = join(held, got, token)
    got = gather_step(held, 2)
    keep1, token = half_product(1, 1, token, "keep1")
    send0, keep0, token = add(keep0, come[0], token)
    come[0] = sum_step(0, send0, 1)
    held, token = join(held, got, token)
    got = gather_step(held, 3)
    send1, keep1, token = add(keep1, come[1], token)
    come[1] = sum_step(1, send1, 1)
    pieces = [held[0], got[0], held[1], got[1]]
    *inverses, token = grow(chips, pieces, slab)
    keeps = [keep0, keep1]
    for step in range(1, 5):
        for n in range(2):
            if step == 4:
                send, keeps[n], _ = add(keeps[n], come[n], token)
            else:
                middle = keeps[n].shape[0] // 2
                send = keeps[n][:middle] + come[n][:middle]
                keeps[n] = keeps[n][middle:] + come[n][middle:]
            come[n] = sum_step(n, send, step + 1)
    history = jnp.concatenate([keeps[n] + come[n] for n in range(2)], axis=1)
    pending = samples.astype(F32) - history

    first = solve_call(True, core_arg, chips, (pending,), pieces, inverses, "solve0")
    other = lax.ppermute(first, "pcol", [(0, 1)])
    return solve_call(False, core_arg, chips, (pending, first, other), pieces, inverses, "solve1")


def solution(mesh):
    cube = Mesh(mesh.devices.reshape(SIDE, SIDE, SIDE, 2), EVERY)
    return jax.shard_map(
        per_device,
        mesh=cube,
        in_specs=(
            P(None, "pcol", AXES),
            P(None, None, AXES),
            P("pcol", AXES),
            P(AXES, "pcol"),
        ),
        out_specs=P(AXES, "pcol"),
        check_vma=False,
    )
```

```python
import functools

import jax
import jax.numpy as jnp
import numpy as np
from jax import lax
from jax.experimental import pallas as pl
from jax.experimental.pallas import tpu as pltpu
from jax.sharding import Mesh
from jax.sharding import PartitionSpec as P

F32 = jnp.float32
BF16 = jnp.bfloat16
SIDE = 4
ROWS = 16
STRIP = 64
BLOCK = 512
AXES = ("z", "y", "x")
EVERY = ("z", "y", "x", "pcol")
PARTS = ((0, 1024, "zyx"), (1024, 1024, "zxy"))
GATHER = ("yx", "xy")
MB = 1 << 20
SMALL = pl.CostEstimate(flops=1000, bytes_accessed=1000, transcendentals=0)
TOKEN = jax.ShapeDtypeStruct((8, 128), F32)


def split2(value):
    high = value.astype(BF16)
    return high, (value - high.astype(F32)).astype(BF16)


def dot(a, b):
    return jnp.dot(a, b, preferred_element_type=F32)


def dot_exact(a, b):
    high, low = split2(a)
    rows = a.shape[0]
    both = dot(jnp.concatenate([high, low], axis=0), b)
    return both[:rows] + both[rows:]


def dot_pair(a, b_high, b_low):
    high, low = split2(a)
    rows = a.shape[0]
    both = dot(jnp.concatenate([high, low], axis=0), b_high)
    return both[:rows] + both[rows:] + dot(high, b_low)


def strip_copies(chips, pieces, lower, below, sems, spans):
    own_a, got_a, own_b, got_b = pieces
    half = lower.shape[0] // 2
    cut = STRIP // 2
    groups = ([], [], [])

    def add(group, source, start, count, target, to):
        cols = pl.ds(*spans[group])
        groups[group].append(
            pltpu.make_async_copy(
                source.at[pl.ds(start, count), cols],
                target.at[pl.ds(pl.multiple_of(to, cut), count), cols],
                sems.at[group],
            )
        )

    for position in range(16):
        base = (position % 8) * (STRIP + cut)
        row = pl.multiple_of(chips[position] * STRIP, STRIP)
        source = own_a if position < 8 else got_a
        add(0, source, base, STRIP, lower, row)
        add(1, source, base + STRIP, cut, lower, half + row)
        row = pl.multiple_of(chips[16 + position] * STRIP, STRIP)
        source = own_b if position < 8 else got_b
        add(1, source, base, cut, lower, half + row + cut)
        if below is not None:
            add(2, source, base + cut, STRIP, below, row)
    return groups


def start_all(copies):
    for copy in copies:
        copy.start()


def wait_for(target, sem):
    pltpu.make_async_copy(target, target, sem).wait()


def grow_kernel(chips, own_a, got_a, own_b, got_b, out_high, out_low, token, lower, sems):
    slab = lower.shape[0]
    half = slab // 2
    spans = ((0, slab), (0, slab), (0, slab))
    even, odd, _ = strip_copies(chips, (own_a, got_a, own_b, got_b), lower, None, sems, spans)
    start_all(even)
    start_all(odd)
    del token
    wait_for(lower.at[:half], sems.at[0])
    wait_for(lower.at[half:], sems.at[1])

    rows = lax.broadcasted_iota(jnp.int32, (128, 128), 0)
    lanes = lax.broadcasted_iota(jnp.int32, (128, 128), 1)
    corner = (rows < STRIP) & (lanes >= STRIP)
    same = (rows < STRIP) == (lanes < STRIP)
    upright, turned = [], []
    for k in range(half // 128):
        rng = slice(half + k * 128, half + k * 128 + 128)
        pair = lower[rng, :128].astype(F32) + lower[rng, 128:256].astype(F32)
        swapped = pltpu.roll(pair, STRIP, 1)
        upright.append(jnp.where(same, jnp.where(rows < STRIP, pair, swapped), 0.0))
        turned.append(jnp.where(same, jnp.where(rows < STRIP, swapped, pair), 0.0))
    level = []
    for k, both in enumerate(upright + turned):
        rng = slice(k * 128, k * 128 + 128)
        off = jnp.where(corner, lower[rng, rng].astype(F32), 0.0).astype(BF16)
        level.append(both - dot_pair(dot_exact(both, off), *split2(both)))
    size = 128
    while size < BLOCK:
        grown = []
        for n in range(0, len(level), 2):
            start = n * size
            off = lower[start : start + size, start + size : start + 2 * size]
            high, low = split2(level[n + 1])
            corner_block = -dot_pair(dot_exact(level[n], off), high, low)
            if 2 * size < BLOCK:
                top = jnp.concatenate([level[n], corner_block], axis=1)
                bottom = jnp.concatenate([jnp.zeros_like(corner_block), level[n + 1]], axis=1)
                grown.append(jnp.concatenate([top, bottom], axis=0))
            else:
                b = n // 2
                corner_high, corner_low = split2(corner_block)
                first_high, first_low = split2(level[n])
                zero = jnp.zeros((size, size), BF16)
                for ref, first, mixed, second in (
                    (out_high, first_high, corner_high, high),
                    (out_low, first_low, corner_low, low),
                ):
                    ref[b, :size, :size] = first
                    ref[b, :size, size:] = mixed
                    ref[b, size:, :size] = zero
                    ref[b, size:, size:] = second
        level = grown
        size *= 2


def grow(chips, pieces, slab):
    inverse = jax.ShapeDtypeStruct((slab // BLOCK, BLOCK, BLOCK), BF16)
    vmem = pl.BlockSpec(memory_space=pltpu.VMEM)
    return pl.pallas_call(
        grow_kernel,
        out_shape=(inverse, inverse, TOKEN),
        in_specs=[pl.BlockSpec(memory_space=pltpu.SMEM)] + [pl.BlockSpec(memory_space=pl.ANY)] * 4,
        out_specs=[vmem] * 2 + [pl.BlockSpec(memory_space=pltpu.HBM)],
        scratch_shapes=[pltpu.VMEM((slab, slab), BF16), pltpu.SemaphoreType.DMA((2,))],
        compiler_params=pltpu.CompilerParams(vmem_limit_bytes=28 * MB),
        cost_estimate=SMALL,
        name="grow_inverse",
    )(chips, *pieces)


def solve_block(blocks, pending, factor, high, low, out, wait, before_update, after):
    for b in range(blocks):
        cols = slice(b * BLOCK, (b + 1) * BLOCK)
        wait(b)
        y = dot_pair(pending[:, cols], high[b], low[b])
        out[: pending.shape[0], cols] = y
        before_update(b)
        if b + 1 < blocks:
            rest = slice((b + 1) * BLOCK, blocks * BLOCK)
            pending[:, rest] = pending[:, rest] - dot_exact(y, factor[cols, rest])
        after(b, y)


def inverse_copies(inv_high, inv_low, high, low, sems):
    return [
        [
            pltpu.make_async_copy(inv_high.at[b], high.at[b], sems.at[0, b]),
            pltpu.make_async_copy(inv_low.at[b], low.at[b], sems.at[1, b]),
        ]
        for b in range(high.shape[0])
    ]


def solve_kernel(first, core, chips, right, *refs):
    dense = refs[: 0 if first else 2]
    pieces = refs[len(dense) : len(dense) + 4]
    inv_high, inv_low, out, factor, under, high, low, pending, sems, strip_sems = refs[len(dense) + 4 :]
    rows, slab = right.shape
    half = slab // 2
    inner = half // BLOCK
    active = (core[0] == 0) if first else (core[0] != 0)

    @pl.when(active)
    def _():
        spans = ((BLOCK, slab - BLOCK), (half + BLOCK, half - BLOCK), (0, slab))
        even, odd, below = strip_copies(chips, pieces, factor, under, strip_sems, spans)
        inverse = inverse_copies(inv_high, inv_low, high, low, sems)
        order = [inverse[0], even, *inverse[1:], odd, below] if first else [below, *inverse, even, odd]
        for copies in order:
            start_all(copies)
        if first:
            pending[...] = right[...]
        else:
            own, other = dense
            pending[...] = right[...] - other[rows:, :]
            wait_for(under, strip_sems.at[2])
            pending[...] = pending[...] - dot_exact(other[:rows, half:], under[...])

        def wait(b):
            for copy in inverse[b]:
                copy.wait()

        def after(b, y):
            if first and b + 1 == inner:
                wait_for(under, strip_sems.at[2])
                out[rows:, :] = dot_exact(out[:rows, :half], under[...])

        def before_update(b):
            if b == 0:
                wait_for(factor.at[:half, BLOCK:], strip_sems.at[0])
            if b == inner:
                wait_for(factor.at[half:, half + BLOCK :], strip_sems.at[1])

        solve_block(slab // BLOCK, pending, factor, high, low, out, wait, before_update, after)

    @pl.when(jnp.logical_not(active))
    def _():
        out[...] = jnp.zeros_like(out) if first else dense[0][:rows, :]


def solve_call(first, core, chips, dense, pieces, inverses, name):
    rows, slab = dense[0].shape
    blocks = slab // BLOCK
    vmem = pl.BlockSpec(memory_space=pltpu.VMEM)
    smem = pl.BlockSpec(memory_space=pltpu.SMEM)
    return pl.pallas_call(
        functools.partial(solve_kernel, first),
        out_shape=jax.ShapeDtypeStruct((2 * rows if first else rows, slab), F32),
        in_specs=[smem, smem] + [vmem] * len(dense) + [pl.BlockSpec(memory_space=pl.ANY)] * 6,
        out_specs=vmem,
        scratch_shapes=[
            pltpu.VMEM((slab, slab), BF16),
            pltpu.VMEM((slab // 2, slab), BF16),
            pltpu.VMEM((blocks, BLOCK, BLOCK), BF16),
            pltpu.VMEM((blocks, BLOCK, BLOCK), BF16),
            pltpu.VMEM((rows, slab), F32),
            pltpu.SemaphoreType.DMA((2, blocks)),
            pltpu.SemaphoreType.DMA((3,)),
        ],
        compiler_params=pltpu.CompilerParams(vmem_limit_bytes=36 * MB),
        cost_estimate=SMALL,
        name=name,
    )(core, chips, *dense, *pieces, *inverses)


def product_kernel(parts, half, order, left, right, _, *refs):
    outs, token, (a, b, picked, a_sems, b_sems) = refs[: len(parts)], refs[len(parts)], refs[len(parts) + 1 :]
    del token
    groups, _, depth = left.shape
    rows = picked.shape[0]
    slab = rows // 2
    step = b.shape[1]
    spans = [(n, col) for n in range(len(parts)) for col in range(0, parts[n][2], step)]
    lanes = [pl.ds(g * depth, depth) for g in range(groups)]

    def slabs(n):
        copies = []
        for h in range(2):
            block = order[(2 * parts[n][0] + half) * (rows // ROWS) + h * (slab // ROWS)]
            source = pl.ds(pl.multiple_of(block // (slab // ROWS) * slab, slab), slab)
            for g in range(groups):
                copies.append(
                    pltpu.make_async_copy(
                        left.at[g, source], a.at[pl.ds(h * slab, slab), lanes[g]], a_sems.at[h, g]
                    )
                )
        return copies

    loads = slabs(0)
    for copy in loads:
        copy.start()
    tiles = []
    for t, (n, col) in enumerate(spans):
        tile = [
            pltpu.make_async_copy(
                right.at[g, pl.ds(parts[n][1] + col, step)], b.at[t, :, lanes[g]], b_sems.at[t, g]
            )
            for g in range(groups)
        ]
        for copy in tile:
            copy.start()
        tiles.append(tile)
    for copy in loads:
        copy.wait()
    for t, (n, col) in enumerate(spans):
        if col == 0:
            base = (2 * parts[n][0] + half) * (rows // ROWS)
            for r in range(rows // ROWS):
                inside = order[base + r] % (slab // ROWS) + r // (slab // ROWS) * (slab // ROWS)
                source = pl.ds(pl.multiple_of(inside * ROWS, ROWS), ROWS)
                picked[r * ROWS : (r + 1) * ROWS, :] = a[source, :]
        for copy in tiles[t]:
            copy.wait()
        outs[n][:, col : col + step] = lax.dot_general(
            picked[...], b[t], (((1,), (1,)), ((), ())), preferred_element_type=F32
        )


def product(order, left, right, token, parts, half, name):
    groups, rows, depth = left.shape
    width = sum(part[2] for part in parts)
    step = parts[0][2]
    return pl.pallas_call(
        functools.partial(product_kernel, parts, half),
        out_shape=[jax.ShapeDtypeStruct((rows // 2, part[2]), F32) for part in parts] + [TOKEN],
        in_specs=[pl.BlockSpec(memory_space=pltpu.SMEM)]
        + [pl.BlockSpec(memory_space=pltpu.HBM)] * 3,
        out_specs=[pl.BlockSpec(memory_space=pltpu.VMEM)] * len(parts)
        + [pl.BlockSpec(memory_space=pltpu.HBM)],
        scratch_shapes=[
            pltpu.VMEM((rows // 2, groups * depth), BF16),
            pltpu.VMEM((width // step, step, groups * depth), BF16),
            pltpu.VMEM((rows // 2, groups * depth), BF16),
            pltpu.SemaphoreType.DMA((2, groups)),
            pltpu.SemaphoreType.DMA((width // step, groups)),
        ],
        compiler_params=pltpu.CompilerParams(vmem_limit_bytes=48 * MB),
        cost_estimate=SMALL,
        name=name,
    )(order, left, right, token)


def chip_index(z, y, x, c):
    return ((z * SIDE + y) * SIDE + x) * 2 + c


def flip_pairs(axis, masks):
    pairs = []
    for z, y, x, c in np.ndindex(SIDE, SIDE, SIDE, 2):
        place = {"z": z, "y": y, "x": x}
        place[axis] ^= masks[c]
        pairs.append((chip_index(z, y, x, c), chip_index(place["z"], place["y"], place["x"], c)))
    return pairs


def partner_pairs(axis, second):
    return flip_pairs(axis, (3, 1) if second else (1, 3))


def block_order(axes, place, core):
    flip = jnp.where(core == 0, 1, 3)
    masks = jnp.stack([jnp.full_like(flip, 2), flip, flip ^ 2, jnp.zeros_like(flip)])
    lists = {name: place[name] ^ masks for name in AXES}
    shape = {name: [1, 1, 1] for name in AXES}
    for position, name in enumerate(axes):
        shape[name][position] = SIDE
    at = {name: lists[name].reshape(shape[name]) for name in AXES}
    return (((at["z"] * SIDE + at["y"]) * SIDE + at["x"]).reshape(-1)).astype(jnp.int32)


def choose_kernel(which, flags, held, got, *rest):
    out = rest[-2]
    out[...] = jnp.where(flags[which] > 0, held[...], got[...])


def pack_kernel(flags, held, got, under, got_under, out_a, out_b, token, odd):
    del token
    mine = flags[3] > 0
    width = held.shape[1]
    cut = STRIP // 2
    even = out_a.at[:STRIP]
    even[...] = jnp.where(mine, held[...], got[...])
    odd[...] = jnp.where(mine, got[...], held[...])
    out_b[cut:] = jnp.where(mine, under[...], got_under[...])

    at = pl.multiple_of(flags[4] * 128, 128)
    turn = flags[5] > 0
    one = even[:, pl.ds(at, 128)].astype(F32)
    two = odd[:, pl.ds(pl.multiple_of(at + width // 2, 128), 128)].astype(F32)
    one = jnp.where(turn, pltpu.roll(one, STRIP, 1), one)
    two = jnp.where(turn, two, pltpu.roll(two, STRIP, 1))
    rows = lax.broadcasted_iota(jnp.int32, (STRIP, 128), 0)
    lanes = lax.broadcasted_iota(jnp.int32, (STRIP, 128), 1)
    left = lanes < STRIP
    inner = jnp.where(left, lanes, lanes - STRIP)
    block = jnp.where(left, one, two)
    diagonal = jnp.where(inner == rows, block, 0.0)
    scale = jnp.where(
        left,
        1.0 / jnp.sum(jnp.where(left, diagonal, 0.0), axis=1, keepdims=True),
        1.0 / jnp.sum(jnp.where(left, 0.0, diagonal), axis=1, keepdims=True),
    )
    upper = jnp.where(inner > rows, block, 0.0)
    todo = jnp.where(inner == rows, 1.0, 0.0)
    for k in range(STRIP - 1, 0, -1):
        row = todo[k : k + 1, :] * scale[k : k + 1, :]
        col = jnp.where(left, upper[:, k : k + 1], upper[:, STRIP + k : STRIP + k + 1])
        todo = todo - col * row
    high, low = split2(todo * scale)
    odd[:, :128] = high
    odd[:, 128:256] = low
    out_a[STRIP:] = odd[:cut]
    out_b[:cut] = odd[cut:]


def small_call(kernel, name, shapes, scratch, flags, *operands, token=None):
    vmem = pl.BlockSpec(memory_space=pltpu.VMEM)
    hbm = pl.BlockSpec(memory_space=pltpu.HBM)
    tokens = () if token is None else (token,)
    return pl.pallas_call(
        kernel,
        out_shape=[jax.ShapeDtypeStruct(shape, BF16) for shape in shapes] + [TOKEN],
        in_specs=[pl.BlockSpec(memory_space=pltpu.SMEM)]
        + [vmem] * len(operands)
        + [hbm] * len(tokens),
        out_specs=[vmem] * len(shapes) + [hbm],
        scratch_shapes=scratch,
        compiler_params=pltpu.CompilerParams(vmem_limit_bytes=16 * MB),
        cost_estimate=SMALL,
        name=name,
    )(flags, *operands, *tokens)


def join_kernel(held_a, got_a, held_b, got_b, _, out_a, out_b, token, stage, in_sems, out_sems):
    del token
    loads, stores = [], []
    for n, (held, got, out) in enumerate(((held_a, got_a, out_a), (held_b, got_b, out_b))):
        rows = held.shape[0]
        for h, source in enumerate((held, got)):
            place = pl.ds(h * rows, rows)
            loads.append(pltpu.make_async_copy(source, stage.at[n, place], in_sems.at[n, h]))
            stores.append(pltpu.make_async_copy(stage.at[n, place], out.at[place], out_sems.at[n, h]))
    start_all(loads)
    for load, store in zip(loads, stores):
        load.wait()
        store.start()
    for store in stores:
        store.wait()


def join(held, got, token):
    rows, width = held[0].shape
    shape = jax.ShapeDtypeStruct((2 * rows, width), BF16)
    hbm = pl.BlockSpec(memory_space=pltpu.HBM)
    *joined, token = pl.pallas_call(
        join_kernel,
        out_shape=[shape, shape, TOKEN],
        in_specs=[pl.BlockSpec(memory_space=pl.ANY)] * 4 + [hbm],
        out_specs=[hbm] * 3,
        scratch_shapes=[
            pltpu.VMEM((2, 2 * rows, width), BF16),
            pltpu.SemaphoreType.DMA((2, 2)),
            pltpu.SemaphoreType.DMA((2, 2)),
        ],
        compiler_params=pltpu.CompilerParams(vmem_limit_bytes=12 * MB),
        cost_estimate=SMALL,
        name="join",
    )(held[0], got[0], held[1], got[1], token)
    return joined, token


def add_kernel(keep, got, _, send, kept, token):
    del token
    middle = send.shape[0]
    send[...] = keep[:middle] + got[:middle]
    kept[...] = keep[middle:] + got[middle:]


def add(keep, got, token):
    vmem = pl.BlockSpec(memory_space=pltpu.VMEM)
    hbm = pl.BlockSpec(memory_space=pltpu.HBM)
    shape = jax.ShapeDtypeStruct((keep.shape[0] // 2, keep.shape[1]), F32)
    return pl.pallas_call(
        add_kernel,
        out_shape=[shape, shape, TOKEN],
        in_specs=[vmem, vmem, hbm],
        out_specs=[vmem, vmem, hbm],
        compiler_params=pltpu.CompilerParams(vmem_limit_bytes=16 * MB),
        cost_estimate=SMALL,
        name="add",
    )(keep, got, token)


def gather_order(place, core):
    flip = jnp.where(core == 0, 1, 3)
    masks = jnp.stack([jnp.zeros_like(flip), flip, flip ^ 2, jnp.full_like(flip, 2)])
    ys, xs = place["y"] ^ masks, place["x"] ^ masks
    chips = [
        ys[None, :] * SIDE + xs[:, None],
        ys[:, None] * SIDE + xs[None, :],
    ]
    return jnp.concatenate([c.reshape(-1) for c in chips]).astype(jnp.int32)


def per_device(hist_factor, hist_solution, diag_factor, samples):
    slab = hist_factor.shape[1]
    core = lax.axis_index("pcol")
    place = {name: lax.axis_index(name) for name in AXES}
    core_arg = core.astype(jnp.int32).reshape(1)

    order = jnp.concatenate([block_order(axes, place, core) for _, _, axes in PARTS])
    parts = [(n, start, width) for n, (start, width, _) in enumerate(PARTS)]
    z = place["z"]
    at = place["y"] * SIDE + place["x"]
    outer = (z == 0) | (z == 3)
    flags = jnp.stack(
        [core > 0, (z < 2) == (core == 0), z < 2, outer == (core == 0), at // 2, at % 2]
    ).astype(jnp.int32)
    chips = gather_order(place, core)
    strip = diag_factor.T
    width = strip.shape[1]

    def along_z(*moves):
        return [
            (chip_index(start, y, x, c), chip_index(stop, y, x, d))
            for start, c, stop, d in moves
            for y in range(SIDE)
            for x in range(SIDE)
        ]

    def choose(which, own, got, name, token=None):
        kernel = functools.partial(choose_kernel, which)
        return small_call(kernel, name, [(STRIP, width)], [], flags, own, got, token=token)

    def half_product(n, half, token, name):
        return product(order, hist_solution, hist_factor, token, parts[n : n + 1], half, name)

    def gather_step(held, step):
        return [
            lax.ppermute(held[n], EVERY, partner_pairs(GATHER[n][step // 2], step % 2 == 1))
            for n in range(2)
        ]

    def sum_step(n, send, step):
        return lax.ppermute(send, EVERY, partner_pairs(PARTS[n][2][step // 2], step % 2 == 1))

    got = lax.ppermute(strip, EVERY, along_z((0, 0, 3, 0), (1, 0, 2, 0), (2, 1, 1, 1), (3, 1, 0, 1)))
    got_under = lax.ppermute(strip, EVERY, along_z((0, 1, 0, 0)))
    under, token = choose(0, strip, got_under, "below0")
    got_under = lax.ppermute(under, EVERY, along_z((0, 0, 3, 0), (1, 1, 2, 1)))
    mine, token = choose(1, strip, got, "strip1", token=token)
    got = lax.ppermute(mine, EVERY, flip_pairs("z", (1, 1)))
    send0, token = half_product(0, 0, token, "send0")
    under, token = choose(2, under, got_under, "below1", token=token)
    got_under = lax.ppermute(
        under, EVERY, along_z((0, 0, 1, 0), (3, 0, 2, 0), (1, 1, 0, 1), (2, 1, 3, 1))
    )
    come = [sum_step(0, send0, 0), None]
    share = STRIP + STRIP // 2
    *held, token = small_call(
        pack_kernel,
        "pack",
        [(share, width)] * 2,
        [pltpu.VMEM((STRIP, width), BF16)],
        flags,
        mine,
        got,
        under,
        got_under,
    )
    got = gather_step(held, 0)
    send1, token = half_product(1, 0, token, "send1")
    come[1] = sum_step(1, send1, 0)
    held, token = join(held, got, token)
    got = gather_step(held, 1)
    keep0, token = half_product(0, 1, token, "keep0")
    held, token = join(held, got, token)
    got = gather_step(held, 2)
    keep1, token = half_product(1, 1, token, "keep1")
    send0, keep0, token = add(keep0, come[0], token)
    come[0] = sum_step(0, send0, 1)
    held, token = join(held, got, token)
    got = gather_step(held, 3)
    send1, keep1, token = add(keep1, come[1], token)
    come[1] = sum_step(1, send1, 1)
    pieces = [held[0], got[0], held[1], got[1]]
    *inverses, token = grow(chips, pieces, slab)
    keeps = [keep0, keep1]
    for step in range(1, 5):
        for n in range(2):
            if step == 4:
                send, keeps[n], _ = add(keeps[n], come[n], token)
            else:
                middle = keeps[n].shape[0] // 2
                send = keeps[n][:middle] + come[n][:middle]
                keeps[n] = keeps[n][middle:] + come[n][middle:]
            come[n] = sum_step(n, send, step + 1)
    history = jnp.concatenate([keeps[n] + come[n] for n in range(2)], axis=1)
    pending = samples.astype(F32) - history

    first = solve_call(True, core_arg, chips, (pending,), pieces, inverses, "solve0")
    other = lax.ppermute(first, "pcol", [(0, 1)])
    return solve_call(False, core_arg, chips, (pending, first, other), pieces, inverses, "solve1")


def solution(mesh):
    cube = Mesh(mesh.devices.reshape(SIDE, SIDE, SIDE, 2), EVERY)
    return jax.shard_map(
        per_device,
        mesh=cube,
        in_specs=(
            P(None, "pcol", AXES),
            P(None, None, AXES),
            P("pcol", AXES),
            P(AXES, "pcol"),
        ),
        out_specs=P(AXES, "pcol"),
        check_vma=False,
    )
```

```python
import functools

import jax
import jax.numpy as jnp
import numpy as np
from jax import lax
from jax.experimental import pallas as pl
from jax.experimental.pallas import tpu as pltpu
from jax.sharding import Mesh
from jax.sharding import PartitionSpec as P

F32 = jnp.float32
BF16 = jnp.bfloat16
SIDE = 4
ROWS = 16
STRIP = 64
BLOCK = 512
AXES = ("z", "y", "x")
EVERY = ("z", "y", "x", "pcol")
PARTS = ((0, 1024, "zyx"), (1024, 1024, "zxy"))
GATHER = ("yx", "xy")
MB = 1 << 20
SMALL = pl.CostEstimate(flops=1000, bytes_accessed=1000, transcendentals=0)
TOKEN = jax.ShapeDtypeStruct((8, 128), F32)


def split2(value):
    high = value.astype(BF16)
    return high, (value - high.astype(F32)).astype(BF16)


def dot(a, b):
    return jnp.dot(a, b, preferred_element_type=F32)


def dot_exact(a, b):
    high, low = split2(a)
    rows = a.shape[0]
    both = dot(jnp.concatenate([high, low], axis=0), b)
    return both[:rows] + both[rows:]


def dot_pair(a, b_high, b_low):
    high, low = split2(a)
    rows = a.shape[0]
    both = dot(jnp.concatenate([high, low], axis=0), b_high)
    return both[:rows] + both[rows:] + dot(high, b_low)


def strip_copies(chips, pieces, lower, below, sems, spans):
    own_a, got_a, own_b, got_b = pieces
    half = lower.shape[0] // 2
    cut = STRIP // 2
    groups = ([], [], [])

    def add(group, source, start, count, target, to):
        cols = pl.ds(*spans[group])
        groups[group].append(
            pltpu.make_async_copy(
                source.at[pl.ds(start, count), cols],
                target.at[pl.ds(pl.multiple_of(to, cut), count), cols],
                sems.at[group],
            )
        )

    for position in range(16):
        base = (position % 8) * (STRIP + cut)
        row = pl.multiple_of(chips[position] * STRIP, STRIP)
        source = own_a if position < 8 else got_a
        add(0, source, base, STRIP, lower, row)
        add(1, source, base + STRIP, cut, lower, half + row)
        row = pl.multiple_of(chips[16 + position] * STRIP, STRIP)
        source = own_b if position < 8 else got_b
        add(1, source, base, cut, lower, half + row + cut)
        if below is not None:
            add(2, source, base + cut, STRIP, below, row)
    return groups


def start_all(copies):
    for copy in copies:
        copy.start()


def wait_for(target, sem):
    pltpu.make_async_copy(target, target, sem).wait()


def grow_kernel(chips, own_a, got_a, own_b, got_b, out_high, out_low, token, lower, sems):
    slab = lower.shape[0]
    half = slab // 2
    spans = ((0, slab), (0, slab), (0, slab))
    even, odd, _ = strip_copies(chips, (own_a, got_a, own_b, got_b), lower, None, sems, spans)
    start_all(even)
    start_all(odd)
    del token
    wait_for(lower.at[:half], sems.at[0])
    wait_for(lower.at[half:], sems.at[1])

    rows = lax.broadcasted_iota(jnp.int32, (128, 128), 0)
    lanes = lax.broadcasted_iota(jnp.int32, (128, 128), 1)
    corner = (rows < STRIP) & (lanes >= STRIP)
    same = (rows < STRIP) == (lanes < STRIP)
    upright, turned = [], []
    for k in range(half // 128):
        rng = slice(half + k * 128, half + k * 128 + 128)
        pair = lower[rng, :128].astype(F32) + lower[rng, 128:256].astype(F32)
        swapped = pltpu.roll(pair, STRIP, 1)
        upright.append(jnp.where(same, jnp.where(rows < STRIP, pair, swapped), 0.0))
        turned.append(jnp.where(same, jnp.where(rows < STRIP, swapped, pair), 0.0))
    level = []
    for k, both in enumerate(upright + turned):
        rng = slice(k * 128, k * 128 + 128)
        off = jnp.where(corner, lower[rng, rng].astype(F32), 0.0).astype(BF16)
        level.append(both - dot_pair(dot_exact(both, off), *split2(both)))
    size = 128
    while size < BLOCK:
        grown = []
        for n in range(0, len(level), 2):
            start = n * size
            off = lower[start : start + size, start + size : start + 2 * size]
            high, low = split2(level[n + 1])
            corner_block = -dot_pair(dot_exact(level[n], off), high, low)
            if 2 * size < BLOCK:
                top = jnp.concatenate([level[n], corner_block], axis=1)
                bottom = jnp.concatenate([jnp.zeros_like(corner_block), level[n + 1]], axis=1)
                grown.append(jnp.concatenate([top, bottom], axis=0))
            else:
                b = n // 2
                corner_high, corner_low = split2(corner_block)
                first_high, first_low = split2(level[n])
                zero = jnp.zeros((size, size), BF16)
                for ref, first, mixed, second in (
                    (out_high, first_high, corner_high, high),
                    (out_low, first_low, corner_low, low),
                ):
                    ref[b, :size, :size] = first
                    ref[b, :size, size:] = mixed
                    ref[b, size:, :size] = zero
                    ref[b, size:, size:] = second
        level = grown
        size *= 2


def grow(chips, pieces, slab):
    inverse = jax.ShapeDtypeStruct((slab // BLOCK, BLOCK, BLOCK), BF16)
    vmem = pl.BlockSpec(memory_space=pltpu.VMEM)
    return pl.pallas_call(
        grow_kernel,
        out_shape=(inverse, inverse, TOKEN),
        in_specs=[pl.BlockSpec(memory_space=pltpu.SMEM)] + [pl.BlockSpec(memory_space=pl.ANY)] * 4,
        out_specs=[vmem] * 2 + [pl.BlockSpec(memory_space=pltpu.HBM)],
        scratch_shapes=[pltpu.VMEM((slab, slab), BF16), pltpu.SemaphoreType.DMA((2,))],
        compiler_params=pltpu.CompilerParams(vmem_limit_bytes=28 * MB),
        cost_estimate=SMALL,
        name="grow_inverse",
    )(chips, *pieces)


def solve_block(blocks, pending, factor, high, low, out, wait, before_update, after):
    for b in range(blocks):
        cols = slice(b * BLOCK, (b + 1) * BLOCK)
        wait(b)
        y = dot_pair(pending[:, cols], high[b], low[b])
        out[: pending.shape[0], cols] = y
        before_update(b)
        if b + 1 < blocks:
            rest = slice((b + 1) * BLOCK, blocks * BLOCK)
            pending[:, rest] = pending[:, rest] - dot_exact(y, factor[cols, rest])
        after(b, y)


def inverse_copies(inv_high, inv_low, high, low, sems):
    return [
        [
            pltpu.make_async_copy(inv_high.at[b], high.at[b], sems.at[0, b]),
            pltpu.make_async_copy(inv_low.at[b], low.at[b], sems.at[1, b]),
        ]
        for b in range(high.shape[0])
    ]


def solve_kernel(first, core, chips, right, *refs):
    dense = refs[: 0 if first else 2]
    pieces = refs[len(dense) : len(dense) + 4]
    inv_high, inv_low, out, factor, under, high, low, pending, sems, strip_sems = refs[len(dense) + 4 :]
    rows, slab = right.shape
    half = slab // 2
    inner = half // BLOCK
    active = (core[0] == 0) if first else (core[0] != 0)

    @pl.when(active)
    def _():
        spans = ((BLOCK, slab - BLOCK), (half + BLOCK, half - BLOCK), (0, slab))
        even, odd, below = strip_copies(chips, pieces, factor, under, strip_sems, spans)
        inverse = inverse_copies(inv_high, inv_low, high, low, sems)
        order = [inverse[0], even, *inverse[1:], odd, below] if first else [below, *inverse, even, odd]
        for copies in order:
            start_all(copies)
        if first:
            pending[...] = right[...]
        else:
            own, other = dense
            pending[...] = right[...] - other[rows:, :]
            wait_for(under, strip_sems.at[2])
            pending[...] = pending[...] - dot_exact(other[:rows, half:], under[...])

        def wait(b):
            for copy in inverse[b]:
                copy.wait()

        def after(b, y):
            if first and b + 1 == inner:
                wait_for(under, strip_sems.at[2])
                out[rows:, :] = dot_exact(out[:rows, :half], under[...])

        def before_update(b):
            if b == 0:
                wait_for(factor.at[:half, BLOCK:], strip_sems.at[0])
            if b == inner:
                wait_for(factor.at[half:, half + BLOCK :], strip_sems.at[1])

        solve_block(slab // BLOCK, pending, factor, high, low, out, wait, before_update, after)

    @pl.when(jnp.logical_not(active))
    def _():
        out[...] = jnp.zeros_like(out) if first else dense[0][:rows, :]


def solve_call(first, core, chips, dense, pieces, inverses, name):
    rows, slab = dense[0].shape
    blocks = slab // BLOCK
    vmem = pl.BlockSpec(memory_space=pltpu.VMEM)
    smem = pl.BlockSpec(memory_space=pltpu.SMEM)
    return pl.pallas_call(
        functools.partial(solve_kernel, first),
        out_shape=jax.ShapeDtypeStruct((2 * rows if first else rows, slab), F32),
        in_specs=[smem, smem] + [vmem] * len(dense) + [pl.BlockSpec(memory_space=pl.ANY)] * 6,
        out_specs=vmem,
        scratch_shapes=[
            pltpu.VMEM((slab, slab), BF16),
            pltpu.VMEM((slab // 2, slab), BF16),
            pltpu.VMEM((blocks, BLOCK, BLOCK), BF16),
            pltpu.VMEM((blocks, BLOCK, BLOCK), BF16),
            pltpu.VMEM((rows, slab), F32),
            pltpu.SemaphoreType.DMA((2, blocks)),
            pltpu.SemaphoreType.DMA((3,)),
        ],
        compiler_params=pltpu.CompilerParams(vmem_limit_bytes=36 * MB),
        cost_estimate=SMALL,
        name=name,
    )(core, chips, *dense, *pieces, *inverses)


def product_kernel(parts, half, order, left, right, _, *refs):
    outs, token, (a, b, picked, a_sems, b_sems) = refs[: len(parts)], refs[len(parts)], refs[len(parts) + 1 :]
    del token
    groups, _, depth = left.shape
    rows = picked.shape[0]
    slab = rows // 2
    step = b.shape[1]
    spans = [(n, col) for n in range(len(parts)) for col in range(0, parts[n][2], step)]
    lanes = [pl.ds(g * depth, depth) for g in range(groups)]

    def slabs(n):
        copies = []
        for h in range(2):
            block = order[(2 * parts[n][0] + half) * (rows // ROWS) + h * (slab // ROWS)]
            source = pl.ds(pl.multiple_of(block // (slab // ROWS) * slab, slab), slab)
            for g in range(groups):
                copies.append(
                    pltpu.make_async_copy(
                        left.at[g, source], a.at[pl.ds(h * slab, slab), lanes[g]], a_sems.at[h, g]
                    )
                )
        return copies

    loads = slabs(0)
    for copy in loads:
        copy.start()
    tiles = []
    for t, (n, col) in enumerate(spans):
        tile = [
            pltpu.make_async_copy(
                right.at[g, pl.ds(parts[n][1] + col, step)], b.at[t, :, lanes[g]], b_sems.at[t, g]
            )
            for g in range(groups)
        ]
        for copy in tile:
            copy.start()
        tiles.append(tile)
    for copy in loads:
        copy.wait()
    for t, (n, col) in enumerate(spans):
        if col == 0:
            base = (2 * parts[n][0] + half) * (rows // ROWS)
            for r in range(rows // ROWS):
                inside = order[base + r] % (slab // ROWS) + r // (slab // ROWS) * (slab // ROWS)
                source = pl.ds(pl.multiple_of(inside * ROWS, ROWS), ROWS)
                picked[r * ROWS : (r + 1) * ROWS, :] = a[source, :]
        for copy in tiles[t]:
            copy.wait()
        outs[n][:, col : col + step] = lax.dot_general(
            picked[...], b[t], (((1,), (1,)), ((), ())), preferred_element_type=F32
        )


def product(order, left, right, token, parts, half, name):
    groups, rows, depth = left.shape
    width = sum(part[2] for part in parts)
    step = parts[0][2]
    return pl.pallas_call(
        functools.partial(product_kernel, parts, half),
        out_shape=[jax.ShapeDtypeStruct((rows // 2, part[2]), F32) for part in parts] + [TOKEN],
        in_specs=[pl.BlockSpec(memory_space=pltpu.SMEM)]
        + [pl.BlockSpec(memory_space=pltpu.HBM)] * 3,
        out_specs=[pl.BlockSpec(memory_space=pltpu.VMEM)] * len(parts)
        + [pl.BlockSpec(memory_space=pltpu.HBM)],
        scratch_shapes=[
            pltpu.VMEM((rows // 2, groups * depth), BF16),
            pltpu.VMEM((width // step, step, groups * depth), BF16),
            pltpu.VMEM((rows // 2, groups * depth), BF16),
            pltpu.SemaphoreType.DMA((2, groups)),
            pltpu.SemaphoreType.DMA((width // step, groups)),
        ],
        compiler_params=pltpu.CompilerParams(vmem_limit_bytes=48 * MB),
        cost_estimate=SMALL,
        name=name,
    )(order, left, right, token)


def chip_index(z, y, x, c):
    return ((z * SIDE + y) * SIDE + x) * 2 + c


def flip_pairs(axis, masks):
    pairs = []
    for z, y, x, c in np.ndindex(SIDE, SIDE, SIDE, 2):
        place = {"z": z, "y": y, "x": x}
        place[axis] ^= masks[c]
        pairs.append((chip_index(z, y, x, c), chip_index(place["z"], place["y"], place["x"], c)))
    return pairs


def partner_pairs(axis, second):
    return flip_pairs(axis, (3, 1) if second else (1, 3))


def block_order(axes, place, core):
    flip = jnp.where(core == 0, 1, 3)
    masks = jnp.stack([jnp.full_like(flip, 2), flip, flip ^ 2, jnp.zeros_like(flip)])
    lists = {name: place[name] ^ masks for name in AXES}
    shape = {name: [1, 1, 1] for name in AXES}
    for position, name in enumerate(axes):
        shape[name][position] = SIDE
    at = {name: lists[name].reshape(shape[name]) for name in AXES}
    return (((at["z"] * SIDE + at["y"]) * SIDE + at["x"]).reshape(-1)).astype(jnp.int32)


def choose_kernel(which, flags, held, got, *rest):
    out = rest[-2]
    out[...] = jnp.where(flags[which] > 0, held[...], got[...])


def pack_kernel(flags, held, got, under, got_under, out_a, out_b, token, odd):
    del token
    mine = flags[3] > 0
    width = held.shape[1]
    cut = STRIP // 2
    even = out_a.at[:STRIP]
    even[...] = jnp.where(mine, held[...], got[...])
    odd[...] = jnp.where(mine, got[...], held[...])
    out_b[cut:] = jnp.where(mine, under[...], got_under[...])

    at = pl.multiple_of(flags[4] * 128, 128)
    turn = flags[5] > 0
    one = even[:, pl.ds(at, 128)].astype(F32)
    two = odd[:, pl.ds(pl.multiple_of(at + width // 2, 128), 128)].astype(F32)
    one = jnp.where(turn, pltpu.roll(one, STRIP, 1), one)
    two = jnp.where(turn, two, pltpu.roll(two, STRIP, 1))
    rows = lax.broadcasted_iota(jnp.int32, (STRIP, 128), 0)
    lanes = lax.broadcasted_iota(jnp.int32, (STRIP, 128), 1)
    left = lanes < STRIP
    inner = jnp.where(left, lanes, lanes - STRIP)
    block = jnp.where(left, one, two)
    diagonal = jnp.where(inner == rows, block, 0.0)
    scale = jnp.where(
        left,
        1.0 / jnp.sum(jnp.where(left, diagonal, 0.0), axis=1, keepdims=True),
        1.0 / jnp.sum(jnp.where(left, 0.0, diagonal), axis=1, keepdims=True),
    )
    upper = jnp.where(inner > rows, block, 0.0)
    todo = jnp.where(inner == rows, 1.0, 0.0)
    for k in range(STRIP - 1, 0, -1):
        row = todo[k : k + 1, :] * scale[k : k + 1, :]
        col = jnp.where(left, upper[:, k : k + 1], upper[:, STRIP + k : STRIP + k + 1])
        todo = todo - col * row
    high, low = split2(todo * scale)
    odd[:, :128] = high
    odd[:, 128:256] = low
    out_a[STRIP:] = odd[:cut]
    out_b[:cut] = odd[cut:]


def small_call(kernel, name, shapes, scratch, flags, *operands, token=None):
    vmem = pl.BlockSpec(memory_space=pltpu.VMEM)
    hbm = pl.BlockSpec(memory_space=pltpu.HBM)
    tokens = () if token is None else (token,)
    return pl.pallas_call(
        kernel,
        out_shape=[jax.ShapeDtypeStruct(shape, BF16) for shape in shapes] + [TOKEN],
        in_specs=[pl.BlockSpec(memory_space=pltpu.SMEM)]
        + [vmem] * len(operands)
        + [hbm] * len(tokens),
        out_specs=[vmem] * len(shapes) + [hbm],
        scratch_shapes=scratch,
        compiler_params=pltpu.CompilerParams(vmem_limit_bytes=16 * MB),
        cost_estimate=SMALL,
        name=name,
    )(flags, *operands, *tokens)


def join_kernel(held_a, got_a, held_b, got_b, _, out_a, out_b, token, stage, in_sems, out_sems):
    del token
    loads, stores = [], []
    for n, (held, got, out) in enumerate(((held_a, got_a, out_a), (held_b, got_b, out_b))):
        rows = held.shape[0]
        for h, source in enumerate((held, got)):
            place = pl.ds(h * rows, rows)
            loads.append(pltpu.make_async_copy(source, stage.at[n, place], in_sems.at[n, h]))
            stores.append(pltpu.make_async_copy(stage.at[n, place], out.at[place], out_sems.at[n, h]))
    start_all(loads)
    for load, store in zip(loads, stores):
        load.wait()
        store.start()
    for store in stores:
        store.wait()


def join(held, got, token):
    rows, width = held[0].shape
    shape = jax.ShapeDtypeStruct((2 * rows, width), BF16)
    hbm = pl.BlockSpec(memory_space=pltpu.HBM)
    *joined, token = pl.pallas_call(
        join_kernel,
        out_shape=[shape, shape, TOKEN],
        in_specs=[pl.BlockSpec(memory_space=pl.ANY)] * 4 + [hbm],
        out_specs=[hbm] * 3,
        scratch_shapes=[
            pltpu.VMEM((2, 2 * rows, width), BF16),
            pltpu.SemaphoreType.DMA((2, 2)),
            pltpu.SemaphoreType.DMA((2, 2)),
        ],
        compiler_params=pltpu.CompilerParams(vmem_limit_bytes=12 * MB),
        cost_estimate=SMALL,
        name="join",
    )(held[0], got[0], held[1], got[1], token)
    return joined, token


def add_kernel(keep, got, _, send, kept, token):
    del token
    middle = send.shape[0]
    send[...] = keep[:middle] + got[:middle]
    kept[...] = keep[middle:] + got[middle:]


def add(keep, got, token):
    vmem = pl.BlockSpec(memory_space=pltpu.VMEM)
    hbm = pl.BlockSpec(memory_space=pltpu.HBM)
    shape = jax.ShapeDtypeStruct((keep.shape[0] // 2, keep.shape[1]), F32)
    return pl.pallas_call(
        add_kernel,
        out_shape=[shape, shape, TOKEN],
        in_specs=[vmem, vmem, hbm],
        out_specs=[vmem, vmem, hbm],
        compiler_params=pltpu.CompilerParams(vmem_limit_bytes=16 * MB),
        cost_estimate=SMALL,
        name="add",
    )(keep, got, token)


def gather_order(place, core):
    flip = jnp.where(core == 0, 1, 3)
    masks = jnp.stack([jnp.zeros_like(flip), flip, flip ^ 2, jnp.full_like(flip, 2)])
    ys, xs = place["y"] ^ masks, place["x"] ^ masks
    chips = [
        ys[None, :] * SIDE + xs[:, None],
        ys[:, None] * SIDE + xs[None, :],
    ]
    return jnp.concatenate([c.reshape(-1) for c in chips]).astype(jnp.int32)


def per_device(hist_factor, hist_solution, diag_factor, samples):
    slab = hist_factor.shape[1]
    core = lax.axis_index("pcol")
    place = {name: lax.axis_index(name) for name in AXES}
    core_arg = core.astype(jnp.int32).reshape(1)

    order = jnp.concatenate([block_order(axes, place, core) for _, _, axes in PARTS])
    parts = [(n, start, width) for n, (start, width, _) in enumerate(PARTS)]
    z = place["z"]
    at = place["y"] * SIDE + place["x"]
    outer = (z == 0) | (z == 3)
    flags = jnp.stack(
        [core > 0, (z < 2) == (core == 0), z < 2, outer == (core == 0), at // 2, at % 2]
    ).astype(jnp.int32)
    chips = gather_order(place, core)
    strip = diag_factor.T
    width = strip.shape[1]

    def along_z(*moves):
        return [
            (chip_index(start, y, x, c), chip_index(stop, y, x, d))
            for start, c, stop, d in moves
            for y in range(SIDE)
            for x in range(SIDE)
        ]

    def choose(which, own, got, name, token=None):
        kernel = functools.partial(choose_kernel, which)
        return small_call(kernel, name, [(STRIP, width)], [], flags, own, got, token=token)

    def half_product(n, half, token, name):
        return product(order, hist_solution, hist_factor, token, parts[n : n + 1], half, name)

    def gather_step(held, step):
        return [
            lax.ppermute(held[n], EVERY, partner_pairs(GATHER[n][step // 2], step % 2 == 1))
            for n in range(2)
        ]

    def sum_step(n, send, step):
        return lax.ppermute(send, EVERY, partner_pairs(PARTS[n][2][step // 2], step % 2 == 1))

    got = lax.ppermute(strip, EVERY, along_z((0, 0, 3, 0), (1, 0, 2, 0), (2, 1, 1, 1), (3, 1, 0, 1)))
    got_under = lax.ppermute(strip, EVERY, along_z((0, 1, 0, 0)))
    under, token = choose(0, strip, got_under, "below0")
    got_under = lax.ppermute(under, EVERY, along_z((0, 0, 3, 0), (1, 1, 2, 1)))
    mine, token = choose(1, strip, got, "strip1", token=token)
    got = lax.ppermute(mine, EVERY, flip_pairs("z", (1, 1)))
    send0, token = half_product(0, 0, token, "send0")
    under, token = choose(2, under, got_under, "below1", token=token)
    got_under = lax.ppermute(
        under, EVERY, along_z((0, 0, 1, 0), (3, 0, 2, 0), (1, 1, 0, 1), (2, 1, 3, 1))
    )
    come = [sum_step(0, send0, 0), None]
    share = STRIP + STRIP // 2
    *held, token = small_call(
        pack_kernel,
        "pack",
        [(share, width)] * 2,
        [pltpu.VMEM((STRIP, width), BF16)],
        flags,
        mine,
        got,
        under,
        got_under,
    )
    got = gather_step(held, 0)
    held, token = join(held, got, token)
    got = gather_step(held, 1)
    send1, token = half_product(1, 0, token, "send1")
    come[1] = sum_step(1, send1, 0)
    held, token = join(held, got, token)
    got = gather_step(held, 2)
    keep0, token = half_product(0, 1, token, "keep0")
    send0, keep0, token = add(keep0, come[0], token)
    come[0] = sum_step(0, send0, 1)
    keep1, token = half_product(1, 1, token, "keep1")
    held, token = join(held, got, token)
    got = gather_step(held, 3)
    send1, keep1, token = add(keep1, come[1], token)
    come[1] = sum_step(1, send1, 1)
    pieces = [held[0], got[0], held[1], got[1]]
    *inverses, token = grow(chips, pieces, slab)
    keeps = [keep0, keep1]
    for step in range(1, 5):
        for n in range(2):
            if step == 4:
                send, keeps[n], _ = add(keeps[n], come[n], token)
            else:
                middle = keeps[n].shape[0] // 2
                send = keeps[n][:middle] + come[n][:middle]
                keeps[n] = keeps[n][middle:] + come[n][middle:]
            come[n] = sum_step(n, send, step + 1)
    history = jnp.concatenate([keeps[n] + come[n] for n in range(2)], axis=1)
    pending = samples.astype(F32) - history

    first = solve_call(True, core_arg, chips, (pending,), pieces, inverses, "solve0")
    other = lax.ppermute(first, "pcol", [(0, 1)])
    return solve_call(False, core_arg, chips, (pending, first, other), pieces, inverses, "solve1")


def solution(mesh):
    cube = Mesh(mesh.devices.reshape(SIDE, SIDE, SIDE, 2), EVERY)
    return jax.shard_map(
        per_device,
        mesh=cube,
        in_specs=(
            P(None, "pcol", AXES),
            P(None, None, AXES),
            P("pcol", AXES),
            P(AXES, "pcol"),
        ),
        out_specs=P(AXES, "pcol"),
        check_vma=False,
    )
```

```python
import functools

import jax
import jax.numpy as jnp
import numpy as np
from jax import lax
from jax.experimental import pallas as pl
from jax.experimental.pallas import tpu as pltpu
from jax.sharding import Mesh
from jax.sharding import PartitionSpec as P

F32 = jnp.float32
BF16 = jnp.bfloat16
SIDE = 4
ROWS = 16
STRIP = 64
BLOCK = 512
AXES = ("z", "y", "x")
EVERY = ("z", "y", "x", "pcol")
PARTS = ((0, 1024, "zyx"), (1024, 1024, "zxy"))
GATHER = ("yx", "xy")
MB = 1 << 20
SMALL = pl.CostEstimate(flops=1000, bytes_accessed=1000, transcendentals=0)
TOKEN = jax.ShapeDtypeStruct((8, 128), F32)


def split2(value):
    high = value.astype(BF16)
    return high, (value - high.astype(F32)).astype(BF16)


def dot(a, b):
    return jnp.dot(a, b, preferred_element_type=F32)


def dot_exact(a, b):
    high, low = split2(a)
    rows = a.shape[0]
    both = dot(jnp.concatenate([high, low], axis=0), b)
    return both[:rows] + both[rows:]


def dot_pair(a, b_high, b_low):
    high, low = split2(a)
    rows = a.shape[0]
    both = dot(jnp.concatenate([high, low], axis=0), b_high)
    return both[:rows] + both[rows:] + dot(high, b_low)


def strip_copies(chips, pieces, lower, below, sems, spans):
    own_a, got_a, own_b, got_b = pieces
    half = lower.shape[0] // 2
    cut = STRIP // 2
    groups = ([], [], [])

    def add(group, source, start, count, target, to):
        cols = pl.ds(*spans[group])
        groups[group].append(
            pltpu.make_async_copy(
                source.at[pl.ds(start, count), cols],
                target.at[pl.ds(pl.multiple_of(to, cut), count), cols],
                sems.at[group],
            )
        )

    for position in range(16):
        base = (position % 8) * (STRIP + cut)
        row = pl.multiple_of(chips[position] * STRIP, STRIP)
        source = own_a if position < 8 else got_a
        add(0, source, base, STRIP, lower, row)
        add(1, source, base + STRIP, cut, lower, half + row)
        row = pl.multiple_of(chips[16 + position] * STRIP, STRIP)
        source = own_b if position < 8 else got_b
        add(1, source, base, cut, lower, half + row + cut)
        if below is not None:
            add(2, source, base + cut, STRIP, below, row)
    return groups


def start_all(copies):
    for copy in copies:
        copy.start()


def wait_for(target, sem):
    pltpu.make_async_copy(target, target, sem).wait()


def grow_kernel(chips, own_a, got_a, own_b, got_b, out_high, out_low, token, lower, sems):
    slab = lower.shape[0]
    half = slab // 2
    spans = ((0, slab), (0, slab), (0, slab))
    even, odd, _ = strip_copies(chips, (own_a, got_a, own_b, got_b), lower, None, sems, spans)
    start_all(even)
    start_all(odd)
    del token
    wait_for(lower.at[:half], sems.at[0])
    wait_for(lower.at[half:], sems.at[1])

    rows = lax.broadcasted_iota(jnp.int32, (128, 128), 0)
    lanes = lax.broadcasted_iota(jnp.int32, (128, 128), 1)
    corner = (rows < STRIP) & (lanes >= STRIP)
    same = (rows < STRIP) == (lanes < STRIP)
    upright, turned = [], []
    for k in range(half // 128):
        rng = slice(half + k * 128, half + k * 128 + 128)
        pair = lower[rng, :128].astype(F32) + lower[rng, 128:256].astype(F32)
        swapped = pltpu.roll(pair, STRIP, 1)
        upright.append(jnp.where(same, jnp.where(rows < STRIP, pair, swapped), 0.0))
        turned.append(jnp.where(same, jnp.where(rows < STRIP, swapped, pair), 0.0))
    level = []
    for k, both in enumerate(upright + turned):
        rng = slice(k * 128, k * 128 + 128)
        off = jnp.where(corner, lower[rng, rng].astype(F32), 0.0).astype(BF16)
        level.append(both - dot_pair(dot_exact(both, off), *split2(both)))
    size = 128
    while size < BLOCK:
        grown = []
        for n in range(0, len(level), 2):
            start = n * size
            off = lower[start : start + size, start + size : start + 2 * size]
            high, low = split2(level[n + 1])
            corner_block = -dot_pair(dot_exact(level[n], off), high, low)
            if 2 * size < BLOCK:
                top = jnp.concatenate([level[n], corner_block], axis=1)
                bottom = jnp.concatenate([jnp.zeros_like(corner_block), level[n + 1]], axis=1)
                grown.append(jnp.concatenate([top, bottom], axis=0))
            else:
                b = n // 2
                corner_high, corner_low = split2(corner_block)
                first_high, first_low = split2(level[n])
                zero = jnp.zeros((size, size), BF16)
                for ref, first, mixed, second in (
                    (out_high, first_high, corner_high, high),
                    (out_low, first_low, corner_low, low),
                ):
                    ref[b, :size, :size] = first
                    ref[b, :size, size:] = mixed
                    ref[b, size:, :size] = zero
                    ref[b, size:, size:] = second
        level = grown
        size *= 2


def grow(chips, pieces, slab):
    inverse = jax.ShapeDtypeStruct((slab // BLOCK, BLOCK, BLOCK), BF16)
    vmem = pl.BlockSpec(memory_space=pltpu.VMEM)
    return pl.pallas_call(
        grow_kernel,
        out_shape=(inverse, inverse, TOKEN),
        in_specs=[pl.BlockSpec(memory_space=pltpu.SMEM)] + [pl.BlockSpec(memory_space=pl.ANY)] * 4,
        out_specs=[vmem] * 2 + [pl.BlockSpec(memory_space=pltpu.HBM)],
        scratch_shapes=[pltpu.VMEM((slab, slab), BF16), pltpu.SemaphoreType.DMA((2,))],
        compiler_params=pltpu.CompilerParams(vmem_limit_bytes=28 * MB),
        cost_estimate=SMALL,
        name="grow_inverse",
    )(chips, *pieces)


def solve_block(blocks, pending, factor, high, low, out, wait, before_update, after):
    for b in range(blocks):
        cols = slice(b * BLOCK, (b + 1) * BLOCK)
        wait(b)
        y = dot_pair(pending[:, cols], high[b], low[b])
        out[: pending.shape[0], cols] = y
        before_update(b)
        if b + 1 < blocks:
            rest = slice((b + 1) * BLOCK, blocks * BLOCK)
            pending[:, rest] = pending[:, rest] - dot_exact(y, factor[cols, rest])
        after(b, y)


def inverse_copies(inv_high, inv_low, high, low, sems):
    return [
        [
            pltpu.make_async_copy(inv_high.at[b], high.at[b], sems.at[0, b]),
            pltpu.make_async_copy(inv_low.at[b], low.at[b], sems.at[1, b]),
        ]
        for b in range(high.shape[0])
    ]


def solve_kernel(first, core, chips, right, *refs):
    dense = refs[: 0 if first else 2]
    pieces = refs[len(dense) : len(dense) + 4]
    inv_high, inv_low, out, factor, under, high, low, pending, sems, strip_sems = refs[len(dense) + 4 :]
    rows, slab = right.shape
    half = slab // 2
    inner = half // BLOCK
    active = (core[0] == 0) if first else (core[0] != 0)

    @pl.when(active)
    def _():
        spans = ((BLOCK, slab - BLOCK), (half + BLOCK, half - BLOCK), (0, slab))
        even, odd, below = strip_copies(chips, pieces, factor, under, strip_sems, spans)
        inverse = inverse_copies(inv_high, inv_low, high, low, sems)
        order = [inverse[0], even, *inverse[1:], odd, below] if first else [below, *inverse, even, odd]
        for copies in order:
            start_all(copies)
        if first:
            pending[...] = right[...]
        else:
            own, other = dense
            pending[...] = right[...] - other[rows:, :]
            wait_for(under, strip_sems.at[2])
            pending[...] = pending[...] - dot_exact(other[:rows, half:], under[...])

        def wait(b):
            for copy in inverse[b]:
                copy.wait()

        def after(b, y):
            if first and b + 1 == inner:
                wait_for(under, strip_sems.at[2])
                out[rows:, :] = dot_exact(out[:rows, :half], under[...])

        def before_update(b):
            if b == 0:
                wait_for(factor.at[:half, BLOCK:], strip_sems.at[0])
            if b == inner:
                wait_for(factor.at[half:, half + BLOCK :], strip_sems.at[1])

        solve_block(slab // BLOCK, pending, factor, high, low, out, wait, before_update, after)

    @pl.when(jnp.logical_not(active))
    def _():
        out[...] = jnp.zeros_like(out) if first else dense[0][:rows, :]


def solve_call(first, core, chips, dense, pieces, inverses, name):
    rows, slab = dense[0].shape
    blocks = slab // BLOCK
    vmem = pl.BlockSpec(memory_space=pltpu.VMEM)
    smem = pl.BlockSpec(memory_space=pltpu.SMEM)
    return pl.pallas_call(
        functools.partial(solve_kernel, first),
        out_shape=jax.ShapeDtypeStruct((2 * rows if first else rows, slab), F32),
        in_specs=[smem, smem] + [vmem] * len(dense) + [pl.BlockSpec(memory_space=pl.ANY)] * 6,
        out_specs=vmem,
        scratch_shapes=[
            pltpu.VMEM((slab, slab), BF16),
            pltpu.VMEM((slab // 2, slab), BF16),
            pltpu.VMEM((blocks, BLOCK, BLOCK), BF16),
            pltpu.VMEM((blocks, BLOCK, BLOCK), BF16),
            pltpu.VMEM((rows, slab), F32),
            pltpu.SemaphoreType.DMA((2, blocks)),
            pltpu.SemaphoreType.DMA((3,)),
        ],
        compiler_params=pltpu.CompilerParams(vmem_limit_bytes=36 * MB),
        cost_estimate=SMALL,
        name=name,
    )(core, chips, *dense, *pieces, *inverses)


def product_kernel(parts, half, order, left, right, _, *refs):
    outs, token, (a, b, picked, a_sems, b_sems) = refs[: len(parts)], refs[len(parts)], refs[len(parts) + 1 :]
    del token
    groups, _, depth = left.shape
    rows = picked.shape[0]
    slab = rows // 2
    step = b.shape[1]
    spans = [(n, col) for n in range(len(parts)) for col in range(0, parts[n][2], step)]
    lanes = [pl.ds(g * depth, depth) for g in range(groups)]

    def slabs(n):
        copies = []
        for h in range(2):
            block = order[(2 * parts[n][0] + half) * (rows // ROWS) + h * (slab // ROWS)]
            source = pl.ds(pl.multiple_of(block // (slab // ROWS) * slab, slab), slab)
            for g in range(groups):
                copies.append(
                    pltpu.make_async_copy(
                        left.at[g, source], a.at[pl.ds(h * slab, slab), lanes[g]], a_sems.at[h, g]
                    )
                )
        return copies

    loads = slabs(0)
    for copy in loads:
        copy.start()
    tiles = []
    for t, (n, col) in enumerate(spans):
        tile = [
            pltpu.make_async_copy(
                right.at[g, pl.ds(parts[n][1] + col, step)], b.at[t, :, lanes[g]], b_sems.at[t, g]
            )
            for g in range(groups)
        ]
        for copy in tile:
            copy.start()
        tiles.append(tile)
    for copy in loads:
        copy.wait()
    for t, (n, col) in enumerate(spans):
        if col == 0:
            base = (2 * parts[n][0] + half) * (rows // ROWS)
            for r in range(rows // ROWS):
                inside = order[base + r] % (slab // ROWS) + r // (slab // ROWS) * (slab // ROWS)
                source = pl.ds(pl.multiple_of(inside * ROWS, ROWS), ROWS)
                picked[r * ROWS : (r + 1) * ROWS, :] = a[source, :]
        for copy in tiles[t]:
            copy.wait()
        outs[n][:, col : col + step] = lax.dot_general(
            picked[...], b[t], (((1,), (1,)), ((), ())), preferred_element_type=F32
        )


def product(order, left, right, token, parts, half, name):
    groups, rows, depth = left.shape
    width = sum(part[2] for part in parts)
    step = parts[0][2]
    return pl.pallas_call(
        functools.partial(product_kernel, parts, half),
        out_shape=[jax.ShapeDtypeStruct((rows // 2, part[2]), F32) for part in parts] + [TOKEN],
        in_specs=[pl.BlockSpec(memory_space=pltpu.SMEM)]
        + [pl.BlockSpec(memory_space=pltpu.HBM)] * 3,
        out_specs=[pl.BlockSpec(memory_space=pltpu.VMEM)] * len(parts)
        + [pl.BlockSpec(memory_space=pltpu.HBM)],
        scratch_shapes=[
            pltpu.VMEM((rows // 2, groups * depth), BF16),
            pltpu.VMEM((width // step, step, groups * depth), BF16),
            pltpu.VMEM((rows // 2, groups * depth), BF16),
            pltpu.SemaphoreType.DMA((2, groups)),
            pltpu.SemaphoreType.DMA((width // step, groups)),
        ],
        compiler_params=pltpu.CompilerParams(vmem_limit_bytes=48 * MB),
        cost_estimate=SMALL,
        name=name,
    )(order, left, right, token)


def chip_index(z, y, x, c):
    return ((z * SIDE + y) * SIDE + x) * 2 + c


def flip_pairs(axis, masks):
    pairs = []
    for z, y, x, c in np.ndindex(SIDE, SIDE, SIDE, 2):
        place = {"z": z, "y": y, "x": x}
        place[axis] ^= masks[c]
        pairs.append((chip_index(z, y, x, c), chip_index(place["z"], place["y"], place["x"], c)))
    return pairs


def partner_pairs(axis, second):
    return flip_pairs(axis, (3, 1) if second else (1, 3))


def block_order(axes, place, core):
    flip = jnp.where(core == 0, 1, 3)
    masks = jnp.stack([jnp.full_like(flip, 2), flip, flip ^ 2, jnp.zeros_like(flip)])
    lists = {name: place[name] ^ masks for name in AXES}
    shape = {name: [1, 1, 1] for name in AXES}
    for position, name in enumerate(axes):
        shape[name][position] = SIDE
    at = {name: lists[name].reshape(shape[name]) for name in AXES}
    return (((at["z"] * SIDE + at["y"]) * SIDE + at["x"]).reshape(-1)).astype(jnp.int32)


def choose_kernel(which, flags, held, got, *rest):
    out = rest[-2]
    out[...] = jnp.where(flags[which] > 0, held[...], got[...])


def pack_kernel(flags, held, got, under, got_under, out_a, out_b, token, odd):
    del token
    mine = flags[3] > 0
    width = held.shape[1]
    cut = STRIP // 2
    even = out_a.at[:STRIP]
    even[...] = jnp.where(mine, held[...], got[...])
    odd[...] = jnp.where(mine, got[...], held[...])
    out_b[cut:] = jnp.where(mine, under[...], got_under[...])

    at = pl.multiple_of(flags[4] * 128, 128)
    turn = flags[5] > 0
    one = even[:, pl.ds(at, 128)].astype(F32)
    two = odd[:, pl.ds(pl.multiple_of(at + width // 2, 128), 128)].astype(F32)
    one = jnp.where(turn, pltpu.roll(one, STRIP, 1), one)
    two = jnp.where(turn, two, pltpu.roll(two, STRIP, 1))
    rows = lax.broadcasted_iota(jnp.int32, (STRIP, 128), 0)
    lanes = lax.broadcasted_iota(jnp.int32, (STRIP, 128), 1)
    left = lanes < STRIP
    inner = jnp.where(left, lanes, lanes - STRIP)
    block = jnp.where(left, one, two)
    diagonal = jnp.where(inner == rows, block, 0.0)
    scale = jnp.where(
        left,
        1.0 / jnp.sum(jnp.where(left, diagonal, 0.0), axis=1, keepdims=True),
        1.0 / jnp.sum(jnp.where(left, 0.0, diagonal), axis=1, keepdims=True),
    )
    upper = jnp.where(inner > rows, block, 0.0)
    todo = jnp.where(inner == rows, 1.0, 0.0)
    for k in range(STRIP - 1, 0, -1):
        row = todo[k : k + 1, :] * scale[k : k + 1, :]
        col = jnp.where(left, upper[:, k : k + 1], upper[:, STRIP + k : STRIP + k + 1])
        todo = todo - col * row
    high, low = split2(todo * scale)
    odd[:, :128] = high
    odd[:, 128:256] = low
    out_a[STRIP:] = odd[:cut]
    out_b[:cut] = odd[cut:]


def small_call(kernel, name, shapes, scratch, flags, *operands, token=None):
    vmem = pl.BlockSpec(memory_space=pltpu.VMEM)
    hbm = pl.BlockSpec(memory_space=pltpu.HBM)
    tokens = () if token is None else (token,)
    return pl.pallas_call(
        kernel,
        out_shape=[jax.ShapeDtypeStruct(shape, BF16) for shape in shapes] + [TOKEN],
        in_specs=[pl.BlockSpec(memory_space=pltpu.SMEM)]
        + [vmem] * len(operands)
        + [hbm] * len(tokens),
        out_specs=[vmem] * len(shapes) + [hbm],
        scratch_shapes=scratch,
        compiler_params=pltpu.CompilerParams(vmem_limit_bytes=16 * MB),
        cost_estimate=SMALL,
        name=name,
    )(flags, *operands, *tokens)


def join_kernel(held_a, got_a, held_b, got_b, _, out_a, out_b, token, stage, in_sems, out_sems):
    del token
    loads, stores = [], []
    for n, (held, got, out) in enumerate(((held_a, got_a, out_a), (held_b, got_b, out_b))):
        rows = held.shape[0]
        for h, source in enumerate((held, got)):
            place = pl.ds(h * rows, rows)
            loads.append(pltpu.make_async_copy(source, stage.at[n, place], in_sems.at[n, h]))
            stores.append(pltpu.make_async_copy(stage.at[n, place], out.at[place], out_sems.at[n, h]))
    start_all(loads)
    for load, store in zip(loads, stores):
        load.wait()
        store.start()
    for store in stores:
        store.wait()


def join(held, got, token):
    rows, width = held[0].shape
    shape = jax.ShapeDtypeStruct((2 * rows, width), BF16)
    hbm = pl.BlockSpec(memory_space=pltpu.HBM)
    *joined, token = pl.pallas_call(
        join_kernel,
        out_shape=[shape, shape, TOKEN],
        in_specs=[pl.BlockSpec(memory_space=pl.ANY)] * 4 + [hbm],
        out_specs=[hbm] * 3,
        scratch_shapes=[
            pltpu.VMEM((2, 2 * rows, width), BF16),
            pltpu.SemaphoreType.DMA((2, 2)),
            pltpu.SemaphoreType.DMA((2, 2)),
        ],
        compiler_params=pltpu.CompilerParams(vmem_limit_bytes=12 * MB),
        cost_estimate=SMALL,
        name="join",
    )(held[0], got[0], held[1], got[1], token)
    return joined, token


def add_kernel(keep, got, _, send, kept, token):
    del token
    middle = send.shape[0]
    send[...] = keep[:middle] + got[:middle]
    kept[...] = keep[middle:] + got[middle:]


def add(keep, got, token):
    vmem = pl.BlockSpec(memory_space=pltpu.VMEM)
    hbm = pl.BlockSpec(memory_space=pltpu.HBM)
    shape = jax.ShapeDtypeStruct((keep.shape[0] // 2, keep.shape[1]), F32)
    return pl.pallas_call(
        add_kernel,
        out_shape=[shape, shape, TOKEN],
        in_specs=[vmem, vmem, hbm],
        out_specs=[vmem, vmem, hbm],
        compiler_params=pltpu.CompilerParams(vmem_limit_bytes=16 * MB),
        cost_estimate=SMALL,
        name="add",
    )(keep, got, token)


def gather_order(place, core):
    flip = jnp.where(core == 0, 1, 3)
    masks = jnp.stack([jnp.zeros_like(flip), flip, flip ^ 2, jnp.full_like(flip, 2)])
    ys, xs = place["y"] ^ masks, place["x"] ^ masks
    chips = [
        ys[None, :] * SIDE + xs[:, None],
        ys[:, None] * SIDE + xs[None, :],
    ]
    return jnp.concatenate([c.reshape(-1) for c in chips]).astype(jnp.int32)


def per_device(hist_factor, hist_solution, diag_factor, samples):
    slab = hist_factor.shape[1]
    core = lax.axis_index("pcol")
    place = {name: lax.axis_index(name) for name in AXES}
    core_arg = core.astype(jnp.int32).reshape(1)

    order = jnp.concatenate([block_order(axes, place, core) for _, _, axes in PARTS])
    parts = [(n, start, width) for n, (start, width, _) in enumerate(PARTS)]
    z = place["z"]
    at = place["y"] * SIDE + place["x"]
    outer = (z == 0) | (z == 3)
    flags = jnp.stack(
        [core > 0, (z < 2) == (core == 0), z < 2, outer == (core == 0), at // 2, at % 2]
    ).astype(jnp.int32)
    chips = gather_order(place, core)
    strip = diag_factor.T
    width = strip.shape[1]

    def along_z(*moves):
        return [
            (chip_index(start, y, x, c), chip_index(stop, y, x, d))
            for start, c, stop, d in moves
            for y in range(SIDE)
            for x in range(SIDE)
        ]

    def choose(which, own, got, name, token=None):
        kernel = functools.partial(choose_kernel, which)
        return small_call(kernel, name, [(STRIP, width)], [], flags, own, got, token=token)

    def half_product(n, half, token, name):
        return product(order, hist_solution, hist_factor, token, parts[n : n + 1], half, name)

    def gather_step(held, step):
        return [
            lax.ppermute(held[n], EVERY, partner_pairs(GATHER[n][step // 2], step % 2 == 1))
            for n in range(2)
        ]

    def sum_step(n, send, step):
        return lax.ppermute(send, EVERY, partner_pairs(PARTS[n][2][step // 2], step % 2 == 1))

    got = lax.ppermute(strip, EVERY, along_z((0, 0, 3, 0), (1, 0, 2, 0), (2, 1, 1, 1), (3, 1, 0, 1)))
    got_under = lax.ppermute(strip, EVERY, along_z((0, 1, 0, 0)))
    under, token = choose(0, strip, got_under, "below0")
    got_under = lax.ppermute(under, EVERY, along_z((0, 0, 3, 0), (1, 1, 2, 1)))
    mine, token = choose(1, strip, got, "strip1", token=token)
    got = lax.ppermute(mine, EVERY, flip_pairs("z", (1, 1)))
    send0, token = half_product(0, 0, token, "send0")
    under, token = choose(2, under, got_under, "below1", token=token)
    got_under = lax.ppermute(
        under, EVERY, along_z((0, 0, 1, 0), (3, 0, 2, 0), (1, 1, 0, 1), (2, 1, 3, 1))
    )
    come = [sum_step(0, send0, 0), None]
    share = STRIP + STRIP // 2
    *held, token = small_call(
        pack_kernel,
        "pack",
        [(share, width)] * 2,
        [pltpu.VMEM((STRIP, width), BF16)],
        flags,
        mine,
        got,
        under,
        got_under,
    )
    got = gather_step(held, 0)
    held, token = join(held, got, token)
    got = gather_step(held, 1)
    send1, token = half_product(1, 0, token, "send1")
    come[1] = sum_step(1, send1, 0)
    held, token = join(held, got, token)
    got = gather_step(held, 2)
    keep0, token = half_product(0, 1, token, "keep0")
    send0, keep0, token = add(keep0, come[0], token)
    come[0] = sum_step(0, send0, 1)
    keep1, token = half_product(1, 1, token, "keep1")
    held, token = join(held, got, token)
    got = gather_step(held, 3)
    send1, keep1, token = add(keep1, come[1], token)
    come[1] = sum_step(1, send1, 1)
    pieces = [held[0], got[0], held[1], got[1]]
    *inverses, token = grow(chips, pieces, slab)
    keeps = [keep0, keep1]
    for step in range(1, 5):
        for n in range(2):
            if step == 3:
                send, keeps[n], _ = add(keeps[n], come[n], token)
            else:
                middle = keeps[n].shape[0] // 2
                send = keeps[n][:middle] + come[n][:middle]
                keeps[n] = keeps[n][middle:] + come[n][middle:]
            come[n] = sum_step(n, send, step + 1)
    history = jnp.concatenate([keeps[n] + come[n] for n in range(2)], axis=1)
    pending = samples.astype(F32) - history

    first = solve_call(True, core_arg, chips, (pending,), pieces, inverses, "solve0")
    other = lax.ppermute(first, "pcol", [(0, 1)])
    return solve_call(False, core_arg, chips, (pending, first, other), pieces, inverses, "solve1")


def solution(mesh):
    cube = Mesh(mesh.devices.reshape(SIDE, SIDE, SIDE, 2), EVERY)
    return jax.shard_map(
        per_device,
        mesh=cube,
        in_specs=(
            P(None, "pcol", AXES),
            P(None, None, AXES),
            P("pcol", AXES),
            P(AXES, "pcol"),
        ),
        out_specs=P(AXES, "pcol"),
        check_vma=False,
    )
```

```python
import functools

import jax
import jax.numpy as jnp
import numpy as np
from jax import lax
from jax.experimental import pallas as pl
from jax.experimental.pallas import tpu as pltpu
from jax.sharding import Mesh
from jax.sharding import PartitionSpec as P

F32 = jnp.float32
BF16 = jnp.bfloat16
SIDE = 4
ROWS = 16
STRIP = 64
BLOCK = 512
AXES = ("z", "y", "x")
EVERY = ("z", "y", "x", "pcol")
PARTS = ((0, 1024, "zyx"), (1024, 1024, "zxy"))
GATHER = ("yx", "xy")
MB = 1 << 20
TOKEN = jax.ShapeDtypeStruct((8, 128), F32)


def split2(value):
    high = value.astype(BF16)
    return high, (value - high.astype(F32)).astype(BF16)


def dot(a, b):
    return jnp.dot(a, b, preferred_element_type=F32)


def dot_exact(a, b):
    high, low = split2(a)
    rows = a.shape[0]
    both = dot(jnp.concatenate([high, low], axis=0), b)
    return both[:rows] + both[rows:]


def dot_pair(a, b_high, b_low):
    high, low = split2(a)
    rows = a.shape[0]
    both = dot(jnp.concatenate([high, low], axis=0), b_high)
    return both[:rows] + both[rows:] + dot(high, b_low)


def strip_copies(chips, pieces, lower, below, sems, spans):
    own_a, got_a, own_b, got_b = pieces
    half = lower.shape[0] // 2
    cut = STRIP // 2
    groups = ([], [], [])

    def add(group, source, start, count, target, to):
        cols = pl.ds(*spans[group])
        groups[group].append(
            pltpu.make_async_copy(
                source.at[pl.ds(start, count), cols],
                target.at[pl.ds(pl.multiple_of(to, cut), count), cols],
                sems.at[group],
            )
        )

    for position in range(16):
        base = (position % 8) * (STRIP + cut)
        row = pl.multiple_of(chips[position] * STRIP, STRIP)
        source = own_a if position < 8 else got_a
        add(0, source, base, STRIP, lower, row)
        add(1, source, base + STRIP, cut, lower, half + row)
        row = pl.multiple_of(chips[16 + position] * STRIP, STRIP)
        source = own_b if position < 8 else got_b
        add(1, source, base, cut, lower, half + row + cut)
        if below is not None:
            add(2, source, base + cut, STRIP, below, row)
    return groups


def start_all(copies):
    for copy in copies:
        copy.start()


def wait_for(target, sem):
    pltpu.make_async_copy(target, target, sem).wait()


def grow_kernel(chips, own_a, got_a, own_b, got_b, out_high, out_low, token, lower, sems):
    slab = lower.shape[0]
    half = slab // 2
    spans = ((0, slab), (0, slab), (0, slab))
    even, odd, _ = strip_copies(chips, (own_a, got_a, own_b, got_b), lower, None, sems, spans)
    start_all(even)
    start_all(odd)
    del token
    wait_for(lower.at[:half], sems.at[0])
    wait_for(lower.at[half:], sems.at[1])

    rows = lax.broadcasted_iota(jnp.int32, (128, 128), 0)
    lanes = lax.broadcasted_iota(jnp.int32, (128, 128), 1)
    corner = (rows < STRIP) & (lanes >= STRIP)
    same = (rows < STRIP) == (lanes < STRIP)
    upright, turned = [], []
    for k in range(half // 128):
        rng = slice(half + k * 128, half + k * 128 + 128)
        pair = lower[rng, :128].astype(F32) + lower[rng, 128:256].astype(F32)
        swapped = pltpu.roll(pair, STRIP, 1)
        upright.append(jnp.where(same, jnp.where(rows < STRIP, pair, swapped), 0.0))
        turned.append(jnp.where(same, jnp.where(rows < STRIP, swapped, pair), 0.0))
    level = []
    for k, both in enumerate(upright + turned):
        rng = slice(k * 128, k * 128 + 128)
        off = jnp.where(corner, lower[rng, rng].astype(F32), 0.0).astype(BF16)
        level.append(both - dot_pair(dot_exact(both, off), *split2(both)))
    size = 128
    while size < BLOCK:
        grown = []
        for n in range(0, len(level), 2):
            start = n * size
            off = lower[start : start + size, start + size : start + 2 * size]
            high, low = split2(level[n + 1])
            corner_block = -dot_pair(dot_exact(level[n], off), high, low)
            if 2 * size < BLOCK:
                top = jnp.concatenate([level[n], corner_block], axis=1)
                bottom = jnp.concatenate([jnp.zeros_like(corner_block), level[n + 1]], axis=1)
                grown.append(jnp.concatenate([top, bottom], axis=0))
            else:
                b = n // 2
                corner_high, corner_low = split2(corner_block)
                first_high, first_low = split2(level[n])
                zero = jnp.zeros((size, size), BF16)
                for ref, first, mixed, second in (
                    (out_high, first_high, corner_high, high),
                    (out_low, first_low, corner_low, low),
                ):
                    ref[b, :size, :size] = first
                    ref[b, :size, size:] = mixed
                    ref[b, size:, :size] = zero
                    ref[b, size:, size:] = second
        level = grown
        size *= 2


def grow(chips, pieces, slab):
    inverse = jax.ShapeDtypeStruct((slab // BLOCK, BLOCK, BLOCK), BF16)
    vmem = pl.BlockSpec(memory_space=pltpu.VMEM)
    return pl.pallas_call(
        grow_kernel,
        out_shape=(inverse, inverse, TOKEN),
        in_specs=[pl.BlockSpec(memory_space=pltpu.SMEM)] + [pl.BlockSpec(memory_space=pl.ANY)] * 4,
        out_specs=[vmem] * 2 + [pl.BlockSpec(memory_space=pltpu.HBM)],
        scratch_shapes=[pltpu.VMEM((slab, slab), BF16), pltpu.SemaphoreType.DMA((2,))],
        compiler_params=pltpu.CompilerParams(vmem_limit_bytes=28 * MB),
        cost_estimate=pl.CostEstimate(flops=4 * 10**9, bytes_accessed=2 * slab * slab, transcendentals=0),
        name="grow_inverse",
    )(chips, *pieces)


def solve_block(blocks, pending, factor, high, low, out, wait, before_update, after):
    for b in range(blocks):
        cols = slice(b * BLOCK, (b + 1) * BLOCK)
        wait(b)
        y = dot_pair(pending[:, cols], high[b], low[b])
        out[: pending.shape[0], cols] = y
        before_update(b)
        if b + 1 < blocks:
            rest = slice((b + 1) * BLOCK, blocks * BLOCK)
            pending[:, rest] = pending[:, rest] - dot_exact(y, factor[cols, rest])
        after(b, y)


def inverse_copies(inv_high, inv_low, high, low, sems):
    return [
        [
            pltpu.make_async_copy(inv_high.at[b], high.at[b], sems.at[0, b]),
            pltpu.make_async_copy(inv_low.at[b], low.at[b], sems.at[1, b]),
        ]
        for b in range(high.shape[0])
    ]


def solve_kernel(first, core, chips, right, *refs):
    dense = refs[: 0 if first else 2]
    pieces = refs[len(dense) : len(dense) + 4]
    inv_high, inv_low, out, factor, under, high, low, pending, sems, strip_sems = refs[len(dense) + 4 :]
    rows, slab = right.shape
    half = slab // 2
    inner = half // BLOCK
    active = (core[0] == 0) if first else (core[0] != 0)

    @pl.when(active)
    def _():
        spans = ((BLOCK, slab - BLOCK), (half + BLOCK, half - BLOCK), (0, slab))
        even, odd, below = strip_copies(chips, pieces, factor, under, strip_sems, spans)
        inverse = inverse_copies(inv_high, inv_low, high, low, sems)
        order = [inverse[0], even, *inverse[1:], odd, below] if first else [below, *inverse, even, odd]
        for copies in order:
            start_all(copies)
        if first:
            pending[...] = right[...]
        else:
            own, other = dense
            pending[...] = right[...] - other[rows:, :]
            wait_for(under, strip_sems.at[2])
            pending[...] = pending[...] - dot_exact(other[:rows, half:], under[...])

        def wait(b):
            for copy in inverse[b]:
                copy.wait()

        def after(b, y):
            if first and b + 1 == inner:
                wait_for(under, strip_sems.at[2])
                out[rows:, :] = dot_exact(out[:rows, :half], under[...])

        def before_update(b):
            if b == 0:
                wait_for(factor.at[:half, BLOCK:], strip_sems.at[0])
            if b == inner:
                wait_for(factor.at[half:, half + BLOCK :], strip_sems.at[1])

        solve_block(slab // BLOCK, pending, factor, high, low, out, wait, before_update, after)

    @pl.when(jnp.logical_not(active))
    def _():
        out[...] = jnp.zeros_like(out) if first else dense[0][:rows, :]


def solve_call(first, core, chips, dense, pieces, inverses, name):
    rows, slab = dense[0].shape
    blocks = slab // BLOCK
    vmem = pl.BlockSpec(memory_space=pltpu.VMEM)
    smem = pl.BlockSpec(memory_space=pltpu.SMEM)
    return pl.pallas_call(
        functools.partial(solve_kernel, first),
        out_shape=jax.ShapeDtypeStruct((2 * rows if first else rows, slab), F32),
        in_specs=[smem, smem] + [vmem] * len(dense) + [pl.BlockSpec(memory_space=pl.ANY)] * 6,
        out_specs=vmem,
        scratch_shapes=[
            pltpu.VMEM((slab, slab), BF16),
            pltpu.VMEM((slab // 2, slab), BF16),
            pltpu.VMEM((blocks, BLOCK, BLOCK), BF16),
            pltpu.VMEM((blocks, BLOCK, BLOCK), BF16),
            pltpu.VMEM((rows, slab), F32),
            pltpu.SemaphoreType.DMA((2, blocks)),
            pltpu.SemaphoreType.DMA((3,)),
        ],
        compiler_params=pltpu.CompilerParams(vmem_limit_bytes=36 * MB),
        name=name,
    )(core, chips, *dense, *pieces, *inverses)


def product_kernel(parts, half, order, left, right, _, *refs):
    outs, token, (a, b, picked, a_sems, b_sems) = refs[: len(parts)], refs[len(parts)], refs[len(parts) + 1 :]
    del token
    groups, _, depth = left.shape
    rows = picked.shape[0]
    slab = rows // 2
    step = b.shape[1]
    spans = [(n, col) for n in range(len(parts)) for col in range(0, parts[n][2], step)]
    lanes = [pl.ds(g * depth, depth) for g in range(groups)]

    def slabs(n):
        copies = []
        for h in range(2):
            block = order[(2 * parts[n][0] + half) * (rows // ROWS) + h * (slab // ROWS)]
            source = pl.ds(pl.multiple_of(block // (slab // ROWS) * slab, slab), slab)
            for g in range(groups):
                copies.append(
                    pltpu.make_async_copy(
                        left.at[g, source], a.at[pl.ds(h * slab, slab), lanes[g]], a_sems.at[h, g]
                    )
                )
        return copies

    loads = slabs(0)
    for copy in loads:
        copy.start()
    tiles = []
    for t, (n, col) in enumerate(spans):
        tile = [
            pltpu.make_async_copy(
                right.at[g, pl.ds(parts[n][1] + col, step)], b.at[t, :, lanes[g]], b_sems.at[t, g]
            )
            for g in range(groups)
        ]
        for copy in tile:
            copy.start()
        tiles.append(tile)
    for copy in loads:
        copy.wait()
    for t, (n, col) in enumerate(spans):
        if col == 0:
            base = (2 * parts[n][0] + half) * (rows // ROWS)
            for r in range(rows // ROWS):
                inside = order[base + r] % (slab // ROWS) + r // (slab // ROWS) * (slab // ROWS)
                source = pl.ds(pl.multiple_of(inside * ROWS, ROWS), ROWS)
                picked[r * ROWS : (r + 1) * ROWS, :] = a[source, :]
        for copy in tiles[t]:
            copy.wait()
        outs[n][:, col : col + step] = lax.dot_general(
            picked[...], b[t], (((1,), (1,)), ((), ())), preferred_element_type=F32
        )


def product(order, left, right, token, parts, half, name):
    groups, rows, depth = left.shape
    width = sum(part[2] for part in parts)
    step = parts[0][2]
    return pl.pallas_call(
        functools.partial(product_kernel, parts, half),
        out_shape=[jax.ShapeDtypeStruct((rows // 2, part[2]), F32) for part in parts] + [TOKEN],
        in_specs=[pl.BlockSpec(memory_space=pltpu.SMEM)]
        + [pl.BlockSpec(memory_space=pltpu.HBM)] * 3,
        out_specs=[pl.BlockSpec(memory_space=pltpu.VMEM)] * len(parts)
        + [pl.BlockSpec(memory_space=pltpu.HBM)],
        scratch_shapes=[
            pltpu.VMEM((rows // 2, groups * depth), BF16),
            pltpu.VMEM((width // step, step, groups * depth), BF16),
            pltpu.VMEM((rows // 2, groups * depth), BF16),
            pltpu.SemaphoreType.DMA((2, groups)),
            pltpu.SemaphoreType.DMA((width // step, groups)),
        ],
        compiler_params=pltpu.CompilerParams(vmem_limit_bytes=48 * MB),
        cost_estimate=pl.CostEstimate(
            flops=groups * rows * width * depth,
            bytes_accessed=2 * groups * (rows // 2 + width) * depth + 2 * rows * width,
            transcendentals=0,
        ),
        name=name,
    )(order, left, right, token)


def chip_index(z, y, x, c):
    return ((z * SIDE + y) * SIDE + x) * 2 + c


def flip_pairs(axis, masks):
    pairs = []
    for z, y, x, c in np.ndindex(SIDE, SIDE, SIDE, 2):
        place = {"z": z, "y": y, "x": x}
        place[axis] ^= masks[c]
        pairs.append((chip_index(z, y, x, c), chip_index(place["z"], place["y"], place["x"], c)))
    return pairs


def partner_pairs(axis, second):
    return flip_pairs(axis, (3, 1) if second else (1, 3))


def block_order(axes, place, core):
    flip = jnp.where(core == 0, 1, 3)
    masks = jnp.stack([jnp.full_like(flip, 2), flip, flip ^ 2, jnp.zeros_like(flip)])
    lists = {name: place[name] ^ masks for name in AXES}
    shape = {name: [1, 1, 1] for name in AXES}
    for position, name in enumerate(axes):
        shape[name][position] = SIDE
    at = {name: lists[name].reshape(shape[name]) for name in AXES}
    return (((at["z"] * SIDE + at["y"]) * SIDE + at["x"]).reshape(-1)).astype(jnp.int32)


def pair_kernel(flags, strip, got, both, token):
    del token
    both[:STRIP] = strip[...]
    both[STRIP:] = jnp.where(flags[0] > 0, strip[...], got[...])


def choose_kernel(flags, held, got, _, both, token):
    del token
    both[:STRIP] = jnp.where(flags[1] > 0, held[:STRIP], got[:STRIP])
    both[STRIP:] = jnp.where(flags[2] > 0, held[STRIP:], got[STRIP:])


def pack_kernel(flags, held, got, _, out_a, out_b, token, odd):
    del token
    mine = flags[3] > 0
    width = held.shape[1]
    cut = STRIP // 2
    even = out_a.at[:STRIP]
    even[...] = jnp.where(mine, held[:STRIP], got[:STRIP])
    odd[...] = jnp.where(mine, got[:STRIP], held[:STRIP])
    out_b[cut:] = jnp.where(mine, held[STRIP:], got[STRIP:])

    at = pl.multiple_of(flags[4] * 128, 128)
    turn = flags[5] > 0
    one = even[:, pl.ds(at, 128)].astype(F32)
    two = odd[:, pl.ds(pl.multiple_of(at + width // 2, 128), 128)].astype(F32)
    one = jnp.where(turn, pltpu.roll(one, STRIP, 1), one)
    two = jnp.where(turn, two, pltpu.roll(two, STRIP, 1))
    rows = lax.broadcasted_iota(jnp.int32, (STRIP, 128), 0)
    lanes = lax.broadcasted_iota(jnp.int32, (STRIP, 128), 1)
    left = lanes < STRIP
    inner = jnp.where(left, lanes, lanes - STRIP)
    block = jnp.where(left, one, two)
    diagonal = jnp.where(inner == rows, block, 0.0)
    scale = jnp.where(
        left,
        1.0 / jnp.sum(jnp.where(left, diagonal, 0.0), axis=1, keepdims=True),
        1.0 / jnp.sum(jnp.where(left, 0.0, diagonal), axis=1, keepdims=True),
    )
    upper = jnp.where(inner > rows, block, 0.0)
    todo = jnp.where(inner == rows, 1.0, 0.0)
    for k in range(STRIP - 1, 0, -1):
        row = todo[k : k + 1, :] * scale[k : k + 1, :]
        col = jnp.where(left, upper[:, k : k + 1], upper[:, STRIP + k : STRIP + k + 1])
        todo = todo - col * row
    high, low = split2(todo * scale)
    odd[:, :128] = high
    odd[:, 128:256] = low
    out_a[STRIP:] = odd[:cut]
    out_b[:cut] = odd[cut:]


def small_call(kernel, name, shapes, scratch, flags, *operands, token=None):
    vmem = pl.BlockSpec(memory_space=pltpu.VMEM)
    hbm = pl.BlockSpec(memory_space=pltpu.HBM)
    tokens = () if token is None else (token,)
    return pl.pallas_call(
        kernel,
        out_shape=[jax.ShapeDtypeStruct(shape, BF16) for shape in shapes] + [TOKEN],
        in_specs=[pl.BlockSpec(memory_space=pltpu.SMEM)]
        + [vmem] * len(operands)
        + [hbm] * len(tokens),
        out_specs=[vmem] * len(shapes) + [hbm],
        scratch_shapes=scratch,
        compiler_params=pltpu.CompilerParams(vmem_limit_bytes=16 * MB),
        name=name,
    )(flags, *operands, *tokens)


def join_kernel(held_a, got_a, held_b, got_b, _, out_a, out_b, token, stage, in_sems, out_sems):
    del token
    loads, stores = [], []
    for n, (held, got, out) in enumerate(((held_a, got_a, out_a), (held_b, got_b, out_b))):
        rows = held.shape[0]
        for h, source in enumerate((held, got)):
            place = pl.ds(h * rows, rows)
            loads.append(pltpu.make_async_copy(source, stage.at[n, place], in_sems.at[n, h]))
            stores.append(pltpu.make_async_copy(stage.at[n, place], out.at[place], out_sems.at[n, h]))
    start_all(loads)
    for load, store in zip(loads, stores):
        load.wait()
        store.start()
    for store in stores:
        store.wait()


def join(held, got, token):
    rows, width = held[0].shape
    shape = jax.ShapeDtypeStruct((2 * rows, width), BF16)
    hbm = pl.BlockSpec(memory_space=pltpu.HBM)
    *joined, token = pl.pallas_call(
        join_kernel,
        out_shape=[shape, shape, TOKEN],
        in_specs=[pl.BlockSpec(memory_space=pl.ANY)] * 4 + [hbm],
        out_specs=[hbm] * 3,
        scratch_shapes=[
            pltpu.VMEM((2, 2 * rows, width), BF16),
            pltpu.SemaphoreType.DMA((2, 2)),
            pltpu.SemaphoreType.DMA((2, 2)),
        ],
        compiler_params=pltpu.CompilerParams(vmem_limit_bytes=12 * MB),
        name="join",
    )(held[0], got[0], held[1], got[1], token)
    return joined, token


def add_kernel(keep, got, _, send, kept, token):
    del token
    middle = send.shape[0]
    send[...] = keep[:middle] + got[:middle]
    kept[...] = keep[middle:] + got[middle:]


def add(keep, got, token):
    vmem = pl.BlockSpec(memory_space=pltpu.VMEM)
    hbm = pl.BlockSpec(memory_space=pltpu.HBM)
    shape = jax.ShapeDtypeStruct((keep.shape[0] // 2, keep.shape[1]), F32)
    return pl.pallas_call(
        add_kernel,
        out_shape=[shape, shape, TOKEN],
        in_specs=[vmem, vmem, hbm],
        out_specs=[vmem, vmem, hbm],
        compiler_params=pltpu.CompilerParams(vmem_limit_bytes=16 * MB),
        name="add",
    )(keep, got, token)


def gather_order(place, core):
    flip = jnp.where(core == 0, 1, 3)
    masks = jnp.stack([jnp.zeros_like(flip), flip, flip ^ 2, jnp.full_like(flip, 2)])
    ys, xs = place["y"] ^ masks, place["x"] ^ masks
    chips = [
        ys[None, :] * SIDE + xs[:, None],
        ys[:, None] * SIDE + xs[None, :],
    ]
    return jnp.concatenate([c.reshape(-1) for c in chips]).astype(jnp.int32)


def per_device(hist_factor, hist_solution, diag_factor, samples):
    slab = hist_factor.shape[1]
    core = lax.axis_index("pcol")
    place = {name: lax.axis_index(name) for name in AXES}
    core_arg = core.astype(jnp.int32).reshape(1)

    order = jnp.concatenate([block_order(axes, place, core) for _, _, axes in PARTS])
    parts = [(n, start, width) for n, (start, width, _) in enumerate(PARTS)]
    z = place["z"]
    at = place["y"] * SIDE + place["x"]
    outer = (z == 0) | (z == 3)
    flags = jnp.stack(
        [core > 0, (z < 2) == (core == 0), z < 2, outer == (core == 0), at // 2, at % 2]
    ).astype(jnp.int32)
    chips = gather_order(place, core)
    strip = diag_factor.T
    width = strip.shape[1]

    to_first = [
        (chip_index(0, y, x, 1), chip_index(0, y, x, 0)) for y in range(SIDE) for x in range(SIDE)
    ]
    def half_product(n, half, token, name):
        return product(order, hist_solution, hist_factor, token, parts[n : n + 1], half, name)

    def gather_step(held, step):
        return [
            lax.ppermute(held[n], EVERY, partner_pairs(GATHER[n][step // 2], step % 2 == 1))
            for n in range(2)
        ]

    def sum_step(n, send, step):
        return lax.ppermute(send, EVERY, partner_pairs(PARTS[n][2][step // 2], step % 2 == 1))

    got = lax.ppermute(strip, EVERY, to_first)
    held, token = small_call(pair_kernel, "pair", [(2 * STRIP, width)], [], flags, strip, got)
    needed = [
        (chip_index(start, y, x, c), chip_index(3 - start, y, x, c))
        for start, c in ((0, 0), (1, 0), (1, 1), (2, 1), (3, 1))
        for y in range(SIDE)
        for x in range(SIDE)
    ]
    got = lax.ppermute(held, EVERY, needed)
    send0, token = half_product(0, 0, token, "send0")
    held, token = small_call(
        choose_kernel, "choose", [(2 * STRIP, width)], [], flags, held, got, token=token
    )
    got = lax.ppermute(held, EVERY, flip_pairs("z", (1, 1)))
    come = [sum_step(0, send0, 0), None]
    share = STRIP + STRIP // 2
    *held, token = small_call(
        pack_kernel,
        "pack",
        [(share, width)] * 2,
        [pltpu.VMEM((STRIP, width), BF16)],
        flags,
        held,
        got,
        token=token,
    )
    got = gather_step(held, 0)
    send1, token = half_product(1, 0, token, "send1")
    come[1] = sum_step(1, send1, 0)
    held, token = join(held, got, token)
    got = gather_step(held, 1)
    keep0, token = half_product(0, 1, token, "keep0")
    held, token = join(held, got, token)
    got = gather_step(held, 2)
    send0, keep0, token = add(keep0, come[0], token)
    come[0] = sum_step(0, send0, 1)
    keep1, token = half_product(1, 1, token, "keep1")
    send1, keep1, token = add(keep1, come[1], token)
    come[1] = sum_step(1, send1, 1)
    held, token = join(held, got, token)
    got = gather_step(held, 3)
    pieces = [held[0], got[0], held[1], got[1]]
    *inverses, token = grow(chips, pieces, slab)
    keeps = [keep0, keep1]
    for step in range(1, 5):
        for n in range(2):
            if step == 4:
                send, keeps[n], _ = add(keeps[n], come[n], token)
            else:
                middle = keeps[n].shape[0] // 2
                send = keeps[n][:middle] + come[n][:middle]
                keeps[n] = keeps[n][middle:] + come[n][middle:]
            come[n] = sum_step(n, send, step + 1)
    history = jnp.concatenate([keeps[n] + come[n] for n in range(2)], axis=1)
    pending = samples.astype(F32) - history

    first = solve_call(True, core_arg, chips, (pending,), pieces, inverses, "solve0")
    other = lax.ppermute(first, "pcol", [(0, 1)])
    return solve_call(False, core_arg, chips, (pending, first, other), pieces, inverses, "solve1")


def solution(mesh):
    cube = Mesh(mesh.devices.reshape(SIDE, SIDE, SIDE, 2), EVERY)
    return jax.shard_map(
        per_device,
        mesh=cube,
        in_specs=(
            P(None, "pcol", AXES),
            P(None, None, AXES),
            P("pcol", AXES),
            P(AXES, "pcol"),
        ),
        out_specs=P(AXES, "pcol"),
        check_vma=False,
    )
```
